256 devices in a mesh: gx: 32 (over x, y, core), gy: 8 (over z).
Axes of the slice: x: 4, y: 4, z: 8, core: 2. Of those that a mesh axis runs over, the one named last changes fastest.
Arguments:
- sens_temp: float32 [48, 512, 1024], P(None, 'gx', 'gy'), may hold values from -8.5 to 8.5
- sens_salt: float32 [48, 512, 1024], P(None, 'gx', 'gy'), may hold values from -8.5 to 8.5
- sens_surface: float32 [512, 1024], P('gx', 'gy'), may hold values from -8.5 to 8.5
- flow_east: float32 [48, 512, 1024], P(None, 'gx', 'gy'), may hold values from -4 to 4
- flow_north: float32 [48, 512, 1024], P(None, 'gx', 'gy'), may hold values from -4 to 4
- mix_profile: float32 [48], replicated, may hold values from 0.2 to 5
- thermal_weight: float32 [48], replicated, may hold values from 0.1 to 0.5
- haline_weight: float32 [48], replicated, may hold values from 0.1 to 0.5
- surface_diag: float32 [512, 1024], P('gx', 'gy'), may hold values from 0.05 to 1
- land_mask: int32 [48, 512, 1024], P(None, 'gx', 'gy'), may hold values 0 or 1
- bottom_level: int32 [512, 1024], P('gx', 'gy'), may hold values from 24 to 48
Outputs:
- start_temp: float32 [48, 512, 1024], P(None, 'gx', 'gy')
- start_salt: float32 [48, 512, 1024], P(None, 'gx', 'gy')
- start_surface: float32 [512, 1024], P('gx', 'gy')
The draws below stay inside these ranges and needn't reach their ends.
All inputs are finite; a program needn't handle non-finite values. No bound on the sum of `land_mask` on one device may be relied on, other than what follows from the above.
Results may differ from the reference program's by a relative error of at most 0.0001.
Values sent between devices are 32-bit elements; how exact they have to be, the bound alone decides.
No kernel may reach another device: no remote copies, remote signals or barrier semaphores. Data moves between devices by JAX's collectives and lax.ppermute only.
A program may use at most 128 MiB of HBM per device.

```python
import math
import jax
import jax.numpy as jnp
from jax import lax

NZ = 48
CG_ITERS = 4
STEPS = 2
NX = 512
NY = 1024


def ramp_ratios(shape, lon_axis, lat_axis):
    lon_ratio = lax.broadcasted_iota(jnp.float32, shape, lon_axis) / shape[lon_axis]
    lat_ratio = lax.broadcasted_iota(jnp.float32, shape, lat_axis) / shape[lat_axis]
    return (lon_ratio, lat_ratio)


def draw_sens_temp(key, part):
    shape = (NZ, NX, NY)
    lon_ratio, lat_ratio = ramp_ratios(shape, 1, 2)
    sub_key = jax.random.fold_in(key, 11)
    base_values = jnp.clip(jax.random.normal(sub_key, shape, jnp.float32), -3.0, 3.0)
    factor = 10.0 ** (lon_ratio - 0.5) * 3.0 ** (lat_ratio - 0.5) * 0.5
    return base_values * factor


def draw_sens_salt(key, part):
    shape = (NZ, NX, NY)
    lon_ratio, lat_ratio = ramp_ratios(shape, 1, 2)
    sub_key = jax.random.fold_in(key, 23)
    base_values = jnp.clip(jax.random.normal(sub_key, shape, jnp.float32), -3.0, 3.0)
    factor = 10.0 ** (lon_ratio - 0.5) * 3.0 ** (lat_ratio - 0.5) * 0.5
    return base_values * factor


def draw_sens_surface(key, part):
    shape = (NX, NY)
    lon_ratio, lat_ratio = ramp_ratios(shape, 0, 1)
    sub_key = jax.random.fold_in(key, 37)
    base_values = jnp.clip(jax.random.normal(sub_key, shape, jnp.float32), -3.0, 3.0)
    factor = 10.0 ** (lon_ratio - 0.5) * 3.0 ** (lat_ratio - 0.5) * 0.5
    return base_values * factor


def set_ends(values, stream_key, low, high):
    place = [jax.random.randint(jax.random.fold_in(stream_key, axis), (), 0, length) for axis, length in enumerate(values.shape)]
    main_axis = values.shape.index(max(values.shape))
    neighbour = place[:main_axis] + [(place[main_axis] + 1) % values.shape[main_axis]] + place[main_axis + 1:]
    return values.at[tuple(place)].set(low).at[tuple(neighbour)].set(high)


def shard_levels(rng, shape, cuts, least, largest):
    def one(position, shards_of):
        steps = jax.random.uniform(jax.random.fold_in(jax.random.fold_in(rng, 6), position), (shards_of,), jnp.float32, least / len(cuts), largest / len(cuts))
        return jnp.repeat(jnp.exp(steps), shape[position] // shards_of).reshape((-1,) + (1,) * (len(shape) - position - 1))

    loudness = one(*cuts[0])
    for cut in cuts[1:]:
        loudness = loudness * one(*cut)
    return loudness


def centred(stream_key, shape, width, most, cuts=(), dtype=jnp.bfloat16):
    values = jax.random.normal(stream_key, shape, jnp.float32) * width
    if len(cuts) > 0:
        values = shard_levels(stream_key, shape, cuts, -0.22, 0.18) * values
    return jnp.clip(values, min=-most, max=most).astype(dtype)


def setup_inputs(seed: int = 0) -> dict:
    keys = jax.random.split(jax.random.key(seed), 12)
    return {
        "sens_temp": draw_sens_temp(jax.random.fold_in(keys[11], 71), 0),
        "sens_salt": draw_sens_salt(jax.random.fold_in(keys[11], 71), 0),
        "sens_surface": draw_sens_surface(jax.random.fold_in(keys[11], 71), 0),
        "flow_east": centred(keys[3], (NZ, NX, NY), 1.0, 4.0, ((1, 32), (2, 8)), jnp.float32),
        "flow_north": centred(keys[4], (NZ, NX, NY), 1.0, 4.0, ((1, 32), (2, 8)), jnp.float32),
        "mix_profile": jnp.clip(jnp.exp(jax.random.uniform(keys[5], (NZ,), jnp.float32, math.log(0.2), math.log(5.0))), 0.2, 5.0),
        "thermal_weight": jnp.clip(jnp.exp(jax.random.uniform(keys[6], (NZ,), jnp.float32, math.log(0.1), math.log(0.5))), 0.1, 0.5),
        "haline_weight": jnp.clip(jnp.exp(jax.random.uniform(keys[7], (NZ,), jnp.float32, math.log(0.1), math.log(0.5))), 0.1, 0.5),
        "surface_diag": jnp.clip(jnp.exp(math.log(1.0) - 2.9957323 * jax.random.uniform(keys[8], (NX, NY), jnp.float32) ** shard_levels(keys[8], (NX, NY), ((0, 32), (1, 8)), -0.2, 0.2)), 0.05, 1.0),
        "land_mask": set_ends((jax.random.randint(keys[9], (NZ, NX, NY), 0, 8) < 7).astype(jnp.int32), jax.random.fold_in(keys[9], 1), 0, 1),
        "bottom_level": set_ends(jax.random.randint(keys[10], (NX, NY), NZ // 2, NZ + 1), jax.random.fold_in(keys[10], 1), NZ // 2, NZ).astype(jnp.int32),
    }


diffusion_coef = 0.5
hyper_coef = 0.1
step_scale = 0.1


def roll_longitude(grid_field, offset):
    return jnp.roll(grid_field, offset, axis=grid_field.ndim - 2)


def shift_latitude(grid_field, offset):
    extent = grid_field.shape[-1]
    widths = [(0, 0)] * (grid_field.ndim - 1) + [(1, 1)]
    padded = jnp.pad(grid_field, widths)
    return lax.slice_in_dim(padded, 1 - offset, 1 - offset + extent, axis=grid_field.ndim - 1)


def laplacian(grid_field, wet_mask):
    summed = roll_longitude(wet_mask, -1) * (roll_longitude(grid_field, -1) - grid_field)
    summed = summed + roll_longitude(wet_mask, 1) * (roll_longitude(grid_field, 1) - grid_field)
    summed = summed + shift_latitude(wet_mask, -1) * (shift_latitude(grid_field, -1) - grid_field)
    summed = summed + shift_latitude(wet_mask, 1) * (shift_latitude(grid_field, 1) - grid_field)
    return wet_mask * summed


def level_transport(inputs):
    adjoint, wet_mask, east_flow, north_flow, diag_level = inputs
    east_flux = wet_mask * east_flow
    north_flux = wet_mask * north_flow
    east_out = (diffusion_coef * wet_mask - 0.5 * east_flux) * adjoint
    west_out = (diffusion_coef * wet_mask + 0.5 * east_flux) * adjoint
    north_out = (diffusion_coef * wet_mask - 0.5 * north_flux) * adjoint
    south_out = (diffusion_coef * wet_mask + 0.5 * north_flux) * adjoint
    incoming = roll_longitude(east_out, 1) + roll_longitude(west_out, -1) + shift_latitude(north_out, 1) + shift_latitude(south_out, -1)
    return wet_mask * incoming - diag_level * adjoint - hyper_coef * laplacian(laplacian(adjoint, wet_mask), wet_mask)


def vertical_solve(right_side, couple):
    levels = right_side.shape[-3]
    no_coupling = jnp.zeros_like(couple[0])
    ratios = []
    partial_values = []
    for level_index in range(levels):
        coupling_up = couple[level_index - 1] if level_index > 0 else no_coupling
        coupling_down = couple[level_index] if level_index < levels - 1 else no_coupling
        pivot_value = 1.0 + coupling_up + coupling_down
        source = right_side[..., level_index, :, :]
        if level_index > 0:
            pivot_value = pivot_value - coupling_up * ratios[-1]
            source = source + coupling_up * partial_values[-1]
        ratios.append(coupling_down / pivot_value)
        partial_values.append(source / pivot_value)
    solved = [partial_values[-1]]
    for level_index in range(levels - 2, -1, -1):
        solved.append(partial_values[level_index] + ratios[level_index] * solved[-1])
    return jnp.stack(solved[::-1], axis=-3)


def reference(sens_temp, sens_salt, sens_surface, flow_east, flow_north, mix_profile, thermal_weight, haline_weight, surface_diag, land_mask, bottom_level):
    level_ids = lax.broadcasted_iota(jnp.int32, land_mask.shape, 0)
    wet_cells = land_mask.astype(jnp.float32) * (level_ids < bottom_level[None, :, :]).astype(jnp.float32)
    column_depth = jnp.sum(wet_cells, axis=0) / NZ
    face_east = jnp.minimum(column_depth, roll_longitude(column_depth, -1))
    face_west = roll_longitude(face_east, 1)
    face_north = jnp.minimum(column_depth, shift_latitude(column_depth, -1))
    face_south = shift_latitude(face_north, 1)
    diagonal = wet_cells * (roll_longitude(wet_cells, -1) * (diffusion_coef - 0.5 * flow_east) + roll_longitude(wet_cells, 1) * (diffusion_coef + 0.5 * flow_east) + shift_latitude(wet_cells, -1) * (diffusion_coef - 0.5 * flow_north) + shift_latitude(wet_cells, 1) * (diffusion_coef + 0.5 * flow_north))
    couple = mix_profile[:-1, None, None] * wet_cells[:-1] * wet_cells[1:]

    def operate(direction):
        return surface_diag * direction + face_east * (direction - roll_longitude(direction, -1)) + face_west * (direction - roll_longitude(direction, 1)) + face_north * (direction - shift_latitude(direction, -1)) + face_south * (direction - shift_latitude(direction, 1))

    def transport(tracer):
        return lax.map(level_transport, (tracer, wet_cells, flow_east, flow_north, diagonal))

    temp = sens_temp
    salt = sens_salt
    surface = sens_surface
    for repeat in range(STEPS):
        combined = surface + jnp.sum(wet_cells * (thermal_weight[:, None, None] * temp - haline_weight[:, None, None] * salt), axis=0)
        solution = jnp.zeros_like(combined)
        residual = combined
        direction = combined
        norm_now = jnp.sum(residual * residual)
        for iteration in range(CG_ITERS):
            applied = operate(direction)
            step_length = norm_now / jnp.sum(direction * applied)
            solution = solution + step_length * direction
            residual = residual - step_length * applied
            norm_next = jnp.sum(residual * residual)
            direction = residual + (norm_next / norm_now) * direction
            norm_now = norm_next
        surface = surface_diag * solution
        temp = vertical_solve(temp + thermal_weight[:, None, None] * wet_cells * solution[None, :, :], couple)
        salt = vertical_solve(salt - haline_weight[:, None, None] * wet_cells * solution[None, :, :], couple)
        temp = temp + step_scale * transport(temp)
        salt = salt + step_scale * transport(salt)
    return temp, salt, surface
```

```python
import functools

import jax
import jax.numpy as jnp
from jax import lax
from jax.experimental import pallas as pl
from jax.experimental.pallas import tpu as pltpu
from jax.sharding import PartitionSpec as P

LEVELS = 48
ROWS = 16
COLS = 128
GROUPS = LEVELS // 4
F32 = jnp.float32
PAIRS = [(i, j) for i in range(4) for j in range(i, 5)]


def two_sum(a, b):
    s = a + b
    t = s - a
    return s, (a - (s - t)) + (b - t)


def fast_two_sum(a, b):
    s = a + b
    return s, b - (s - a)


def split(a):
    c = a * 4097.0
    high = c - (c - a)
    return high, a - high


def two_prod(a, b, a_parts=None, b_parts=None):
    ah, al = split(a) if a_parts is None else a_parts
    bh, bl = split(b) if b_parts is None else b_parts
    p = a * b
    return p, ((ah * bh - p) + ah * bl + al * bh) + al * bl


def pair_add(x, y):
    s, t = two_sum(x[0], y[0])
    return fast_two_sum(s, t + (x[1] + y[1]))


def pair_mul(x, y):
    p, e = two_prod(x[0], y[0])
    return fast_two_sum(p, e + (x[0] * y[1] + x[1] * y[0]))


def pair_neg(x):
    return -x[0], -x[1]


def pair_div(x, y):
    first = x[0] / y[0]
    p, e = two_prod(first, y[0])
    rest = ((x[0] - p) - e + x[1]) - first * y[1]
    return fast_two_sum(first, rest / y[0])


def roll(x, shift, axis):
    shift = shift % x.shape[axis]
    return x if shift == 0 else pltpu.roll(x, shift, axis)


def iota(shape, axis):
    return lax.broadcasted_iota(jnp.int32, shape, axis)


def put_rows(low_ref, high_ref, first, field, group, j, cells):
    at = first + field * GROUPS + group
    low_ref[at, 2 * j : 2 * j + 2, :] = cells[:2]
    high_ref[at, 2 * j : 2 * j + 2, :] = cells[ROWS - 2 :]


def packed(acc, cells, level):
    low, high = acc
    mine = lax.shift_right_logical(iota((ROWS, COLS), 1), 1) == level
    low = jnp.where(mine, pltpu.roll(cells, 2 * level, 1), low)
    high = jnp.where(mine, pltpu.roll(cells, 2 * level + 2, 1), high)
    return low, high


def put_surface(refs, fields):
    row_low, row_high, col_low, col_high = refs
    low = jnp.zeros((ROWS, COLS), F32)
    high = low
    lane_group = iota((ROWS, COLS), 1) // 8
    for n, cells in enumerate(fields):
        row_low[n] = cells[:8]
        row_high[n] = cells[8:]
        low = jnp.where(lane_group == n, roll(cells, 8 * n, 1), low)
        high = jnp.where(lane_group == n, roll(cells, 8 * n + 8, 1), high)
    col_low[0] = low
    col_high[0] = high


def put_corners(col_low, col_high, corners, count):
    south_west, south_east, north_west, north_east = corners
    for n in range(count):
        south_west[n] = col_low[n, :8, :]
        south_east[n] = col_low[n, 8:, :]
        north_west[n] = col_high[n, :8, :]
        north_east[n] = col_high[n, 8:, :]


def prepare_kernel(
    thermal, haline, temp, salt, east, north, mask, bottom, surface, diag,
    row_low, row_high, col_low, col_high, *corners,
):
    last = bottom[...]
    zero = jnp.zeros((ROWS, COLS), F32)

    def body(group, carry):
        total, depth, packs = carry
        for j in range(4):
            level = group * 4 + j
            wet = jnp.where(last > level, mask[level], 0).astype(F32)
            t, s = temp[level], salt[level]
            total = total + wet * (thermal[level] * t - haline[level] * s)
            depth = depth + wet
            for field, cells in enumerate((t, s, wet, east[level])):
                put_rows(row_low, row_high, 3, field, group, j, cells)
            packs = tuple(
                packed(acc, cells, level) for acc, cells in zip(packs, (t, s, wet, north[level]))
            )
        return total, depth, packs

    total, depth, packs = lax.fori_loop(0, GROUPS, body, (zero, zero, ((zero, zero),) * 4))
    for n, (low, high) in enumerate(packs):
        col_low[n + 1] = low
        col_high[n + 1] = high
    put_surface(
        (row_low, row_high, col_low, col_high),
        (surface[...] + total, depth / LEVELS, diag[...]),
    )
    put_corners(col_low, col_high, corners, 4)


def wide_surface(n, own, rows_e, rows_w, cols_n, cols_s, ne, nw, se, sw):
    main = jnp.concatenate([own, rows_e[n], rows_w[n]], axis=0)
    to_north = jnp.concatenate([cols_n[0], ne[0], nw[0]], axis=0)
    to_south = jnp.concatenate([cols_s[0], se[0], sw[0]], axis=0)
    lane = iota((32, COLS), 1)
    side = jnp.where(
        lane < 8,
        roll(to_north, -8 * n, 1),
        jnp.where(lane >= COLS - 8, roll(to_south, 120 - 8 * n, 1), 0.0),
    )
    return jnp.concatenate([main, side], axis=1)


def krylov(c, diag, depth, basis_ref, gram_ref):
    def nb(v):
        return pltpu.roll(v, 31, 0), pltpu.roll(v, 1, 0), pltpu.roll(v, 255, 1), pltpu.roll(v, 1, 1)

    faces = [jnp.minimum(depth, d) for d in nb(depth)]
    centre = (diag - 1.0) + ((faces[0] + faces[1]) + (faces[2] + faces[3]))
    v = c
    own = []
    for k in range(5):
        if k < 4:
            basis_ref[k] = v
        mine = v[:ROWS, :COLS]
        own.append((mine, split(mine)))
        if k < 4:
            e, w, n, s = nb(v)
            v = centre * v - ((faces[0] * e + faces[1] * w) + (faces[2] * n + faces[3] * s))
    highs, lows = [], []
    for i, j in PAIRS:
        p, e = two_prod(own[i][0], own[j][0], own[i][1], own[j][1])
        s, t = two_sum(p[:8], p[8:])
        highs.append(s)
        lows.append(t + (e[:8] + e[8:]))
    pad = [jnp.zeros((8, COLS), F32)] * (16 - len(PAIRS))
    high = jnp.concatenate(highs + pad, axis=0).T
    low = jnp.concatenate(lows + pad, axis=0).T
    parts = [(high[8 * n : 8 * n + 8], low[8 * n : 8 * n + 8]) for n in range(16)]
    while len(parts) > 1:
        parts = [pair_add(a, b) for a, b in zip(parts[::2], parts[1::2])]
    total = parts[0]
    for shift in (4, 2, 1):
        total = pair_add(total, tuple(roll(x, shift, 0) for x in total))
    total = pair_add(total, tuple(roll(x, 124, 1) for x in total))
    first_half = (iota((8, COLS), 1) % 8) < 4
    sums = jnp.where(first_half, total[0], roll(total[1], 4, 1))
    gram_ref[...] = jnp.concatenate([sums] * (gram_ref.shape[0] // 8), axis=0)


def first_surface_kernel(
    own_low, own_high, rows_e, rows_w, cols_n, cols_s, ne, nw, se, sw, basis, gram, fixed
):
    fields = [
        wide_surface(
            n, jnp.concatenate([own_low[n], own_high[n]], axis=0),
            rows_e, rows_w, cols_n, cols_s, ne, nw, se, sw,
        )
        for n in range(3)
    ]
    fixed[0] = fields[1]
    fixed[1] = fields[2]
    krylov(fields[0], fields[2], fields[1], basis, gram)


def next_surface_kernel(
    own_low, own_high, rows_e, rows_w, cols_n, cols_s, ne, nw, se, sw, fixed, basis, gram
):
    c = wide_surface(
        0, jnp.concatenate([own_low[0], own_high[0]], axis=0),
        rows_e, rows_w, cols_n, cols_s, ne, nw, se, sw,
    )
    krylov(c, fixed[1], fixed[0], basis, gram)


def coefficients(gathered):
    parts = [(gathered[8 * n : 8 * n + 8], None) for n in range(gathered.shape[0] // 8)]
    parts = [(p, jnp.zeros_like(p)) for p, _ in parts]
    while len(parts) > 1:
        parts = [pair_add(a, b) for a, b in zip(parts[::2], parts[1::2])]
    total = parts[0]
    for shift in (4, 2, 1):
        total = pair_add(total, tuple(roll(x, shift, 0) for x in total))
    for shift in (4, 2, 1):
        total = pair_add(total, tuple(roll(x, COLS - shift, 1) for x in total))
    table = {}
    for n, (i, j) in enumerate(PAIRS):
        entry = tuple(jnp.broadcast_to(x[:, 8 * n : 8 * n + 1], (8, COLS)) for x in total)
        table[i, j] = table[j, i] = entry
    one = (jnp.ones((8, COLS), F32), jnp.zeros((8, COLS), F32))
    r, p, x = [one], [one], []
    rr = table[0, 0]
    for it in range(4):
        image = [p[0]] + [pair_add(p[k], p[k - 1]) for k in range(1, it + 1)] + [p[it]]
        dot = functools.reduce(
            pair_add, [pair_mul(table[it, k], image[k]) for k in range(it + 2)]
        )
        step = pair_div(rr, pair_mul(p[it], dot))
        x = [
            pair_add(x[k], pair_mul(step, p[k])) if k < len(x) else pair_mul(step, p[k])
            for k in range(it + 1)
        ]
        if it < 3:
            minus = pair_neg(step)
            moved = [pair_mul(minus, a) for a in image]
            r = [pair_add(r[k], moved[k]) if k < len(r) else moved[k] for k in range(it + 2)]
            dot = functools.reduce(
                pair_add, [pair_mul(table[it + 1, k], r[k]) for k in range(it + 2)]
            )
            new = pair_mul(r[it + 1], dot)
            ratio = pair_div(new, rr)
            p = [
                pair_add(r[k], pair_mul(ratio, p[k])) if k < len(p) else r[k]
                for k in range(it + 2)
            ]
            rr = new
    return [a[0] for a in x]


def step_kernel(
    final,
    mix, thermal, haline, temp, salt, east, north, mask, bottom, diag, basis, gathered,
    a_rows_e, a_rows_w, a_cols_n, a_cols_s, a_ne, a_nw, a_se, a_sw,
    *rest,
):
    if final:
        (t_rows_e, t_rows_w, t_cols_n, t_cols_s, t_ne, t_nw, t_se, t_sw,
         new_temp, new_salt, new_surface,
         wet_wide, part_t, part_s, ratios, sides) = rest
        skip = 1
    else:
        (new_temp, new_salt, new_surface, row_low, row_high, col_low, col_high,
         c_sw, c_se, c_nw, c_ne,
         wet_wide, part_t, part_s, ratios, sides) = rest
        t_rows_e, t_rows_w, t_cols_n, t_cols_s, t_ne, t_nw, t_se, t_sw = (
            a_rows_e, a_rows_w, a_cols_n, a_cols_s, a_ne, a_nw, a_se, a_sw
        )
        skip = 3
    sub = iota((8, COLS), 0)
    lane = iota((24, COLS), 1)

    def set_side(n, block, cols, first, second):
        sides[n, :ROWS, :] = cols[block]
        sides[n, ROWS:, :] = jnp.where(sub < 4, first[block], second[block])

    for n, block in enumerate((1, 2)):
        set_side(2 * n, block, t_cols_n, t_ne, t_nw)
        set_side(2 * n + 1, block, t_cols_s, t_se, t_sw)
    set_side(4, 3, a_cols_n, a_ne, a_nw)
    set_side(5, 3, a_cols_s, a_se, a_sw)

    def beyond(north_side, south_side, level, rows):
        shift = COLS - 2 * level
        return jnp.where(
            lane[:rows] < 64,
            pltpu.roll(north_side, shift & 127, 1),
            pltpu.roll(south_side, (shift + 126) & 127, 1),
        )

    def end_rows(rows_e, rows_w, at, j):
        return jnp.where(sub < 4, roll(rows_e[at], -2 * j, 0), roll(rows_w[at], 6 - 2 * j, 0))

    def widened(own, rows_e, rows_w, at, j, side, level):
        main = jnp.concatenate([own, end_rows(rows_e, rows_w, at, j)], axis=0)
        return jnp.concatenate([main, beyond(sides[side], sides[side + 1], level, 24)], axis=1)

    last = bottom[...]

    def wet_body(group, _):
        for j in range(4):
            level = group * 4 + j
            wet = jnp.where(last > level, mask[level], 0).astype(F32)
            wet_wide[level] = widened(
                wet, a_rows_e, a_rows_w, 3 + 2 * GROUPS + group, j, 4, level
            )
        return 0

    lax.fori_loop(0, GROUPS, wet_body, 0)
    wet_wide[LEVELS] = jnp.zeros((24, 2 * COLS), F32)

    weights = coefficients(gathered[...])
    weights = [jnp.concatenate([jnp.concatenate([w] * 4, axis=0)] * 2, axis=1) for w in weights]
    full = sum(weights[k] * basis[k] for k in range(4))
    sub2 = iota((8, 2 * COLS), 0)
    multiplier = jnp.concatenate(
        [full[:ROWS], jnp.where(sub2 < 4, full[16:24], full[24:32])], axis=0
    )
    surface = diag[...] * full[:ROWS, :COLS]
    new_surface[...] = surface

    zero = jnp.zeros((24, 2 * COLS), F32)

    def forward(group, carry):
        up, ratio, pt, ps, wet = carry
        for j in range(4):
            level = group * 4 + j
            below = wet_wide[level + 1]
            down = mix[level] * (wet * below)
            inverse = 1.0 / ((1.0 + up + down) - up * ratio)
            t = widened(temp[level], t_rows_e, t_rows_w, skip + group, j, 0, level)
            s = widened(salt[level], t_rows_e, t_rows_w, skip + GROUPS + group, j, 2, level)
            wm = wet * multiplier
            pt = (t + thermal[level] * wm + up * pt) * inverse
            ps = (s - haline[level] * wm + up * ps) * inverse
            ratio = down * inverse
            part_t[level] = pt
            part_s[level] = ps
            ratios[level] = ratio
            up = down
            wet = below
        return up, ratio, pt, ps, wet

    lax.fori_loop(0, GROUPS, forward, (zero, zero, zero, zero, wet_wide[0]))

    def ends(v):
        return pltpu.roll(v, v.shape[0] - 1, 0), pltpu.roll(v, 1, 0)

    def flanks(v):
        return pltpu.roll(v, 2 * COLS - 1, 1), pltpu.roll(v, 1, 1)

    def backward(count, carry):
        xt, xs, total, packs = carry
        group = GROUPS - 1 - count
        for j in (3, 2, 1, 0):
            level = group * 4 + j
            ratio = ratios[level]
            xt = part_t[level] + ratio * xt
            xs = part_s[level] + ratio * xs
            wet = wet_wide[level]
            we, ww = ends(wet)
            wn, ws = flanks(wet)
            around = wet * ((we + ww) + (wn + ws))
            at = 3 + 3 * GROUPS + group
            fe = jnp.concatenate([east[level], end_rows(a_rows_e, a_rows_w, at, j)], axis=0)
            fn = jnp.concatenate(
                [north[level], beyond(a_cols_n[4], a_cols_s[4], level, ROWS)], axis=1
            )
            own = slice(0, ROWS), slice(0, COLS)
            wet_own = wet[own]
            around_own = around[own]
            diagonal = around_own + wet_own * (
                fe[:ROWS] * (ww - we)[own] + fn[:, :COLS] * (ws - wn)[own]
            )
            done = []
            for x in (xt, xs):
                q = wet * x
                qe, qw = ends(q)
                qn, qs = flanks(q)
                near = (qe + qw) + (qn + qs)
                lap = wet * near - around * x
                le, lw = ends(lap[:, :COLS])
                ln, ls = flanks(lap[:ROWS])
                lap2 = (
                    wet_own * ((le + lw)[:ROWS] + (ln + ls)[:, :COLS]) - around_own * lap[own]
                )
                be, bw = ends(fe * q[:, :COLS])
                dn, ds = flanks(fn * q[:ROWS])
                incoming = near[own] + ((be - bw)[:ROWS] + (dn - ds)[:, :COLS])
                x_own = x[own]
                done.append(
                    x_own + 0.05 * (wet_own * incoming - diagonal * x_own) - 0.01 * lap2
                )
            t, s = done
            new_temp[level] = t
            new_salt[level] = s
            if not final:
                total = total + wet_own * (thermal[level] * t - haline[level] * s)
                for field, cells in enumerate(done):
                    put_rows(row_low, row_high, 1, field, group, j, cells)
                packs = tuple(packed(acc, cells, level) for acc, cells in zip(packs, done))
        return xt, xs, total, packs

    small = jnp.zeros((ROWS, COLS), F32)
    packs = () if final else ((small, small), (small, small))
    xt, xs, total, packs = lax.fori_loop(0, GROUPS, backward, (zero, zero, small, packs))
    if not final:
        for n, (low, high) in enumerate(packs):
            col_low[n + 1] = low
            col_high[n + 1] = high
        put_surface((row_low, row_high, col_low, col_high), (surface + total,))
        put_corners(col_low, col_high, (c_sw, c_se, c_nw, c_ne), 3)


def shape(*dims):
    return jax.ShapeDtypeStruct(dims, F32)


VMEM = pl.BlockSpec(memory_space=pltpu.VMEM)
SMEM = pl.BlockSpec(memory_space=pltpu.SMEM)


def head(*block):
    return pl.BlockSpec(block, lambda i: (0,) * len(block), memory_space=pltpu.VMEM)


def call(kernel, outs, in_specs, out_specs=None, scratch=(), name=None, grid=None):
    extra = {} if grid is None else {"grid": grid}
    return pl.pallas_call(
        kernel,
        out_shape=outs,
        in_specs=in_specs,
        out_specs=[VMEM] * len(outs) if out_specs is None else out_specs,
        scratch_shapes=scratch,
        compiler_params=pltpu.CompilerParams(vmem_limit_bytes=40 * 1024 * 1024),
        name=name,
        **extra,
    )


def message_shapes(surfaces, row_fields, col_fields, corner_fields):
    rows = shape(surfaces + GROUPS * row_fields, 8, COLS)
    cols = shape(1 + col_fields, ROWS, COLS)
    corner = shape(1 + corner_fields, 8, COLS)
    return [rows, rows, cols, cols] + [corner] * 4


def solution(mesh):
    nx, ny = mesh.shape["gx"], mesh.shape["gy"]
    devices = nx * ny
    both = ("gx", "gy")

    def route(di, dj):
        return [
            (i * ny + j, (i + di) % nx * ny + j + dj)
            for i in range(nx)
            for j in range(ny)
            if 0 <= j + dj < ny
        ]

    def exchange(messages):
        row_low, row_high, col_low, col_high, sw, se, nw, ne = messages
        sends = (
            (row_low, -1, 0), (row_high, 1, 0), (col_low, 0, -1), (col_high, 0, 1),
            (sw, -1, -1), (se, 1, -1), (nw, -1, 1), (ne, 1, 1),
        )
        return [lax.ppermute(m, both, route(di, dj)) for m, di, dj in sends]

    def all_sum(block):
        return lax.all_to_all(block, both, 0, 0, tiled=True)

    def surface_specs(count):
        return (
            [head(count, 8, COLS)] * 4
            + [head(1, ROWS, COLS)] * 2
            + [head(1, 8, COLS)] * 4
        )

    basis_shape = shape(4, 32, 2 * COLS)
    gram_shape = shape(devices, COLS)
    field = shape(LEVELS, ROWS, COLS)
    tile = shape(ROWS, COLS)

    def whole(*dims):
        return head(*dims)

    def per_device(
        sens_temp, sens_salt, sens_surface, flow_east, flow_north, mix_profile,
        thermal_weight, haline_weight, surface_diag, land_mask, bottom_level,
    ):
        first = call(
            prepare_kernel, message_shapes(3, 4, 4, 3), [SMEM] * 2 + [VMEM] * 8, name="prepare"
        )(
            thermal_weight, haline_weight, sens_temp, sens_salt, flow_east, flow_north,
            land_mask, bottom_level, sens_surface, surface_diag,
        )
        got = exchange(first)
        basis, gram, fixed = call(
            first_surface_kernel,
            [basis_shape, gram_shape, shape(2, 32, 2 * COLS)],
            surface_specs(3),
            [whole(4, 32, 2 * COLS), whole(devices, COLS), whole(2, 32, 2 * COLS)],
            name="first_surface",
            grid=(1,),
        )(first[0], first[1], *got)
        gathered = all_sum(gram)

        scratch = [
            pltpu.VMEM((LEVELS + 1, 24, 2 * COLS), F32),
            pltpu.VMEM((LEVELS, 24, 2 * COLS), F32),
            pltpu.VMEM((LEVELS, 24, 2 * COLS), F32),
            pltpu.VMEM((LEVELS, 24, 2 * COLS), F32),
            pltpu.VMEM((6, 24, COLS), F32),
        ]

        def step(final, temp, salt, basis, gathered, more, outs):
            return call(
                functools.partial(step_kernel, final),
                outs,
                [SMEM] * 3 + [VMEM] * (17 + len(more)),
                scratch=scratch,
                name="last_step" if final else "first_step",
            )(
                mix_profile, thermal_weight, haline_weight, temp, salt, flow_east, flow_north,
                land_mask, bottom_level, surface_diag, basis, gathered, *got, *more,
            )

        temp, salt, _, *second = step(
            False, sens_temp, sens_salt, basis, gathered, [],
            [field, field, tile] + message_shapes(1, 2, 2, 2),
        )
        more = exchange(second)
        basis, gram = call(
            next_surface_kernel,
            [basis_shape, gram_shape],
            surface_specs(1) + [whole(2, 32, 2 * COLS)],
            [whole(4, 32, 2 * COLS), whole(devices, COLS)],
            name="next_surface",
            grid=(1,),
        )(second[0], second[1], *more, fixed)
        gathered = all_sum(gram)
        return tuple(step(True, temp, salt, basis, gathered, more, [field, field, tile]))

    in_specs = (
        P(None, "gx", "gy"),
        P(None, "gx", "gy"),
        P("gx", "gy"),
        P(None, "gx", "gy"),
        P(None, "gx", "gy"),
        P(),
        P(),
        P(),
        P("gx", "gy"),
        P(None, "gx", "gy"),
        P("gx", "gy"),
    )
    out_specs = (P(None, "gx", "gy"), P(None, "gx", "gy"), P("gx", "gy"))
    return jax.shard_map(
        per_device, mesh=mesh, in_specs=in_specs, out_specs=out_specs, check_vma=False
    )
```

```python
import functools

import jax
import jax.numpy as jnp
from jax import lax
from jax.experimental import pallas as pl
from jax.experimental.pallas import tpu as pltpu
from jax.sharding import PartitionSpec as P

LEVELS = 48
ROWS = 16
COLS = 128
GROUPS = LEVELS // 4
CHUNK = 12
F32 = jnp.float32
PAIRS = [(i, j) for i in range(4) for j in range(i, 5)]


def two_sum(a, b):
    s = a + b
    t = s - a
    return s, (a - (s - t)) + (b - t)


def fast_two_sum(a, b):
    s = a + b
    return s, b - (s - a)


def split(a):
    c = a * 4097.0
    high = c - (c - a)
    return high, a - high


def two_prod(a, b, a_parts=None, b_parts=None):
    ah, al = split(a) if a_parts is None else a_parts
    bh, bl = split(b) if b_parts is None else b_parts
    p = a * b
    return p, ((ah * bh - p) + ah * bl + al * bh) + al * bl


def pair_add(x, y):
    s, t = two_sum(x[0], y[0])
    return fast_two_sum(s, t + (x[1] + y[1]))


def pair_mul(x, y):
    p, e = two_prod(x[0], y[0])
    return fast_two_sum(p, e + (x[0] * y[1] + x[1] * y[0]))


def pair_neg(x):
    return -x[0], -x[1]


def pair_div(x, y):
    first = x[0] / y[0]
    p, e = two_prod(first, y[0])
    rest = ((x[0] - p) - e + x[1]) - first * y[1]
    return fast_two_sum(first, rest / y[0])


def roll(x, shift, axis):
    shift = shift % x.shape[axis]
    return x if shift == 0 else pltpu.roll(x, shift, axis)


def iota(shape, axis):
    return lax.broadcasted_iota(jnp.int32, shape, axis)


def put_rows(low_ref, high_ref, first, field, group, j, cells):
    at = first + field * GROUPS + group
    low_ref[at, 2 * j : 2 * j + 2, :] = cells[:2]
    high_ref[at, 2 * j : 2 * j + 2, :] = cells[ROWS - 2 :]


def packed(acc, cells, level):
    low, high = acc
    mine = lax.shift_right_logical(iota((ROWS, COLS), 1), 1) == level
    low = jnp.where(mine, pltpu.roll(cells, 2 * level, 1), low)
    high = jnp.where(mine, pltpu.roll(cells, 2 * level + 2, 1), high)
    return low, high


def put_surface(refs, first, fields):
    row_low, row_high, col_low, col_high = refs
    low = jnp.zeros((ROWS, COLS), F32)
    high = low
    lane_group = iota((ROWS, COLS), 1) // 8
    for n, cells in enumerate(fields):
        row_low[first + n] = cells[:8]
        row_high[first + n] = cells[8:]
        low = jnp.where(lane_group == n, roll(cells, 8 * n, 1), low)
        high = jnp.where(lane_group == n, roll(cells, 8 * n + 8, 1), high)
    put_cols(refs, 0, low, high)


def put_cols(refs, n, low, high):
    row_low, row_high, col_low, col_high = refs
    count = corners_of(row_low)
    for col, side, cells in ((col_low, 0, low), (col_high, count, high)):
        col[2 * n] = cells[:8]
        col[2 * n + 1] = cells[8:]
        if n < count:
            row_low[side + n] = cells[:8]
            row_high[side + n] = cells[8:]


def corners_of(rows):
    return {3 + 4 * GROUPS + 8: 4, 1 + 2 * GROUPS + 6: 3}[rows.shape[0]]


def forward_kernel(own_low, own_high, rows_e, rows_w, to_south, to_north):
    count = rows_e.shape[0] // 2
    own = own_low.shape[0]
    for out, mine, side in ((to_south, own_low, 0), (to_north, own_high, count)):
        out[:own] = mine[...]
        out[own : own + count] = rows_e[side : side + count]
        out[own + count :] = rows_w[side : side + count]


def prepare_kernel(
    thermal, haline, temp_in, salt_in, east_in, north_in, mask_in, bottom, surface, diag,
    row_low, row_high, col_low, col_high,
    temp, salt, east, north, mask, sems,
):
    last = bottom[...]
    zero = jnp.zeros((ROWS, COLS), F32)
    fields = list(
        zip((temp_in, salt_in, mask_in, east_in, north_in), (temp, salt, mask, east, north))
    )

    def copy(n, part):
        source, target = fields[n]
        levels = pl.ds(part * CHUNK, CHUNK)
        return pltpu.make_async_copy(source.at[levels], target.at[levels], sems.at[n, part])

    for part in range(LEVELS // CHUNK):
        for n in range(5):
            copy(n, part).start()

    def body(group, carry):
        total, depth, packs = carry
        for j in range(4):
            level = group * 4 + j
            wet = jnp.where(last > level, mask[level], 0).astype(F32)
            t, s = temp[level], salt[level]
            total = total + wet * (thermal[level] * t - haline[level] * s)
            depth = depth + wet
            for field, cells in enumerate((t, s, wet, east[level])):
                put_rows(row_low, row_high, 11, field, group, j, cells)
            packs = tuple(
                packed(acc, cells, level) for acc, cells in zip(packs, (t, s, wet, north[level]))
            )
        return total, depth, packs

    carry = (zero, zero, ((zero, zero),) * 4)
    step = CHUNK // 4
    for part in range(LEVELS // CHUNK):
        for n in range(5):
            copy(n, part).wait()
        carry = lax.fori_loop(part * step, (part + 1) * step, body, carry)
    total, depth, packs = carry
    refs = row_low, row_high, col_low, col_high
    put_surface(refs, 8, (surface[...] + total, depth / LEVELS, diag[...]))
    for n, (low, high) in enumerate(packs):
        put_cols(refs, n + 1, low, high)


def wide_surface(n, own, rows_e, rows_w, from_north, from_south):
    main = jnp.concatenate([own, rows_e, rows_w], axis=0)
    to_north = jnp.concatenate(from_north, axis=0)
    to_south = jnp.concatenate(from_south, axis=0)
    lane = iota((32, COLS), 1)
    side = jnp.where(
        lane < 8,
        roll(to_north, -8 * n, 1),
        jnp.where(lane >= COLS - 8, roll(to_south, 120 - 8 * n, 1), 0.0),
    )
    return jnp.concatenate([main, side], axis=1)


def krylov(c, diag, depth, basis_ref, gram_ref):
    def nb(v):
        return pltpu.roll(v, 31, 0), pltpu.roll(v, 1, 0), pltpu.roll(v, 255, 1), pltpu.roll(v, 1, 1)

    faces = [jnp.minimum(depth, d) for d in nb(depth)]
    centre = (diag - 1.0) + ((faces[0] + faces[1]) + (faces[2] + faces[3]))
    v = c
    own = []
    for k in range(5):
        if k < 4:
            basis_ref[k] = v
        mine = v[:ROWS, :COLS]
        own.append((mine, split(mine)))
        if k < 4:
            e, w, n, s = nb(v)
            v = centre * v - ((faces[0] * e + faces[1] * w) + (faces[2] * n + faces[3] * s))
    highs, lows = [], []
    for i, j in PAIRS:
        p, e = two_prod(own[i][0], own[j][0], own[i][1], own[j][1])
        s, t = two_sum(p[:8], p[8:])
        highs.append(s)
        lows.append(t + (e[:8] + e[8:]))
    pad = [jnp.zeros((8, COLS), F32)] * (16 - len(PAIRS))
    high = jnp.concatenate(highs + pad, axis=0).T
    low = jnp.concatenate(lows + pad, axis=0).T
    parts = [(high[8 * n : 8 * n + 8], low[8 * n : 8 * n + 8]) for n in range(16)]
    while len(parts) > 1:
        parts = [pair_add(a, b) for a, b in zip(parts[::2], parts[1::2])]
    total = parts[0]
    for shift in (4, 2, 1):
        total = pair_add(total, tuple(roll(x, shift, 0) for x in total))
    total = pair_add(total, tuple(roll(x, 124, 1) for x in total))
    first_half = (iota((8, COLS), 1) % 8) < 4
    sums = jnp.where(first_half, total[0], roll(total[1], 4, 1))
    gram_ref[...] = jnp.concatenate([sums] * (gram_ref.shape[0] // 8), axis=0)


def surface_fields(low, high, rows_e, rows_w, cols_n, cols_s, count):
    corners = count + 1 if count == 3 else 3
    first = 2 * corners

    def column(cols):
        own = cols.shape[0] - 2 * corners
        return [cols[0], cols[1], cols[own], cols[own + corners]]

    return [
        wide_surface(
            n, jnp.concatenate([low[first + n], high[first + n]], axis=0),
            rows_e[first + n], rows_w[first + n], column(cols_n), column(cols_s),
        )
        for n in range(count)
    ]


def first_surface_kernel(low, high, rows_e, rows_w, cols_n, cols_s, basis, gram, fixed):
    c, depth, diag = surface_fields(low, high, rows_e, rows_w, cols_n, cols_s, 3)
    fixed[0] = depth
    fixed[1] = diag
    krylov(c, diag, depth, basis, gram)


def next_surface_kernel(low, high, rows_e, rows_w, cols_n, cols_s, fixed, basis, gram):
    (c,) = surface_fields(low, high, rows_e, rows_w, cols_n, cols_s, 1)
    krylov(c, fixed[1], fixed[0], basis, gram)


def coefficients(gathered):
    parts = [(gathered[8 * n : 8 * n + 8], None) for n in range(gathered.shape[0] // 8)]
    parts = [(p, jnp.zeros_like(p)) for p, _ in parts]
    while len(parts) > 1:
        parts = [pair_add(a, b) for a, b in zip(parts[::2], parts[1::2])]
    total = parts[0]
    for shift in (4, 2, 1):
        total = pair_add(total, tuple(roll(x, shift, 0) for x in total))
    for shift in (4, 2, 1):
        total = pair_add(total, tuple(roll(x, COLS - shift, 1) for x in total))
    table = {}
    for n, (i, j) in enumerate(PAIRS):
        entry = tuple(jnp.broadcast_to(x[:, 8 * n : 8 * n + 1], (8, COLS)) for x in total)
        table[i, j] = table[j, i] = entry
    one = (jnp.ones((8, COLS), F32), jnp.zeros((8, COLS), F32))
    r, p, x = [one], [one], []
    rr = table[0, 0]
    for it in range(4):
        image = [p[0]] + [pair_add(p[k], p[k - 1]) for k in range(1, it + 1)] + [p[it]]
        dot = functools.reduce(
            pair_add, [pair_mul(table[it, k], image[k]) for k in range(it + 2)]
        )
        step = pair_div(rr, pair_mul(p[it], dot))
        x = [
            pair_add(x[k], pair_mul(step, p[k])) if k < len(x) else pair_mul(step, p[k])
            for k in range(it + 1)
        ]
        if it < 3:
            minus = pair_neg(step)
            moved = [pair_mul(minus, a) for a in image]
            r = [pair_add(r[k], moved[k]) if k < len(r) else moved[k] for k in range(it + 2)]
            dot = functools.reduce(
                pair_add, [pair_mul(table[it + 1, k], r[k]) for k in range(it + 2)]
            )
            new = pair_mul(r[it + 1], dot)
            ratio = pair_div(new, rr)
            p = [
                pair_add(r[k], pair_mul(ratio, p[k])) if k < len(p) else r[k]
                for k in range(it + 2)
            ]
            rr = new
    return [a[0] for a in x]


def step_kernel(
    final,
    mix, thermal, haline, temp, salt, east, north, mask, bottom, diag, basis, gathered,
    a_rows_e, a_rows_w, a_cols_n, a_cols_s,
    *rest,
):
    if final:
        (t_rows_e, t_rows_w, t_cols_n, t_cols_s,
         new_temp, new_salt, new_surface,
         wet_wide, part_t, part_s, ratios, sides) = rest
        skip = 7
    else:
        (new_temp, new_salt, new_surface, row_low, row_high, col_low, col_high,
         wet_wide, part_t, part_s, ratios, sides) = rest
        t_rows_e, t_rows_w, t_cols_n, t_cols_s = a_rows_e, a_rows_w, a_cols_n, a_cols_s
        skip = 11
    sub = iota((8, COLS), 0)
    lane = iota((24, COLS), 1)

    def set_side(n, block, cols):
        corners = (cols.shape[0] - 10) // 2 if cols.shape[0] == 18 else 3
        own = cols.shape[0] - 2 * corners
        sides[n, :8, :] = cols[2 * block]
        sides[n, 8:ROWS, :] = cols[2 * block + 1]
        sides[n, ROWS:, :] = jnp.where(sub < 4, cols[own + block], cols[own + corners + block])

    for n, block in enumerate((1, 2)):
        set_side(2 * n, block, t_cols_n)
        set_side(2 * n + 1, block, t_cols_s)
    set_side(4, 3, a_cols_n)
    set_side(5, 3, a_cols_s)
    north_n = jnp.concatenate([a_cols_n[8], a_cols_n[9]], axis=0)
    north_s = jnp.concatenate([a_cols_s[8], a_cols_s[9]], axis=0)

    def beyond(north_side, south_side, level, rows):
        shift = COLS - 2 * level
        return jnp.where(
            lane[:rows] < 64,
            pltpu.roll(north_side, shift & 127, 1),
            pltpu.roll(south_side, (shift + 126) & 127, 1),
        )

    def end_rows(rows_e, rows_w, at, j):
        return jnp.where(sub < 4, roll(rows_e[at], -2 * j, 0), roll(rows_w[at], 6 - 2 * j, 0))

    def widened(own, rows_e, rows_w, at, j, side, level):
        main = jnp.concatenate([own, end_rows(rows_e, rows_w, at, j)], axis=0)
        return jnp.concatenate([main, beyond(sides[side], sides[side + 1], level, 24)], axis=1)

    last = bottom[...]

    def wet_body(group, _):
        for j in range(4):
            level = group * 4 + j
            wet = jnp.where(last > level, mask[level], 0).astype(F32)
            wet_wide[level] = widened(
                wet, a_rows_e, a_rows_w, 11 + 2 * GROUPS + group, j, 4, level
            )
        return 0

    lax.fori_loop(0, GROUPS, wet_body, 0)
    wet_wide[LEVELS] = jnp.zeros((24, 2 * COLS), F32)

    weights = coefficients(gathered[...])
    weights = [jnp.concatenate([jnp.concatenate([w] * 4, axis=0)] * 2, axis=1) for w in weights]
    full = sum(weights[k] * basis[k] for k in range(4))
    sub2 = iota((8, 2 * COLS), 0)
    multiplier = jnp.concatenate(
        [full[:ROWS], jnp.where(sub2 < 4, full[16:24], full[24:32])], axis=0
    )
    surface = diag[...] * full[:ROWS, :COLS]
    new_surface[...] = surface

    zero = jnp.zeros((24, 2 * COLS), F32)

    def forward(group, carry):
        up, ratio, pt, ps, wet = carry
        for j in range(4):
            level = group * 4 + j
            below = wet_wide[level + 1]
            down = mix[level] * (wet * below)
            inverse = 1.0 / ((1.0 + up + down) - up * ratio)
            t = widened(temp[level], t_rows_e, t_rows_w, skip + group, j, 0, level)
            s = widened(salt[level], t_rows_e, t_rows_w, skip + GROUPS + group, j, 2, level)
            wm = wet * multiplier
            pt = (t + thermal[level] * wm + up * pt) * inverse
            ps = (s - haline[level] * wm + up * ps) * inverse
            ratio = down * inverse
            part_t[level] = pt
            part_s[level] = ps
            ratios[level] = ratio
            up = down
            wet = below
        return up, ratio, pt, ps, wet

    lax.fori_loop(0, GROUPS, forward, (zero, zero, zero, zero, wet_wide[0]))

    def ends(v):
        return pltpu.roll(v, v.shape[0] - 1, 0), pltpu.roll(v, 1, 0)

    def flanks(v):
        return pltpu.roll(v, 2 * COLS - 1, 1), pltpu.roll(v, 1, 1)

    def backward(count, carry):
        xt, xs, total, packs = carry
        group = GROUPS - 1 - count
        for j in (3, 2, 1, 0):
            level = group * 4 + j
            ratio = ratios[level]
            xt = part_t[level] + ratio * xt
            xs = part_s[level] + ratio * xs
            wet = wet_wide[level]
            we, ww = ends(wet)
            wn, ws = flanks(wet)
            around = wet * ((we + ww) + (wn + ws))
            at = 11 + 3 * GROUPS + group
            fe = jnp.concatenate([east[level], end_rows(a_rows_e, a_rows_w, at, j)], axis=0)
            fn = jnp.concatenate(
                [north[level], beyond(north_n, north_s, level, ROWS)], axis=1
            )
            own = slice(0, ROWS), slice(0, COLS)
            wet_own = wet[own]
            around_own = around[own]
            diagonal = around_own + wet_own * (
                fe[:ROWS] * (ww - we)[own] + fn[:, :COLS] * (ws - wn)[own]
            )
            done = []
            for x in (xt, xs):
                q = wet * x
                qe, qw = ends(q)
                qn, qs = flanks(q)
                near = (qe + qw) + (qn + qs)
                lap = wet * near - around * x
                le, lw = ends(lap[:, :COLS])
                ln, ls = flanks(lap[:ROWS])
                lap2 = (
                    wet_own * ((le + lw)[:ROWS] + (ln + ls)[:, :COLS]) - around_own * lap[own]
                )
                be, bw = ends(fe * q[:, :COLS])
                dn, ds = flanks(fn * q[:ROWS])
                incoming = near[own] + ((be - bw)[:ROWS] + (dn - ds)[:, :COLS])
                x_own = x[own]
                done.append(
                    x_own + 0.05 * (wet_own * incoming - diagonal * x_own) - 0.01 * lap2
                )
            t, s = done
            new_temp[level] = t
            new_salt[level] = s
            if not final:
                total = total + wet_own * (thermal[level] * t - haline[level] * s)
                for field, cells in enumerate(done):
                    put_rows(row_low, row_high, 7, field, group, j, cells)
                packs = tuple(packed(acc, cells, level) for acc, cells in zip(packs, done))
        return xt, xs, total, packs

    small = jnp.zeros((ROWS, COLS), F32)
    packs = () if final else ((small, small), (small, small))
    xt, xs, total, packs = lax.fori_loop(0, GROUPS, backward, (zero, zero, small, packs))
    if not final:
        refs = row_low, row_high, col_low, col_high
        put_surface(refs, 6, (surface + total,))
        for n, (low, high) in enumerate(packs):
            put_cols(refs, n + 1, low, high)


def shape(*dims):
    return jax.ShapeDtypeStruct(dims, F32)


VMEM = pl.BlockSpec(memory_space=pltpu.VMEM)
HBM = pl.BlockSpec(memory_space=pltpu.HBM)
SMEM = pl.BlockSpec(memory_space=pltpu.SMEM)


def head(*block):
    return pl.BlockSpec(block, lambda i: (0,) * len(block), memory_space=pltpu.VMEM)


def call(kernel, outs, in_specs, out_specs=None, scratch=(), name=None, grid=None):
    extra = {} if grid is None else {"grid": grid}
    return pl.pallas_call(
        kernel,
        out_shape=outs,
        in_specs=in_specs,
        out_specs=[VMEM] * len(outs) if out_specs is None else out_specs,
        scratch_shapes=scratch,
        compiler_params=pltpu.CompilerParams(vmem_limit_bytes=40 * 1024 * 1024),
        name=name,
        **extra,
    )


def message_shapes(surfaces, row_fields, col_fields, corner_fields):
    rows = shape(2 * (1 + corner_fields) + surfaces + GROUPS * row_fields, 8, COLS)
    cols = shape(2 * (1 + col_fields), 8, COLS)
    return [rows, rows, cols, cols]


def solution(mesh):
    nx, ny = mesh.shape["gx"], mesh.shape["gy"]
    devices = nx * ny
    both = ("gx", "gy")
    eastward = [(i, (i + 1) % nx) for i in range(nx)]
    northward = [(j, j + 1) for j in range(ny - 1)]

    def back(pairs):
        return [(b, a) for a, b in pairs]

    def exchange(messages, corners):
        row_low, row_high, col_low, col_high = messages
        rows_e = lax.ppermute(row_low, "gx", back(eastward))
        rows_w = lax.ppermute(row_high, "gx", eastward)
        own = col_low.shape[0]
        out = shape(own + 2 * corners, 8, COLS)
        to_south, to_north = call(
            forward_kernel, [out, out],
            [head(own, 8, COLS)] * 2 + [head(2 * corners, 8, COLS)] * 2,
            [head(*out.shape)] * 2, name="corners", grid=(1,),
        )(col_low, col_high, rows_e, rows_w)
        cols_n = lax.ppermute(to_south, "gy", back(northward))
        cols_s = lax.ppermute(to_north, "gy", northward)
        return [rows_e, rows_w, cols_n, cols_s]

    def all_sum(block):
        return lax.all_to_all(block, both, 0, 0, tiled=True)

    def surface_specs(rows, cols):
        return [head(rows, 8, COLS)] * 4 + [head(cols, 8, COLS)] * 2

    basis_shape = shape(4, 32, 2 * COLS)
    gram_shape = shape(devices, COLS)
    field = shape(LEVELS, ROWS, COLS)
    tile = shape(ROWS, COLS)

    def whole(*dims):
        return head(*dims)

    def per_device(
        sens_temp, sens_salt, sens_surface, flow_east, flow_north, mix_profile,
        thermal_weight, haline_weight, surface_diag, land_mask, bottom_level,
    ):
        first = call(
            prepare_kernel, message_shapes(3, 4, 4, 3), [SMEM] * 2 + [HBM] * 5 + [VMEM] * 3,
            scratch=[pltpu.VMEM((LEVELS, ROWS, COLS), F32)] * 4
            + [
                pltpu.VMEM((LEVELS, ROWS, COLS), jnp.int32),
                pltpu.SemaphoreType.DMA((5, LEVELS // CHUNK)),
            ],
            name="prepare",
        )(
            thermal_weight, haline_weight, sens_temp, sens_salt, flow_east, flow_north,
            land_mask, bottom_level, sens_surface, surface_diag,
        )
        got = exchange(first, 4)
        basis, gram, fixed = call(
            first_surface_kernel,
            [basis_shape, gram_shape, shape(2, 32, 2 * COLS)],
            surface_specs(11, 18),
            [whole(4, 32, 2 * COLS), whole(devices, COLS), whole(2, 32, 2 * COLS)],
            name="first_surface",
            grid=(1,),
        )(first[0], first[1], *got)
        gathered = all_sum(gram)

        scratch = [
            pltpu.VMEM((LEVELS + 1, 24, 2 * COLS), F32),
            pltpu.VMEM((LEVELS, 24, 2 * COLS), F32),
            pltpu.VMEM((LEVELS, 24, 2 * COLS), F32),
            pltpu.VMEM((LEVELS, 24, 2 * COLS), F32),
            pltpu.VMEM((6, 24, COLS), F32),
        ]

        def step(final, temp, salt, basis, gathered, more, outs):
            return call(
                functools.partial(step_kernel, final),
                outs,
                [SMEM] * 3 + [VMEM] * (13 + len(more)),
                scratch=scratch,
                name="last_step" if final else "first_step",
            )(
                mix_profile, thermal_weight, haline_weight, temp, salt, flow_east, flow_north,
                land_mask, bottom_level, surface_diag, basis, gathered, *got, *more,
            )

        temp, salt, _, *second = step(
            False, sens_temp, sens_salt, basis, gathered, [],
            [field, field, tile] + message_shapes(1, 2, 2, 2),
        )
        more = exchange(second, 3)
        basis, gram = call(
            next_surface_kernel,
            [basis_shape, gram_shape],
            surface_specs(7, 12) + [whole(2, 32, 2 * COLS)],
            [whole(4, 32, 2 * COLS), whole(devices, COLS)],
            name="next_surface",
            grid=(1,),
        )(second[0], second[1], *more, fixed)
        gathered = all_sum(gram)
        return tuple(step(True, temp, salt, basis, gathered, more, [field, field, tile]))

    in_specs = (
        P(None, "gx", "gy"),
        P(None, "gx", "gy"),
        P("gx", "gy"),
        P(None, "gx", "gy"),
        P(None, "gx", "gy"),
        P(),
        P(),
        P(),
        P("gx", "gy"),
        P(None, "gx", "gy"),
        P("gx", "gy"),
    )
    out_specs = (P(None, "gx", "gy"), P(None, "gx", "gy"), P("gx", "gy"))
    return jax.shard_map(
        per_device, mesh=mesh, in_specs=in_specs, out_specs=out_specs, check_vma=False
    )
```

```python
import functools

import jax
import jax.numpy as jnp
from jax import lax
from jax.experimental import pallas as pl
from jax.experimental.pallas import tpu as pltpu
from jax.sharding import PartitionSpec as P

LEVELS = 48
ROWS = 16
COLS = 128
GROUPS = LEVELS // 4
CHUNK = 12
F32 = jnp.float32
PAIRS = [(i, j) for i in range(4) for j in range(i, 5)]


def two_sum(a, b):
    s = a + b
    t = s - a
    return s, (a - (s - t)) + (b - t)


def fast_two_sum(a, b):
    s = a + b
    return s, b - (s - a)


def split(a):
    c = a * 4097.0
    high = c - (c - a)
    return high, a - high


def two_prod(a, b, a_parts=None, b_parts=None):
    ah, al = split(a) if a_parts is None else a_parts
    bh, bl = split(b) if b_parts is None else b_parts
    p = a * b
    return p, ((ah * bh - p) + ah * bl + al * bh) + al * bl


def pair_add(x, y):
    s, t = two_sum(x[0], y[0])
    return fast_two_sum(s, t + (x[1] + y[1]))


def pair_mul(x, y):
    p, e = two_prod(x[0], y[0])
    return fast_two_sum(p, e + (x[0] * y[1] + x[1] * y[0]))


def pair_neg(x):
    return -x[0], -x[1]


def pair_div(x, y):
    first = x[0] / y[0]
    p, e = two_prod(first, y[0])
    rest = ((x[0] - p) - e + x[1]) - first * y[1]
    return fast_two_sum(first, rest / y[0])


def roll(x, shift, axis):
    shift = shift % x.shape[axis]
    return x if shift == 0 else pltpu.roll(x, shift, axis)


def iota(shape, axis):
    return lax.broadcasted_iota(jnp.int32, shape, axis)


A_CORNERS, T_CORNERS = 6, 3
A_SURFACE, T_SURFACE = 2 * A_CORNERS, 2 * T_CORNERS
A_ROWS, T_ROWS = A_SURFACE + 3, T_SURFACE + 1


def put_rows(low_ref, high_ref, first, field, group, j, cells):
    at = first + field * GROUPS + group
    low_ref[at, 2 * j : 2 * j + 2, :] = cells[:2]
    high_ref[at, 2 * j : 2 * j + 2, :] = cells[ROWS - 2 :]


def packed(acc, cells, level):
    low, high = acc
    mine = lax.shift_right_logical(iota((ROWS, COLS), 1), 1) == level
    low = jnp.where(mine, pltpu.roll(cells, 2 * level, 1), low)
    high = jnp.where(mine, pltpu.roll(cells, 2 * level + 2, 1), high)
    return low, high


def put_surface(refs, first, fields):
    row_low, row_high, col_low, col_high = refs
    low = jnp.zeros((ROWS, COLS), F32)
    high = low
    lane_group = iota((ROWS, COLS), 1) // 8
    for n, cells in enumerate(fields):
        row_low[first + n] = cells[:8]
        row_high[first + n] = cells[8:]
        low = jnp.where(lane_group == n, roll(cells, 8 * n, 1), low)
        high = jnp.where(lane_group == n, roll(cells, 8 * n + 8, 1), high)
    put_cols(refs, 0, low, high)


def put_cols(refs, n, low, high):
    row_low, row_high, col_low, col_high = refs
    count = corners_of(row_low)
    for col, side, cells in ((col_low, 0, low), (col_high, count, high)):
        col[2 * n] = cells[:8]
        col[2 * n + 1] = cells[8:]
        if n < count:
            row_low[side + n] = cells[:8]
            row_high[side + n] = cells[8:]


def corners_of(rows):
    return A_CORNERS if rows.shape[0] == A_ROWS + 6 * GROUPS else T_CORNERS


def forward_kernel(own_low, own_high, rows_e, rows_w, to_south, to_north):
    count = rows_e.shape[0] // 2
    own = own_low.shape[0]
    for out, mine, side in ((to_south, own_low, 0), (to_north, own_high, count)):
        out[:own] = mine[...]
        out[own : own + count] = rows_e[side : side + count]
        out[own + count :] = rows_w[side : side + count]


def wet_at(mask, last, level):
    return jnp.where(last > level, mask[jnp.minimum(level, LEVELS - 1)], 0).astype(F32)


def prepare_kernel(
    mix, thermal, haline, temp_in, salt_in, east_in, north_in, mask_in, bottom, surface, diag,
    row_low, row_high, col_low, col_high, *rest,
):
    solved, (inverses, ratios, temp, salt, east, north, mask, sems) = rest[:4], rest[4:]
    last = bottom[...]
    zero = jnp.zeros((ROWS, COLS), F32)
    pair = (zero, zero)
    fields = list(
        zip((mask_in, temp_in, salt_in, east_in, north_in), (mask, temp, salt, east, north))
    )

    def copy(n, part):
        source, target = fields[n]
        levels = pl.ds(part * CHUNK, CHUNK)
        return pltpu.make_async_copy(source.at[levels], target.at[levels], sems.at[n, part])

    parts = LEVELS // CHUNK
    for part in range(parts):
        copy(0, part).start()
    for part in range(parts):
        for n in range(1, 5):
            copy(n, part).start()

    def down_body(group, carry):
        total, depth, up, ratio, values, wet, packs = carry
        for j in range(4):
            level = group * 4 + j
            below = wet_at(mask, last, level + 1)
            down = mix[level] * (wet * below)
            inverse = 1.0 / ((1.0 + up + down) - up * ratio)
            t, s = temp[level], salt[level]
            tw, hw = thermal[level] * wet, haline[level] * wet
            total = total + (tw * t - hw * s)
            depth = depth + wet
            values = tuple((r + up * v) * inverse for r, v in zip((t, s, tw, hw), values))
            for ref, v in zip(solved, values):
                ref[level] = v
            ratio = down * inverse
            inverses[level] = inverse
            ratios[level] = ratio
            put_rows(row_low, row_high, A_ROWS, 2, group, j, wet)
            put_rows(row_low, row_high, A_ROWS, 5, group, j, east[level])
            packs = tuple(packed(acc, v, level) for acc, v in zip(packs, (wet, north[level])))
            up = down
            wet = below
        return total, depth, up, ratio, values, wet, packs

    for part in range(parts):
        copy(0, part).wait()
    carry = (zero, zero, zero, zero, (zero,) * 4, wet_at(mask, last, 0), (pair, pair))
    step = CHUNK // 4
    for part in range(parts):
        for n in range(1, 5):
            copy(n, part).wait()
        carry = lax.fori_loop(part * step, (part + 1) * step, down_body, carry)
    total, depth, _, _, _, _, packs = carry
    refs = row_low, row_high, col_low, col_high
    put_surface(refs, A_SURFACE, (surface[...] + total, depth / LEVELS, diag[...]))
    put_cols(refs, 3, *packs[0])
    put_cols(refs, 6, *packs[1])
    back_substitute(refs, A_ROWS, solved, ratios, ((0, 1), (1, 2), (3, 4), (4, 5)))


def back_substitute(refs, first, solved, ratios, places):
    row_low, row_high = refs[:2]
    zero = jnp.zeros((ROWS, COLS), F32)

    def up_body(count, carry):
        values, packs = carry
        group = GROUPS - 1 - count
        for j in (3, 2, 1, 0):
            level = group * 4 + j
            ratio = ratios[level]
            values = tuple(ref[level] + ratio * v for ref, v in zip(solved, values))
            for ref, v, (field, _) in zip(solved, values, places):
                ref[level] = v
                put_rows(row_low, row_high, first, field, group, j, v)
            packs = tuple(packed(acc, v, level) for acc, v in zip(packs, values))
        return values, packs

    n = len(places)
    _, packs = lax.fori_loop(0, GROUPS, up_body, ((zero,) * n, ((zero, zero),) * n))
    for (_, block), acc in zip(places, packs):
        put_cols(refs, block, *acc)


def wide_surface(n, own, rows_e, rows_w, from_north, from_south):
    main = jnp.concatenate([own, rows_e, rows_w], axis=0)
    to_north = jnp.concatenate(from_north, axis=0)
    to_south = jnp.concatenate(from_south, axis=0)
    lane = iota((32, COLS), 1)
    side = jnp.where(
        lane < 8,
        roll(to_north, -8 * n, 1),
        jnp.where(lane >= COLS - 8, roll(to_south, 120 - 8 * n, 1), 0.0),
    )
    return jnp.concatenate([main, side], axis=1)


def krylov(c, diag, depth, basis_ref, gram_ref):
    def nb(v):
        return pltpu.roll(v, 31, 0), pltpu.roll(v, 1, 0), pltpu.roll(v, 255, 1), pltpu.roll(v, 1, 1)

    faces = [jnp.minimum(depth, d) for d in nb(depth)]
    centre = (diag - 1.0) + ((faces[0] + faces[1]) + (faces[2] + faces[3]))
    v = c
    own = []
    for k in range(5):
        if k < 4:
            basis_ref[k] = v
        mine = v[:ROWS, :COLS]
        own.append((mine, split(mine)))
        if k < 4:
            e, w, n, s = nb(v)
            v = centre * v - ((faces[0] * e + faces[1] * w) + (faces[2] * n + faces[3] * s))
    highs, lows = [], []
    for i, j in PAIRS:
        p, e = two_prod(own[i][0], own[j][0], own[i][1], own[j][1])
        s, t = two_sum(p[:8], p[8:])
        highs.append(s)
        lows.append(t + (e[:8] + e[8:]))
    pad = [jnp.zeros((8, COLS), F32)] * (16 - len(PAIRS))
    high = jnp.concatenate(highs + pad, axis=0).T
    low = jnp.concatenate(lows + pad, axis=0).T
    parts = [(high[8 * n : 8 * n + 8], low[8 * n : 8 * n + 8]) for n in range(16)]
    while len(parts) > 1:
        parts = [pair_add(a, b) for a, b in zip(parts[::2], parts[1::2])]
    total = parts[0]
    for shift in (4, 2, 1):
        total = pair_add(total, tuple(roll(x, shift, 0) for x in total))
    total = pair_add(total, tuple(roll(x, 124, 1) for x in total))
    first_half = (iota((8, COLS), 1) % 8) < 4
    sums = jnp.where(first_half, total[0], roll(total[1], 4, 1))
    gram_ref[...] = jnp.concatenate([sums] * (gram_ref.shape[0] // 8), axis=0)


def surface_fields(low, high, rows_e, rows_w, cols_n, cols_s, count):
    corners = A_CORNERS if count == 3 else T_CORNERS
    first = 2 * corners

    def column(cols):
        own = cols.shape[0] - 2 * corners
        return [cols[0], cols[1], cols[own], cols[own + corners]]

    return [
        wide_surface(
            n, jnp.concatenate([low[first + n], high[first + n]], axis=0),
            rows_e[first + n], rows_w[first + n], column(cols_n), column(cols_s),
        )
        for n in range(count)
    ]


def first_surface_kernel(low, high, rows_e, rows_w, cols_n, cols_s, basis, gram, fixed):
    c, depth, diag = surface_fields(low, high, rows_e, rows_w, cols_n, cols_s, 3)
    fixed[0] = depth
    fixed[1] = diag
    krylov(c, diag, depth, basis, gram)


def next_surface_kernel(low, high, rows_e, rows_w, cols_n, cols_s, fixed, basis, gram):
    (c,) = surface_fields(low, high, rows_e, rows_w, cols_n, cols_s, 1)
    krylov(c, fixed[1], fixed[0], basis, gram)


def coefficients(gathered):
    parts = [(gathered[8 * n : 8 * n + 8], None) for n in range(gathered.shape[0] // 8)]
    parts = [(p, jnp.zeros_like(p)) for p, _ in parts]
    while len(parts) > 1:
        parts = [pair_add(a, b) for a, b in zip(parts[::2], parts[1::2])]
    total = parts[0]
    for shift in (4, 2, 1):
        total = pair_add(total, tuple(roll(x, shift, 0) for x in total))
    for shift in (4, 2, 1):
        total = pair_add(total, tuple(roll(x, COLS - shift, 1) for x in total))
    table = {}
    for n, (i, j) in enumerate(PAIRS):
        entry = tuple(jnp.broadcast_to(x[:, 8 * n : 8 * n + 1], (8, COLS)) for x in total)
        table[i, j] = table[j, i] = entry
    one = (jnp.ones((8, COLS), F32), jnp.zeros((8, COLS), F32))
    r, p, x = [one], [one], []
    rr = table[0, 0]
    for it in range(4):
        image = [p[0]] + [pair_add(p[k], p[k - 1]) for k in range(1, it + 1)] + [p[it]]
        dot = functools.reduce(
            pair_add, [pair_mul(table[it, k], image[k]) for k in range(it + 2)]
        )
        step = pair_div(rr, pair_mul(p[it], dot))
        x = [
            pair_add(x[k], pair_mul(step, p[k])) if k < len(x) else pair_mul(step, p[k])
            for k in range(it + 1)
        ]
        if it < 3:
            minus = pair_neg(step)
            moved = [pair_mul(minus, a) for a in image]
            r = [pair_add(r[k], moved[k]) if k < len(r) else moved[k] for k in range(it + 2)]
            dot = functools.reduce(
                pair_add, [pair_mul(table[it + 1, k], r[k]) for k in range(it + 2)]
            )
            new = pair_mul(r[it + 1], dot)
            ratio = pair_div(new, rr)
            p = [
                pair_add(r[k], pair_mul(ratio, p[k])) if k < len(p) else r[k]
                for k in range(it + 2)
            ]
            rr = new
    return [a[0] for a in x]


class Halo:
    def __init__(self, refs, first, corners):
        self.low, self.high, self.own_s, self.own_n, self.e, self.w, self.n, self.s = refs
        self.first, self.corners = first, corners
        self.even_row = iota((8, COLS), 0) % 2 == 0
        self.even_lane = iota((8, COLS), 1) % 2 == 0
        self.sub = iota((8, COLS), 0)

    def rows(self, field, group):
        at = self.first + field * GROUPS + group
        e, w = self.e[at], self.w[at]
        return (
            jnp.where(self.even_row, roll(self.high[at], -1, 0), roll(self.low[at], 1, 0)),
            jnp.where(self.even_row, e, w),
            jnp.where(self.even_row, roll(e, -1, 0), roll(w, 1, 0)),
        )

    def edge_rows(self, field, group):
        at = self.first + field * GROUPS + group
        return jnp.where(self.even_row, self.e[at], self.w[at])

    def edge_columns(self, block):
        return jnp.concatenate(
            [
                jnp.where(self.even_lane, self.n[2 * block + h], self.s[2 * block + h])
                for h in range(2)
            ],
            axis=0,
        )

    def columns(self, block):
        inner, outer = [], []
        for h in range(2):
            at = 2 * block + h
            inner.append(
                jnp.where(self.even_lane, roll(self.own_n[at], -1, 1), roll(self.own_s[at], 1, 1))
            )
            outer.append(jnp.where(self.even_lane, roll(self.n[at], -1, 1), roll(self.s[at], 1, 1)))
        east = self.n.shape[0] - 2 * self.corners + block
        west = east + self.corners
        corner = jnp.where(
            self.sub < 4,
            jnp.where(self.even_lane, self.n[east], self.s[east]),
            jnp.where(self.even_lane, self.n[west], self.s[west]),
        )
        return (
            jnp.concatenate(inner, axis=0),
            jnp.concatenate([self.edge_columns(block), corner], axis=0),
            jnp.concatenate(outer, axis=0),
        )


def ends(v):
    return pltpu.roll(v, v.shape[0] - 1, 0), pltpu.roll(v, 1, 0)


def step_kernel(
    final,
    mix, thermal, haline, temp, salt, temp_response, salt_response, east, north, mask, bottom,
    diag, basis, gathered,
    *refs,
):
    a_halo = Halo(refs[:8], A_ROWS, A_CORNERS)
    if final:
        t_halo = Halo(refs[8:16], T_ROWS, T_CORNERS)
        new_temp, new_salt, new_surface = refs[16:]
    else:
        t_halo = a_halo
        inverses, ratios, new_temp, new_salt, row_low, row_high, col_low, col_high = refs[8:]
    tracers = ((temp, temp_response, 0, 3, 1.0), (salt, salt_response, 1, 4, -1.0))

    weights = coefficients(gathered[...])
    weights = [jnp.concatenate([jnp.concatenate([w] * 4, axis=0)] * 2, axis=1) for w in weights]
    full = sum(weights[k] * basis[k] for k in range(4))
    multiplier = full[:ROWS, :COLS]
    surface = diag[...] * multiplier
    if final:
        new_surface[...] = surface

    sub = iota((8, COLS), 0)
    even_row = sub % 2 == 0
    ring = jnp.concatenate([full[:ROWS], jnp.where(
        iota((8, 2 * COLS), 0) < 4, full[16:24], full[24:])], axis=0)
    even_lane = iota((24, COLS), 1) % 2 == 0

    def lanes(a, b):
        return jnp.where(
            even_lane,
            jnp.broadcast_to(ring[:, a : a + 1], (24, COLS)),
            jnp.broadcast_to(ring[:, b : b + 1], (24, COLS)),
        )

    def both_rows(a, b):
        return jnp.where(
            even_row,
            jnp.broadcast_to(full[a : a + 1, :COLS], (8, COLS)),
            jnp.broadcast_to(full[b : b + 1, :COLS], (8, COLS)),
        )

    column_m = [lanes(127, 0)[:ROWS], lanes(128, 255), lanes(129, 254)[:ROWS]]
    row_m = [both_rows(15, 0), both_rows(16, 31), both_rows(17, 30)]

    own = slice(0, ROWS)
    lane_sign = jnp.where(even_lane[own], 0.05, -0.05)
    wet0, wet1, wet2 = a_halo.columns(3)
    north1 = lane_sign * a_halo.edge_columns(6)
    e, w = ends(wet1)
    around1 = wet1[own] * ((e + w)[own] + (wet0 + wet2))
    column_wet = wet1
    column_q, column_out = [], []
    for _, _, field, response, sign in tracers:
        g = [
            b + (sign * m) * a
            for b, m, a in zip(t_halo.columns(field + 1), column_m, a_halo.columns(response + 1))
        ]
        q = wet1 * g[1]
        e, w = ends(q)
        near = (e + w)[own] + (wet0 * g[0] + wet2 * g[2])
        lap = wet1[own] * near - around1 * g[1][own]
        column_q.append(q)
        column_out.append(north1 * q[own] - 0.01 * lap)

    def corner_rows(v):
        return jnp.where(
            even_row,
            jnp.broadcast_to(v[16:17], (8, COLS)),
            jnp.broadcast_to(v[23:24], (8, COLS)),
        )

    corner_wet = corner_rows(column_wet)
    corner_q = [corner_rows(q) for q in column_q]
    column_wet = column_wet[own]
    column_q = [q[own] for q in column_q]

    lane8 = iota((8, COLS), 1)
    lane = iota((ROWS, COLS), 1)
    row = iota((ROWS, COLS), 0)
    row_sign = jnp.where(even_row, 0.05, -0.05)
    last = bottom[...]

    def beside(v, corner):
        return jnp.where(lane8 == COLS - 1, corner, pltpu.roll(v, COLS - 1, 1)) + jnp.where(
            lane8 == 0, corner, pltpu.roll(v, 1, 1)
        )

    def strips(group):
        shifts = [(127 - 2 * (group * 4 + j)) & 127 for j in range(4)]

        def corners(v):
            out = pltpu.roll(v, shifts[0], 1)
            for j in range(1, 4):
                out = jnp.where(sub // 2 == j, pltpu.roll(v, shifts[j], 1), out)
            return out

        wet0, wet1, wet2 = a_halo.rows(2, group)
        east1 = row_sign * a_halo.edge_rows(5, group)
        around1 = wet1 * ((wet0 + wet2) + beside(wet1, corners(corner_wet)))
        qs, outs = [], []
        for n, (_, _, field, response, sign) in enumerate(tracers):
            g = [
                b + (sign * m) * a
                for b, m, a in zip(
                    t_halo.rows(field, group), row_m, a_halo.rows(response, group)
                )
            ]
            q = wet1 * g[1]
            near = (wet0 * g[0] + wet2 * g[2]) + beside(q, corners(corner_q[n]))
            lap = wet1 * near - around1 * g[1]
            qs.append(q)
            outs.append(east1 * q - 0.01 * lap)
        return wet1, qs, outs

    def body(group, carry):
        row_wet, row_q, row_out = strips(group)
        for j in range(4):
            level = group * 4 + j
            shift = (127 - 2 * level) & 127

            def four(ve, vw, vn, vs, row_strip, column_strip):
                r = roll(row_strip, 7 - 2 * j, 0)
                r = jnp.concatenate([r, r], axis=0)
                c = pltpu.roll(column_strip, shift, 1)
                return (
                    jnp.where(row == ROWS - 1, r, pltpu.roll(ve, ROWS - 1, 0)),
                    jnp.where(row == 0, r, pltpu.roll(vw, 1, 0)),
                    jnp.where(lane == COLS - 1, c, pltpu.roll(vn, COLS - 1, 1)),
                    jnp.where(lane == 0, c, pltpu.roll(vs, 1, 1)),
                )

            wet = wet_at(mask, last, level)
            fe, fn = east[level], north[level]
            we, ww, wn, ws = four(wet, wet, wet, wet, row_wet, column_wet)
            around = wet * ((we + ww) + (wn + ws))
            diagonal = around + wet * (fe * (ww - we) + fn * (ws - wn))
            done = []
            for n, (field, response, _, _, sign) in enumerate(tracers):
                g = field[level] + (sign * multiplier) * response[level]
                q = wet * g
                e, w, no, so = four(q, q, q, q, row_q[n], column_q[n])
                near = wet * ((e + w) + (no + so))
                small = 0.01 * (near - around * g)
                u, v = (0.05 * fe) * q, (0.05 * fn) * q
                e, w, no, so = four(
                    u - small, -u - small, v - small, -v - small, row_out[n], column_out[n]
                )
                done.append(
                    (g + 0.05 * (near - diagonal * g))
                    + (wet * ((e + w) + (no + so)) + around * small)
                )
            t, s = done
            if final:
                new_temp[level] = t
                new_salt[level] = s
            else:
                above, total, pt, ps = carry
                total = total + wet * (thermal[level] * t - haline[level] * s)
                up = mix[jnp.maximum(level - 1, 0)] * (above * wet)
                inverse = inverses[level]
                pt = (t + up * pt) * inverse
                ps = (s + up * ps) * inverse
                new_temp[level] = pt
                new_salt[level] = ps
                carry = (wet, total, pt, ps)
        return carry

    zero = jnp.zeros((ROWS, COLS), F32)
    if final:
        lax.fori_loop(0, GROUPS, body, 0)
    else:
        _, total, _, _ = lax.fori_loop(0, GROUPS, body, (zero,) * 4)
        messages = row_low, row_high, col_low, col_high
        put_surface(messages, T_SURFACE, (surface + total,))
        back_substitute(messages, T_ROWS, (new_temp, new_salt), ratios, ((0, 1), (1, 2)))


def shape(*dims):
    return jax.ShapeDtypeStruct(dims, F32)


VMEM = pl.BlockSpec(memory_space=pltpu.VMEM)
HBM = pl.BlockSpec(memory_space=pltpu.HBM)
SMEM = pl.BlockSpec(memory_space=pltpu.SMEM)


def head(*block):
    return pl.BlockSpec(block, lambda i: (0,) * len(block), memory_space=pltpu.VMEM)


def call(kernel, outs, in_specs, out_specs=None, scratch=(), name=None, grid=None, room=40):
    extra = {} if grid is None else {"grid": grid}
    return pl.pallas_call(
        kernel,
        out_shape=outs,
        in_specs=in_specs,
        out_specs=[VMEM] * len(outs) if out_specs is None else out_specs,
        scratch_shapes=scratch,
        compiler_params=pltpu.CompilerParams(vmem_limit_bytes=room * 1024 * 1000),
        name=name,
        **extra,
    )


def message_shapes(surfaces, row_fields, col_fields, corner_fields):
    rows = shape(2 * (1 + corner_fields) + surfaces + GROUPS * row_fields, 8, COLS)
    cols = shape(2 * (1 + col_fields), 8, COLS)
    return [rows, rows, cols, cols]


def solution(mesh):
    nx, ny = mesh.shape["gx"], mesh.shape["gy"]
    devices = nx * ny
    both = ("gx", "gy")
    eastward = [(i, (i + 1) % nx) for i in range(nx)]
    northward = [(j, j + 1) for j in range(ny - 1)]

    def back(pairs):
        return [(b, a) for a, b in pairs]

    def exchange(messages, corners):
        row_low, row_high, col_low, col_high = messages
        rows_e = lax.ppermute(row_low, "gx", back(eastward))
        rows_w = lax.ppermute(row_high, "gx", eastward)
        own = col_low.shape[0]
        out = shape(own + 2 * corners, 8, COLS)
        to_south, to_north = call(
            forward_kernel, [out, out],
            [head(own, 8, COLS)] * 2 + [head(2 * corners, 8, COLS)] * 2,
            [head(*out.shape)] * 2, name="corners", grid=(1,),
        )(col_low, col_high, rows_e, rows_w)
        cols_n = lax.ppermute(to_south, "gy", back(northward))
        cols_s = lax.ppermute(to_north, "gy", northward)
        return [rows_e, rows_w, cols_n, cols_s]

    def all_sum(block):
        return lax.all_to_all(block, both, 0, 0, tiled=True)

    def surface_specs(rows, cols):
        return [head(rows, 8, COLS)] * 4 + [head(cols, 8, COLS)] * 2

    basis_shape = shape(4, 32, 2 * COLS)
    gram_shape = shape(devices, COLS)
    field = shape(LEVELS, ROWS, COLS)
    tile = shape(ROWS, COLS)

    def whole(*dims):
        return head(*dims)

    def per_device(
        sens_temp, sens_salt, sens_surface, flow_east, flow_north, mix_profile,
        thermal_weight, haline_weight, surface_diag, land_mask, bottom_level,
    ):
        *first, temp, salt, temp_response, salt_response, inverses, ratios = call(
            prepare_kernel, message_shapes(3, 6, 6, 5) + [field] * 6,
            [SMEM] * 3 + [HBM] * 5 + [VMEM] * 3,
            scratch=[pltpu.VMEM((LEVELS, ROWS, COLS), F32)] * 4
            + [
                pltpu.VMEM((LEVELS, ROWS, COLS), jnp.int32),
                pltpu.SemaphoreType.DMA((5, LEVELS // CHUNK)),
            ],
            name="prepare",
            room=62,
        )(
            mix_profile, thermal_weight, haline_weight, sens_temp, sens_salt, flow_east,
            flow_north, land_mask, bottom_level, sens_surface, surface_diag,
        )
        got = exchange(first, A_CORNERS)
        basis, gram, fixed = call(
            first_surface_kernel,
            [basis_shape, gram_shape, shape(2, 32, 2 * COLS)],
            surface_specs(A_ROWS, 2 * 7 + 2 * A_CORNERS),
            [head(4, 32, 2 * COLS), head(devices, COLS), head(2, 32, 2 * COLS)],
            name="first_surface",
            grid=(1,),
        )(first[0], first[1], *got)
        gathered = all_sum(gram)

        def step(final, temp, salt, basis, gathered, more, outs):
            return call(
                functools.partial(step_kernel, final),
                outs,
                [SMEM] * 3 + [VMEM] * (19 + len(more)),
                name="last_step" if final else "first_step",
            )(
                mix_profile, thermal_weight, haline_weight, temp, salt, temp_response,
                salt_response, flow_east, flow_north, land_mask, bottom_level, surface_diag,
                basis, gathered, *first, *got, *more,
            )

        temp, salt, *second = step(
            False, temp, salt, basis, gathered, [inverses, ratios],
            [field, field] + message_shapes(1, 2, 2, 2),
        )
        more = exchange(second, T_CORNERS)
        basis, gram = call(
            next_surface_kernel,
            [basis_shape, gram_shape],
            surface_specs(T_ROWS, 2 * 3 + 2 * T_CORNERS) + [head(2, 32, 2 * COLS)],
            [head(4, 32, 2 * COLS), head(devices, COLS)],
            name="next_surface",
            grid=(1,),
        )(second[0], second[1], *more, fixed)
        gathered = all_sum(gram)
        return tuple(
            step(True, temp, salt, basis, gathered, [*second, *more], [field, field, tile])
        )

    in_specs = (
        P(None, "gx", "gy"),
        P(None, "gx", "gy"),
        P("gx", "gy"),
        P(None, "gx", "gy"),
        P(None, "gx", "gy"),
        P(),
        P(),
        P(),
        P("gx", "gy"),
        P(None, "gx", "gy"),
        P("gx", "gy"),
    )
    out_specs = (P(None, "gx", "gy"), P(None, "gx", "gy"), P("gx", "gy"))
    return jax.shard_map(
        per_device, mesh=mesh, in_specs=in_specs, out_specs=out_specs, check_vma=False
    )
```

```python
import functools

import jax
import jax.numpy as jnp
from jax import lax
from jax.experimental import pallas as pl
from jax.experimental.pallas import tpu as pltpu
from jax.sharding import PartitionSpec as P

LEVELS = 48
ROWS = 16
COLS = 128
GROUPS = LEVELS // 4
CHUNK = 12
F32 = jnp.float32
PAIRS = [(i, j) for i in range(4) for j in range(i, 5)]


def two_sum(a, b):
    s = a + b
    t = s - a
    return s, (a - (s - t)) + (b - t)


def fast_two_sum(a, b):
    s = a + b
    return s, b - (s - a)


def split(a):
    c = a * 4097.0
    high = c - (c - a)
    return high, a - high


def two_prod(a, b, a_parts=None, b_parts=None):
    ah, al = split(a) if a_parts is None else a_parts
    bh, bl = split(b) if b_parts is None else b_parts
    p = a * b
    return p, ((ah * bh - p) + ah * bl + al * bh) + al * bl


def pair_add(x, y):
    s, t = two_sum(x[0], y[0])
    return fast_two_sum(s, t + (x[1] + y[1]))


def pair_scale(x, c):
    p, e = two_prod(x[0], c)
    return fast_two_sum(p, e + x[1] * c)


def pair_dot(xs, ys):
    terms, rest = [], []
    for x, y in zip(xs, ys):
        p, e = two_prod(x[0], y[0])
        terms.append(p)
        rest.append(e + (x[0] * y[1] + x[1] * y[0]))
    while len(terms) > 1:
        sums = [two_sum(a, b) for a, b in zip(terms[::2], terms[1::2])]
        rest += [e for _, e in sums]
        terms = [s for s, _ in sums] + terms[len(sums) * 2 :]
    while len(rest) > 1:
        rest = [a + b for a, b in zip(rest[::2], rest[1::2])] + rest[len(rest) // 2 * 2 :]
    return terms[0] + rest[0]


def roll(x, shift, axis):
    shift = shift % x.shape[axis]
    return x if shift == 0 else pltpu.roll(x, shift, axis)


def iota(shape, axis):
    return lax.broadcasted_iota(jnp.int32, shape, axis)


A_CORNERS, T_CORNERS = 6, 3
A_SURFACE, T_SURFACE = 2 * A_CORNERS, 2 * T_CORNERS
A_ROWS, T_ROWS = A_SURFACE + 3, T_SURFACE + 1


def put_rows(low_ref, high_ref, first, field, group, j, cells):
    at = first + field * GROUPS + group
    low_ref[at, 2 * j : 2 * j + 2, :] = cells[:2]
    high_ref[at, 2 * j : 2 * j + 2, :] = cells[ROWS - 2 :]


def packed(acc, cells, level):
    low, high = acc
    mine = lax.shift_right_logical(iota((ROWS, COLS), 1), 1) == level
    low = jnp.where(mine, pltpu.roll(cells, 2 * level, 1), low)
    high = jnp.where(mine, pltpu.roll(cells, 2 * level + 2, 1), high)
    return low, high


def put_surface(refs, first, fields):
    row_low, row_high, col_low, col_high = refs
    low = jnp.zeros((ROWS, COLS), F32)
    high = low
    lane_group = iota((ROWS, COLS), 1) // 8
    for n, cells in enumerate(fields):
        row_low[first + n] = cells[:8]
        row_high[first + n] = cells[8:]
        low = jnp.where(lane_group == n, roll(cells, 8 * n, 1), low)
        high = jnp.where(lane_group == n, roll(cells, 8 * n + 8, 1), high)
    put_cols(refs, 0, low, high)


def put_cols(refs, n, low, high):
    row_low, row_high, col_low, col_high = refs
    count = corners_of(row_low)
    for col, side, cells in ((col_low, 0, low), (col_high, count, high)):
        col[2 * n] = cells[:8]
        col[2 * n + 1] = cells[8:]
        if n < count:
            row_low[side + n] = cells[:8]
            row_high[side + n] = cells[8:]


def corners_of(rows):
    return A_CORNERS if rows.shape[0] == A_ROWS + 6 * GROUPS else T_CORNERS


def forward_kernel(own_low, own_high, rows_e, rows_w, to_south, to_north):
    count = rows_e.shape[0] // 2
    own = own_low.shape[0]
    place = lax.axis_index("gy")
    ends_at = 0, lax.axis_size("gy") - 1
    for out, mine, side, end in zip((to_south, to_north), (own_low, own_high), (0, count), ends_at):
        inner = place != end
        out[:own] = jnp.where(inner, mine[...], 0.0)
        out[own : own + count] = jnp.where(inner, rows_e[side : side + count], 0.0)
        out[own + count :] = jnp.where(inner, rows_w[side : side + count], 0.0)


def wet_at(mask, last, level):
    return jnp.where(last > level, mask[jnp.minimum(level, LEVELS - 1)], 0).astype(F32)


def prepare_kernel(
    mix, thermal, haline, temp_in, salt_in, east_in, north_in, mask_in, bottom, surface, diag,
    row_low, row_high, col_low, col_high, *rest,
):
    solved, (inverses, ratios, east, north, mask, temp, salt, sems) = rest[:4], rest[4:]
    last = bottom[...]
    zero = jnp.zeros((ROWS, COLS), F32)
    pair = (zero, zero)
    fields = list(
        zip((mask_in, temp_in, salt_in, east_in, north_in), (mask, temp, salt, east, north))
    )

    def copy(n, part):
        source, target = fields[n]
        levels = pl.ds(part * CHUNK, CHUNK)
        return pltpu.make_async_copy(source.at[levels], target.at[levels], sems.at[n, part])

    parts = LEVELS // CHUNK
    for part in range(parts):
        copy(0, part).start()
    for part in range(parts):
        for n in range(1, 5):
            copy(n, part).start()

    def down_body(group, carry):
        total, depth, up, ratio, values, wet, packs = carry
        for j in range(4):
            level = group * 4 + j
            below = wet_at(mask, last, level + 1)
            down = mix[level] * (wet * below)
            inverse = 1.0 / ((1.0 + up + down) - up * ratio)
            t, s = temp[level], salt[level]
            tw, hw = thermal[level] * wet, haline[level] * wet
            total = total + (tw * t - hw * s)
            depth = depth + wet
            values = tuple((r + up * v) * inverse for r, v in zip((t, s, tw, hw), values))
            for ref, v in zip(solved, values):
                ref[level] = v
            ratio = down * inverse
            inverses[level] = inverse
            ratios[level] = ratio
            put_rows(row_low, row_high, A_ROWS, 2, group, j, wet)
            put_rows(row_low, row_high, A_ROWS, 5, group, j, east[level])
            packs = tuple(packed(acc, v, level) for acc, v in zip(packs, (wet, north[level])))
            up = down
            wet = below
        return total, depth, up, ratio, values, wet, packs

    for part in range(parts):
        copy(0, part).wait()
    carry = (zero, zero, zero, zero, (zero,) * 4, wet_at(mask, last, 0), (pair, pair))
    step = CHUNK // 4
    for part in range(parts):
        for n in range(1, 5):
            copy(n, part).wait()
        carry = lax.fori_loop(part * step, (part + 1) * step, down_body, carry)
    total, depth, _, _, _, _, packs = carry
    refs = row_low, row_high, col_low, col_high
    put_surface(refs, A_SURFACE, (surface[...] + total, depth / LEVELS, diag[...]))
    put_cols(refs, 3, *packs[0])
    put_cols(refs, 6, *packs[1])
    back_substitute(refs, A_ROWS, solved, ratios, ((0, 1), (1, 2), (3, 4), (4, 5)))


def back_substitute(refs, first, solved, ratios, places):
    row_low, row_high = refs[:2]
    zero = jnp.zeros((ROWS, COLS), F32)

    def up_body(count, carry):
        values, packs = carry
        group = GROUPS - 1 - count
        for j in (3, 2, 1, 0):
            level = group * 4 + j
            ratio = ratios[level]
            values = tuple(ref[level] + ratio * v for ref, v in zip(solved, values))
            for ref, v, (field, _) in zip(solved, values, places):
                ref[level] = v
                put_rows(row_low, row_high, first, field, group, j, v)
            packs = tuple(packed(acc, v, level) for acc, v in zip(packs, values))
        return values, packs

    n = len(places)
    _, packs = lax.fori_loop(0, GROUPS, up_body, ((zero,) * n, ((zero, zero),) * n))
    for (_, block), acc in zip(places, packs):
        put_cols(refs, block, *acc)


def wide_surface(n, own, rows_e, rows_w, from_north, from_south):
    main = jnp.concatenate([own, rows_e, rows_w], axis=0)
    to_north = jnp.concatenate(from_north, axis=0)
    to_south = jnp.concatenate(from_south, axis=0)
    lane = iota((32, COLS), 1)
    side = jnp.where(
        lane < 8,
        roll(to_north, -8 * n, 1),
        jnp.where(lane >= COLS - 8, roll(to_south, 120 - 8 * n, 1), 0.0),
    )
    return jnp.concatenate([main, side], axis=1)


def krylov(c, diag, depth, basis_ref, gram_ref):
    def nb(v):
        return pltpu.roll(v, 31, 0), pltpu.roll(v, 1, 0), pltpu.roll(v, 255, 1), pltpu.roll(v, 1, 1)

    faces = [jnp.minimum(depth, d) for d in nb(depth)]
    centre = (diag - 1.0) + ((faces[0] + faces[1]) + (faces[2] + faces[3]))
    v = c
    own = []
    for k in range(5):
        if k < 4:
            basis_ref[k] = v
        mine = v[:ROWS, :COLS]
        own.append((mine, split(mine)))
        if k < 4:
            e, w, n, s = nb(v)
            v = centre * v - ((faces[0] * e + faces[1] * w) + (faces[2] * n + faces[3] * s))
    highs, lows = [], []
    for i, j in PAIRS:
        p, e = two_prod(own[i][0], own[j][0], own[i][1], own[j][1])
        s, t = two_sum(p[:8], p[8:])
        highs.append(s)
        lows.append(t + (e[:8] + e[8:]))
    pad = [jnp.zeros((8, COLS), F32)] * (16 - len(PAIRS))
    high = jnp.concatenate(highs + pad, axis=0).T
    low = jnp.concatenate(lows + pad, axis=0).T
    parts = [(high[8 * n : 8 * n + 8], low[8 * n : 8 * n + 8]) for n in range(16)]
    while len(parts) > 1:
        parts = [pair_add(a, b) for a, b in zip(parts[::2], parts[1::2])]
    total = parts[0]
    for shift in (4, 2, 1):
        total = pair_add(total, tuple(roll(x, shift, 0) for x in total))
    total = pair_add(total, tuple(roll(x, 124, 1) for x in total))
    first_half = (iota((8, COLS), 1) % 8) < 4
    sums = jnp.where(first_half, total[0], roll(total[1], 4, 1))
    gram_ref[...] = jnp.concatenate([sums] * (gram_ref.shape[0] // 8), axis=0)


def surface_fields(low, high, rows_e, rows_w, cols_n, cols_s, count):
    corners = A_CORNERS if count == 3 else T_CORNERS
    first = 2 * corners

    def column(cols):
        own = cols.shape[0] - 2 * corners
        return [cols[0], cols[1], cols[own], cols[own + corners]]

    return [
        wide_surface(
            n, jnp.concatenate([low[first + n], high[first + n]], axis=0),
            rows_e[first + n], rows_w[first + n], column(cols_n), column(cols_s),
        )
        for n in range(count)
    ]


def first_surface_kernel(low, high, rows_e, rows_w, cols_n, cols_s, basis, gram, fixed):
    c, depth, diag = surface_fields(low, high, rows_e, rows_w, cols_n, cols_s, 3)
    fixed[0] = depth
    fixed[1] = diag
    krylov(c, diag, depth, basis, gram)


def next_surface_kernel(low, high, rows_e, rows_w, cols_n, cols_s, fixed, basis, gram):
    (c,) = surface_fields(low, high, rows_e, rows_w, cols_n, cols_s, 1)
    krylov(c, fixed[1], fixed[0], basis, gram)


def coefficients(gathered):
    parts = [(gathered[8 * n : 8 * n + 8], None) for n in range(gathered.shape[0] // 8)]
    parts = [(p, jnp.zeros_like(p)) for p, _ in parts]
    while len(parts) > 1:
        parts = [pair_add(a, b) for a, b in zip(parts[::2], parts[1::2])]
    total = parts[0]
    for shift in (4, 2, 1):
        total = pair_add(total, tuple(roll(x, shift, 0) for x in total))
    for shift in (4, 2, 1):
        total = pair_add(total, tuple(roll(x, COLS - shift, 1) for x in total))
    table = {}
    for n, (i, j) in enumerate(PAIRS):
        entry = tuple(jnp.broadcast_to(x[:, 8 * n : 8 * n + 1], (8, COLS)) for x in total)
        table[i, j] = table[j, i] = entry
    imaged = {(i, k): pair_add(table[i, k], table[i, k + 1]) for i in range(4) for k in range(i + 1)}
    one = (jnp.ones((8, COLS), F32), jnp.zeros((8, COLS), F32))
    r, p, x = [one], [one], []
    rr = table[0, 0][0]
    for it in range(4):
        den = pair_dot([imaged[it, k] for k in range(it + 1)], p)
        step = rr / (p[it][0] * den)
        x = [x[k] + step * p[k][0] if k < len(x) else step * p[k][0] for k in range(it + 1)]
        if it < 3:
            image = [p[0]] + [pair_add(p[k], p[k - 1]) for k in range(1, it + 1)] + [p[it]]
            moved = [pair_scale(a, -step) for a in image]
            r = [pair_add(r[k], moved[k]) if k < len(r) else moved[k] for k in range(it + 2)]
            new = r[it + 1][0] * pair_dot([table[it + 1, k] for k in range(it + 2)], r)
            ratio = new / rr
            p = [
                pair_add(r[k], pair_scale(p[k], ratio)) if k < len(p) else r[k]
                for k in range(it + 2)
            ]
            rr = new
    return x


class Halo:
    def __init__(self, refs, first, corners):
        self.low, self.high, self.own_s, self.own_n, self.e, self.w, self.n, self.s = refs
        self.first, self.corners = first, corners
        self.even_row = iota((8, COLS), 0) % 2 == 0
        self.even_lane = iota((8, COLS), 1) % 2 == 0
        self.sub = iota((8, COLS), 0)

    def rows(self, field, group):
        at = self.first + field * GROUPS + group
        e, w = self.e[at], self.w[at]
        return (
            jnp.where(self.even_row, roll(self.high[at], -1, 0), roll(self.low[at], 1, 0)),
            jnp.where(self.even_row, e, w),
            jnp.where(self.even_row, roll(e, -1, 0), roll(w, 1, 0)),
        )

    def edge_rows(self, field, group):
        at = self.first + field * GROUPS + group
        return jnp.where(self.even_row, self.e[at], self.w[at])

    def edge_columns(self, block):
        return jnp.concatenate(
            [
                jnp.where(self.even_lane, self.n[2 * block + h], self.s[2 * block + h])
                for h in range(2)
            ],
            axis=0,
        )

    def columns(self, block):
        inner, outer = [], []
        for h in range(2):
            at = 2 * block + h
            inner.append(
                jnp.where(self.even_lane, roll(self.own_n[at], -1, 1), roll(self.own_s[at], 1, 1))
            )
            outer.append(jnp.where(self.even_lane, roll(self.n[at], -1, 1), roll(self.s[at], 1, 1)))
        east = self.n.shape[0] - 2 * self.corners + block
        west = east + self.corners
        corner = jnp.where(
            self.sub < 4,
            jnp.where(self.even_lane, self.n[east], self.s[east]),
            jnp.where(self.even_lane, self.n[west], self.s[west]),
        )
        return (
            jnp.concatenate(inner, axis=0),
            jnp.concatenate([self.edge_columns(block), corner], axis=0),
            jnp.concatenate(outer, axis=0),
        )


def ends(v):
    return pltpu.roll(v, v.shape[0] - 1, 0), pltpu.roll(v, 1, 0)


def step_kernel(
    final,
    temp, salt, temp_response, salt_response, east, north, mask, bottom,
    diag, basis, gathered,
    *refs,
):
    if not final:
        (mix, thermal, haline), refs = refs[:3], refs[3:]
    a_halo = Halo(refs[:8], A_ROWS, A_CORNERS)
    if final:
        t_halo = Halo(refs[8:16], T_ROWS, T_CORNERS)
        new_temp, new_salt, new_surface = refs[16:]
    else:
        t_halo = a_halo
        inverses, ratios, new_temp, new_salt, row_low, row_high, col_low, col_high = refs[8:]
    tracers = ((temp, temp_response, 0, 3, 1.0), (salt, salt_response, 1, 4, -1.0))

    weights = coefficients(gathered[...])
    weights = [jnp.concatenate([jnp.concatenate([w] * 4, axis=0)] * 2, axis=1) for w in weights]
    full = sum(weights[k] * basis[k] for k in range(4))
    multiplier = full[:ROWS, :COLS]
    surface = diag[...] * multiplier
    if final:
        new_surface[...] = surface

    sub = iota((8, COLS), 0)
    even_row = sub % 2 == 0
    ring = jnp.concatenate([full[:ROWS], jnp.where(
        iota((8, 2 * COLS), 0) < 4, full[16:24], full[24:])], axis=0)
    even_lane = iota((24, COLS), 1) % 2 == 0

    def lanes(a, b):
        return jnp.where(
            even_lane,
            jnp.broadcast_to(ring[:, a : a + 1], (24, COLS)),
            jnp.broadcast_to(ring[:, b : b + 1], (24, COLS)),
        )

    def both_rows(a, b):
        return jnp.where(
            even_row,
            jnp.broadcast_to(full[a : a + 1, :COLS], (8, COLS)),
            jnp.broadcast_to(full[b : b + 1, :COLS], (8, COLS)),
        )

    column_m = [lanes(127, 0)[:ROWS], lanes(128, 255), lanes(129, 254)[:ROWS]]
    row_m = [both_rows(15, 0), both_rows(16, 31), both_rows(17, 30)]

    own = slice(0, ROWS)
    lane_sign = jnp.where(even_lane[own], 0.05, -0.05)
    wet0, wet1, wet2 = a_halo.columns(3)
    north1 = lane_sign * a_halo.edge_columns(6)
    e, w = ends(wet1)
    around1 = wet1[own] * ((e + w)[own] + (wet0 + wet2))
    column_wet = wet1
    column_q, column_out = [], []
    for _, _, field, response, sign in tracers:
        g = [
            b + (sign * m) * a
            for b, m, a in zip(t_halo.columns(field + 1), column_m, a_halo.columns(response + 1))
        ]
        q = wet1 * g[1]
        e, w = ends(q)
        near = (e + w)[own] + (wet0 * g[0] + wet2 * g[2])
        lap = wet1[own] * near - around1 * g[1][own]
        column_q.append(q)
        column_out.append(north1 * q[own] - 0.01 * lap)

    def corner_rows(v):
        return jnp.where(
            even_row,
            jnp.broadcast_to(v[16:17], (8, COLS)),
            jnp.broadcast_to(v[23:24], (8, COLS)),
        )

    corner_wet = corner_rows(column_wet)
    corner_q = [corner_rows(q) for q in column_q]
    column_wet = column_wet[own]
    column_q = [q[own] for q in column_q]

    lane8 = iota((8, COLS), 1)
    lane = iota((ROWS, COLS), 1)
    row = iota((ROWS, COLS), 0)
    row_sign = jnp.where(even_row, 0.05, -0.05)
    last = bottom[...]

    def beside(v, corner):
        return jnp.where(lane8 == COLS - 1, corner, pltpu.roll(v, COLS - 1, 1)) + jnp.where(
            lane8 == 0, corner, pltpu.roll(v, 1, 1)
        )

    def strips(group):
        shifts = [(127 - 2 * (group * 4 + j)) & 127 for j in range(4)]

        def corners(v):
            out = pltpu.roll(v, shifts[0], 1)
            for j in range(1, 4):
                out = jnp.where(sub // 2 == j, pltpu.roll(v, shifts[j], 1), out)
            return out

        wet0, wet1, wet2 = a_halo.rows(2, group)
        east1 = row_sign * a_halo.edge_rows(5, group)
        around1 = wet1 * ((wet0 + wet2) + beside(wet1, corners(corner_wet)))
        qs, outs = [], []
        for n, (_, _, field, response, sign) in enumerate(tracers):
            g = [
                b + (sign * m) * a
                for b, m, a in zip(
                    t_halo.rows(field, group), row_m, a_halo.rows(response, group)
                )
            ]
            q = wet1 * g[1]
            near = (wet0 * g[0] + wet2 * g[2]) + beside(q, corners(corner_q[n]))
            lap = wet1 * near - around1 * g[1]
            qs.append(q)
            outs.append(east1 * q - 0.01 * lap)
        return wet1, qs, outs

    def body(group, carry):
        row_wet, row_q, row_out = strips(group)
        for j in range(4):
            level = group * 4 + j
            shift = (127 - 2 * level) & 127

            def four(ve, vw, vn, vs, row_strip, column_strip):
                r = roll(row_strip, 7 - 2 * j, 0)
                r = jnp.concatenate([r, r], axis=0)
                c = pltpu.roll(column_strip, shift, 1)
                return (
                    jnp.where(row == ROWS - 1, r, pltpu.roll(ve, ROWS - 1, 0)),
                    jnp.where(row == 0, r, pltpu.roll(vw, 1, 0)),
                    jnp.where(lane == COLS - 1, c, pltpu.roll(vn, COLS - 1, 1)),
                    jnp.where(lane == 0, c, pltpu.roll(vs, 1, 1)),
                )

            wet = wet_at(mask, last, level)
            fe, fn = east[level], north[level]
            we, ww, wn, ws = four(wet, wet, wet, wet, row_wet, column_wet)
            around = wet * ((we + ww) + (wn + ws))
            diagonal = around + wet * (fe * (ww - we) + fn * (ws - wn))
            done = []
            for n, (field, response, _, _, sign) in enumerate(tracers):
                g = field[level] + (sign * multiplier) * response[level]
                q = wet * g
                e, w, no, so = four(q, q, q, q, row_q[n], column_q[n])
                near = wet * ((e + w) + (no + so))
                small = 0.01 * (near - around * g)
                u, v = (0.05 * fe) * q, (0.05 * fn) * q
                e, w, no, so = four(
                    u - small, -u - small, v - small, -v - small, row_out[n], column_out[n]
                )
                done.append(
                    (g + 0.05 * (near - diagonal * g))
                    + (wet * ((e + w) + (no + so)) + around * small)
                )
            t, s = done
            if final:
                new_temp[level] = t
                new_salt[level] = s
            else:
                above, total, pt, ps = carry
                total = total + wet * (thermal[level] * t - haline[level] * s)
                up = mix[jnp.maximum(level - 1, 0)] * (above * wet)
                inverse = inverses[level]
                pt = (t + up * pt) * inverse
                ps = (s + up * ps) * inverse
                new_temp[level] = pt
                new_salt[level] = ps
                carry = (wet, total, pt, ps)
        return carry

    zero = jnp.zeros((ROWS, COLS), F32)
    if final:
        lax.fori_loop(0, GROUPS, body, 0)
    else:
        _, total, _, _ = lax.fori_loop(0, GROUPS, body, (zero,) * 4)
        messages = row_low, row_high, col_low, col_high
        put_surface(messages, T_SURFACE, (surface + total,))
        back_substitute(messages, T_ROWS, (new_temp, new_salt), ratios, ((0, 1), (1, 2)))


def shape(*dims):
    return jax.ShapeDtypeStruct(dims, F32)


VMEM = pl.BlockSpec(memory_space=pltpu.VMEM)
HBM = pl.BlockSpec(memory_space=pltpu.HBM)
SMEM = pl.BlockSpec(memory_space=pltpu.SMEM)


def head(*block):
    return pl.BlockSpec(block, lambda i: (0,) * len(block), memory_space=pltpu.VMEM)


def call(kernel, outs, in_specs, out_specs=None, scratch=(), name=None, grid=None, room=40):
    extra = {} if grid is None else {"grid": grid}
    return pl.pallas_call(
        kernel,
        out_shape=outs,
        in_specs=in_specs,
        out_specs=[VMEM] * len(outs) if out_specs is None else out_specs,
        scratch_shapes=scratch,
        compiler_params=pltpu.CompilerParams(vmem_limit_bytes=room * 1024 * 1000),
        name=name,
        **extra,
    )


def message_shapes(surfaces, row_fields, col_fields, corner_fields):
    rows = shape(2 * (1 + corner_fields) + surfaces + GROUPS * row_fields, 8, COLS)
    cols = shape(2 * (1 + col_fields), 8, COLS)
    return [rows, rows, cols, cols]


def solution(mesh):
    nx, ny = mesh.shape["gx"], mesh.shape["gy"]
    devices = nx * ny
    both = ("gx", "gy")
    eastward = [(i, (i + 1) % nx) for i in range(nx)]
    northward = [(j, (j + 1) % ny) for j in range(ny)]

    def back(pairs):
        return [(b, a) for a, b in pairs]

    def exchange(messages, corners):
        row_low, row_high, col_low, col_high = messages
        rows_e = lax.ppermute(row_low, "gx", back(eastward))
        rows_w = lax.ppermute(row_high, "gx", eastward)
        own = col_low.shape[0]
        out = shape(own + 2 * corners, 8, COLS)
        to_south, to_north = call(
            forward_kernel, [out, out],
            [head(own, 8, COLS)] * 2 + [head(2 * corners, 8, COLS)] * 2,
            [head(*out.shape)] * 2, name="corners", grid=(1,),
        )(col_low, col_high, rows_e, rows_w)
        cols_n = lax.ppermute(to_south, "gy", back(northward))
        cols_s = lax.ppermute(to_north, "gy", northward)
        return [rows_e, rows_w, cols_n, cols_s]

    def all_sum(block):
        return lax.all_to_all(block, both, 0, 0, tiled=True)

    def surface_specs(rows, cols):
        return [head(rows, 8, COLS)] * 4 + [head(cols, 8, COLS)] * 2

    basis_shape = shape(4, 32, 2 * COLS)
    gram_shape = shape(devices, COLS)
    field = shape(LEVELS, ROWS, COLS)
    tile = shape(ROWS, COLS)

    def whole(*dims):
        return head(*dims)

    def per_device(
        sens_temp, sens_salt, sens_surface, flow_east, flow_north, mix_profile,
        thermal_weight, haline_weight, surface_diag, land_mask, bottom_level,
    ):
        *first, temp, salt, temp_response, salt_response, inverses, ratios, east, north, mask = call(
            prepare_kernel,
            message_shapes(3, 6, 6, 5)
            + [field] * 8
            + [jax.ShapeDtypeStruct((LEVELS, ROWS, COLS), jnp.int32)],
            [SMEM] * 3 + [HBM] * 5 + [VMEM] * 3,
            scratch=[pltpu.VMEM((LEVELS, ROWS, COLS), F32)] * 2
            + [pltpu.SemaphoreType.DMA((5, LEVELS // CHUNK))],
            name="prepare",
        )(
            *(
                pltpu.with_memory_space_constraint(x, pltpu.HBM)
                for x in (
                    mix_profile, thermal_weight, haline_weight, sens_temp, sens_salt, flow_east,
                    flow_north, land_mask, bottom_level, sens_surface, surface_diag,
                )
            )
        )
        got = exchange(first, A_CORNERS)
        basis, gram, fixed = call(
            first_surface_kernel,
            [basis_shape, gram_shape, shape(2, 32, 2 * COLS)],
            surface_specs(A_ROWS, 2 * 7 + 2 * A_CORNERS),
            [head(4, 32, 2 * COLS), head(devices, COLS), head(2, 32, 2 * COLS)],
            name="first_surface",
            grid=(1,),
        )(first[0], first[1], *got)
        gathered = all_sum(gram)

        def step(final, temp, salt, basis, gathered, more, outs):
            weights = [] if final else [mix_profile, thermal_weight, haline_weight]
            return call(
                functools.partial(step_kernel, final),
                outs,
                [VMEM] * 11 + [SMEM] * len(weights) + [VMEM] * (8 + len(more)),
                name="last_step" if final else "first_step",
            )(
                temp, salt, temp_response, salt_response, east, north, mask, bottom_level,
                surface_diag, basis, gathered, *weights, *first, *got, *more,
            )

        temp, salt, *second = step(
            False, temp, salt, basis, gathered, [inverses, ratios],
            [field, field] + message_shapes(1, 2, 2, 2),
        )
        more = exchange(second, T_CORNERS)
        basis, gram = call(
            next_surface_kernel,
            [basis_shape, gram_shape],
            surface_specs(T_ROWS, 2 * 3 + 2 * T_CORNERS) + [head(2, 32, 2 * COLS)],
            [head(4, 32, 2 * COLS), head(devices, COLS)],
            name="next_surface",
            grid=(1,),
        )(second[0], second[1], *more, fixed)
        gathered = all_sum(gram)
        return tuple(
            step(True, temp, salt, basis, gathered, [*second, *more], [field, field, tile])
        )

    in_specs = (
        P(None, "gx", "gy"),
        P(None, "gx", "gy"),
        P("gx", "gy"),
        P(None, "gx", "gy"),
        P(None, "gx", "gy"),
        P(),
        P(),
        P(),
        P("gx", "gy"),
        P(None, "gx", "gy"),
        P("gx", "gy"),
    )
    out_specs = (P(None, "gx", "gy"), P(None, "gx", "gy"), P("gx", "gy"))
    return jax.shard_map(
        per_device, mesh=mesh, in_specs=in_specs, out_specs=out_specs, check_vma=False
    )
```

```python
import functools

import jax
import jax.numpy as jnp
from jax import lax
from jax.experimental import pallas as pl
from jax.experimental.pallas import tpu as pltpu
from jax.sharding import PartitionSpec as P

LEVELS = 48
ROWS = 16
COLS = 128
GROUPS = LEVELS // 4
CHUNK = 12
F32 = jnp.float32
PAIRS = [(i, j) for i in range(4) for j in range(i, 5)]


def two_sum(a, b):
    s = a + b
    t = s - a
    return s, (a - (s - t)) + (b - t)


def fast_two_sum(a, b):
    s = a + b
    return s, b - (s - a)


def split(a):
    c = a * 4097.0
    high = c - (c - a)
    return high, a - high


def two_prod(a, b, a_parts=None, b_parts=None):
    ah, al = split(a) if a_parts is None else a_parts
    bh, bl = split(b) if b_parts is None else b_parts
    p = a * b
    return p, ((ah * bh - p) + ah * bl + al * bh) + al * bl


def pair_add(x, y):
    s, t = two_sum(x[0], y[0])
    return fast_two_sum(s, t + (x[1] + y[1]))


def pair_scale(x, c):
    p, e = two_prod(x[0], c)
    return fast_two_sum(p, e + x[1] * c)


def pair_dot(xs, ys):
    terms, rest = [], []
    for x, y in zip(xs, ys):
        p, e = two_prod(x[0], y[0])
        terms.append(p)
        rest.append(e + (x[0] * y[1] + x[1] * y[0]))
    while len(terms) > 1:
        sums = [two_sum(a, b) for a, b in zip(terms[::2], terms[1::2])]
        rest += [e for _, e in sums]
        terms = [s for s, _ in sums] + terms[len(sums) * 2 :]
    while len(rest) > 1:
        rest = [a + b for a, b in zip(rest[::2], rest[1::2])] + rest[len(rest) // 2 * 2 :]
    return terms[0] + rest[0]


def roll(x, shift, axis):
    shift = shift % x.shape[axis]
    return x if shift == 0 else pltpu.roll(x, shift, axis)


def iota(shape, axis):
    return lax.broadcasted_iota(jnp.int32, shape, axis)


A_CORNERS, T_CORNERS = 6, 3
A_SURFACE, T_SURFACE = 2 * A_CORNERS, 2 * T_CORNERS
A_ROWS, T_ROWS = A_SURFACE + 3, T_SURFACE + 1


def put_rows(low_ref, high_ref, first, field, group, j, cells):
    at = first + field * GROUPS + group
    low_ref[at, 2 * j : 2 * j + 2, :] = cells[:2]
    high_ref[at, 2 * j : 2 * j + 2, :] = cells[ROWS - 2 :]


def packed(acc, cells, level):
    low, high = acc
    mine = lax.shift_right_logical(iota((ROWS, COLS), 1), 1) == level
    low = jnp.where(mine, pltpu.roll(cells, 2 * level, 1), low)
    high = jnp.where(mine, pltpu.roll(cells, 2 * level + 2, 1), high)
    return low, high


def put_surface(refs, first, fields):
    row_low, row_high, col_low, col_high = refs
    low = jnp.zeros((ROWS, COLS), F32)
    high = low
    lane_group = iota((ROWS, COLS), 1) // 8
    for n, cells in enumerate(fields):
        row_low[first + n] = cells[:8]
        row_high[first + n] = cells[8:]
        low = jnp.where(lane_group == n, roll(cells, 8 * n, 1), low)
        high = jnp.where(lane_group == n, roll(cells, 8 * n + 8, 1), high)
    put_cols(refs, 0, low, high)


def put_cols(refs, n, low, high):
    row_low, row_high, col_low, col_high = refs
    count = corners_of(row_low)
    for col, side, cells in ((col_low, 0, low), (col_high, count, high)):
        col[2 * n] = cells[:8]
        col[2 * n + 1] = cells[8:]
        if n < count:
            row_low[side + n] = cells[:8]
            row_high[side + n] = cells[8:]


def corners_of(rows):
    return A_CORNERS if rows.shape[0] == A_ROWS else T_CORNERS


def forward_kernel(own_low, own_high, rows_e, rows_w, to_south, to_north):
    count = rows_e.shape[0] // 2
    own = own_low.shape[0]
    place = lax.axis_index("gy")
    ends_at = 0, lax.axis_size("gy") - 1
    for out, mine, side, end in zip((to_south, to_north), (own_low, own_high), (0, count), ends_at):
        inner = place != end
        out[:own] = jnp.where(inner, mine[...], 0.0)
        out[own : own + count] = jnp.where(inner, rows_e[side : side + count], 0.0)
        out[own + count :] = jnp.where(inner, rows_w[side : side + count], 0.0)


def wet_at(mask, last, level):
    return jnp.where(last > level, mask[jnp.minimum(level, LEVELS - 1)], 0).astype(F32)


def prepare_kernel(
    mix, thermal, haline, temp_in, salt_in, east_in, north_in, mask_in, bottom, surface, diag,
    row_low, row_high, col_low, col_high, strip_low, strip_high, *rest,
):
    solved, rest = rest[:4], rest[4:]
    inverses, ratios, east, north, wets, kept, temp, salt, mask, sems = rest
    last = bottom[...]
    zero = jnp.zeros((ROWS, COLS), F32)
    pair = (zero, zero)
    fields = list(
        zip((mask_in, temp_in, salt_in, east_in, north_in), (mask, temp, salt, east, north))
    )

    def copy(n, part):
        source, target = fields[n]
        levels = pl.ds(part * CHUNK, CHUNK)
        return pltpu.make_async_copy(source.at[levels], target.at[levels], sems.at[n, part])

    parts = LEVELS // CHUNK
    for part in range(parts):
        copy(0, part).start()
    for part in range(parts):
        for n in range(1, 5):
            copy(n, part).start()

    def down_body(group, carry):
        total, depth, up, ratio, values, wet, packs = carry
        for j in range(4):
            level = group * 4 + j
            below = wet_at(mask, last, level + 1)
            down = mix[level] * (wet * below)
            inverse = 1.0 / ((1.0 + up + down) - up * ratio)
            t, s = temp[level], salt[level]
            tw, hw = thermal[level] * wet, haline[level] * wet
            total = total + (tw * t - hw * s)
            depth = depth + wet
            wets[level] = wet
            for n, weight in enumerate((mix, thermal, haline)):
                kept[n, level] = jnp.full((8, COLS), weight[level], F32)
            values = tuple((r + up * v) * inverse for r, v in zip((t, s, tw, hw), values))
            for ref, v in zip(solved, values):
                ref[level] = v
            ratio = down * inverse
            inverses[level] = inverse
            ratios[level] = ratio
            put_rows(strip_low, strip_high, 0, 2, group, j, wet)
            put_rows(strip_low, strip_high, 0, 5, group, j, east[level])
            packs = tuple(packed(acc, v, level) for acc, v in zip(packs, (wet, north[level])))
            up = down
            wet = below
        return total, depth, up, ratio, values, wet, packs

    for part in range(parts):
        copy(0, part).wait()
    carry = (zero, zero, zero, zero, (zero,) * 4, wet_at(mask, last, 0), (pair, pair))
    step = CHUNK // 4
    for part in range(parts):
        for n in range(1, 5):
            copy(n, part).wait()
        carry = lax.fori_loop(part * step, (part + 1) * step, down_body, carry)
    total, depth, _, _, _, _, packs = carry
    refs = row_low, row_high, col_low, col_high
    put_surface(refs, A_SURFACE, (surface[...] + total, depth / LEVELS, diag[...]))
    put_cols(refs, 3, *packs[0])
    put_cols(refs, 6, *packs[1])
    strips = strip_low, strip_high
    back_substitute(refs, strips, 0, solved, ratios, ((0, 1), (1, 2), (3, 4), (4, 5)))


def back_substitute(refs, strips, first, solved, ratios, places):
    zero = jnp.zeros((ROWS, COLS), F32)

    def up_body(count, carry):
        values, packs = carry
        group = GROUPS - 1 - count
        for j in (3, 2, 1, 0):
            level = group * 4 + j
            ratio = ratios[level]
            values = tuple(ref[level] + ratio * v for ref, v in zip(solved, values))
            for ref, v, (field, _) in zip(solved, values, places):
                ref[level] = v
                put_rows(*strips, first, field, group, j, v)
            packs = tuple(packed(acc, v, level) for acc, v in zip(packs, values))
        return values, packs

    n = len(places)
    _, packs = lax.fori_loop(0, GROUPS, up_body, ((zero,) * n, ((zero, zero),) * n))
    for (_, block), acc in zip(places, packs):
        put_cols(refs, block, *acc)


def wide_surface(n, own, rows_e, rows_w, from_north, from_south):
    main = jnp.concatenate([own, rows_e, rows_w], axis=0)
    to_north = jnp.concatenate(from_north, axis=0)
    to_south = jnp.concatenate(from_south, axis=0)
    lane = iota((32, COLS), 1)
    side = jnp.where(
        lane < 8,
        roll(to_north, -8 * n, 1),
        jnp.where(lane >= COLS - 8, roll(to_south, 120 - 8 * n, 1), 0.0),
    )
    return jnp.concatenate([main, side], axis=1)


def krylov(c, diag, depth, basis_ref, gram_ref):
    def nb(v):
        return pltpu.roll(v, 31, 0), pltpu.roll(v, 1, 0), pltpu.roll(v, 255, 1), pltpu.roll(v, 1, 1)

    faces = [jnp.minimum(depth, d) for d in nb(depth)]
    centre = (diag - 1.0) + ((faces[0] + faces[1]) + (faces[2] + faces[3]))
    v = c
    own = []
    for k in range(5):
        if k < 4:
            basis_ref[k] = v
        mine = v[:ROWS, :COLS]
        own.append((mine, split(mine)))
        if k < 4:
            e, w, n, s = nb(v)
            v = centre * v - ((faces[0] * e + faces[1] * w) + (faces[2] * n + faces[3] * s))
    highs, lows = [], []
    for i, j in PAIRS:
        p, e = two_prod(own[i][0], own[j][0], own[i][1], own[j][1])
        s, t = two_sum(p[:8], p[8:])
        highs.append(s)
        lows.append(t + (e[:8] + e[8:]))
    pad = [jnp.zeros((8, COLS), F32)] * (16 - len(PAIRS))
    high = jnp.concatenate(highs + pad, axis=0).T
    low = jnp.concatenate(lows + pad, axis=0).T
    parts = [(high[8 * n : 8 * n + 8], low[8 * n : 8 * n + 8]) for n in range(16)]
    while len(parts) > 1:
        parts = [pair_add(a, b) for a, b in zip(parts[::2], parts[1::2])]
    total = parts[0]
    for shift in (4, 2, 1):
        total = pair_add(total, tuple(roll(x, shift, 0) for x in total))
    total = pair_add(total, tuple(roll(x, 124, 1) for x in total))
    first_half = (iota((8, COLS), 1) % 8) < 4
    sums = jnp.where(first_half, total[0], roll(total[1], 4, 1))
    gram_ref[...] = jnp.concatenate([sums] * (gram_ref.shape[0] // 8), axis=0)


def surface_fields(low, high, rows_e, rows_w, cols_n, cols_s, count):
    corners = A_CORNERS if count == 3 else T_CORNERS
    first = 2 * corners

    def column(cols):
        own = cols.shape[0] - 2 * corners
        return [cols[0], cols[1], cols[own], cols[own + corners]]

    return [
        wide_surface(
            n, jnp.concatenate([low[first + n], high[first + n]], axis=0),
            rows_e[first + n], rows_w[first + n], column(cols_n), column(cols_s),
        )
        for n in range(count)
    ]


def first_surface_kernel(low, high, rows_e, rows_w, cols_n, cols_s, basis, gram, fixed):
    c, depth, diag = surface_fields(low, high, rows_e, rows_w, cols_n, cols_s, 3)
    fixed[0] = depth
    fixed[1] = diag
    krylov(c, diag, depth, basis, gram)


def next_surface_kernel(low, high, rows_e, rows_w, cols_n, cols_s, fixed, basis, gram):
    (c,) = surface_fields(low, high, rows_e, rows_w, cols_n, cols_s, 1)
    krylov(c, fixed[1], fixed[0], basis, gram)


def coefficients(gathered):
    parts = [(gathered[8 * n : 8 * n + 8], None) for n in range(gathered.shape[0] // 8)]
    parts = [(p, jnp.zeros_like(p)) for p, _ in parts]
    while len(parts) > 1:
        parts = [pair_add(a, b) for a, b in zip(parts[::2], parts[1::2])]
    total = parts[0]
    for shift in (4, 2, 1):
        total = pair_add(total, tuple(roll(x, shift, 0) for x in total))
    for shift in (4, 2, 1):
        total = pair_add(total, tuple(roll(x, COLS - shift, 1) for x in total))
    table = {}
    for n, (i, j) in enumerate(PAIRS):
        entry = tuple(jnp.broadcast_to(x[:, 8 * n : 8 * n + 1], (8, COLS)) for x in total)
        table[i, j] = table[j, i] = entry
    imaged = {(i, k): pair_add(table[i, k], table[i, k + 1]) for i in range(4) for k in range(i + 1)}
    one = (jnp.ones((8, COLS), F32), jnp.zeros((8, COLS), F32))
    r, p, x = [one], [one], []
    rr = table[0, 0][0]
    for it in range(4):
        den = pair_dot([imaged[it, k] for k in range(it + 1)], p)
        step = rr / (p[it][0] * den)
        x = [x[k] + step * p[k][0] if k < len(x) else step * p[k][0] for k in range(it + 1)]
        if it < 3:
            image = [p[0]] + [pair_add(p[k], p[k - 1]) for k in range(1, it + 1)] + [p[it]]
            moved = [pair_scale(a, -step) for a in image]
            r = [pair_add(r[k], moved[k]) if k < len(r) else moved[k] for k in range(it + 2)]
            new = r[it + 1][0] * pair_dot([table[it + 1, k] for k in range(it + 2)], r)
            ratio = new / rr
            p = [
                pair_add(r[k], pair_scale(p[k], ratio)) if k < len(p) else r[k]
                for k in range(it + 2)
            ]
            rr = new
    return x


class Halo:
    def __init__(self, refs, first, corners):
        self.low, self.high, self.own_s, self.own_n, self.e, self.w, self.n, self.s = refs
        self.first, self.corners = first, corners
        self.even_row = iota((8, COLS), 0) % 2 == 0
        self.even_lane = iota((8, COLS), 1) % 2 == 0
        self.sub = iota((8, COLS), 0)

    def rows(self, field, group):
        at = self.first + field * GROUPS + group
        e, w = self.e[at], self.w[at]
        return (
            jnp.where(self.even_row, roll(self.high[at], -1, 0), roll(self.low[at], 1, 0)),
            jnp.where(self.even_row, e, w),
            jnp.where(self.even_row, roll(e, -1, 0), roll(w, 1, 0)),
        )

    def edge_rows(self, field, group):
        at = self.first + field * GROUPS + group
        return jnp.where(self.even_row, self.e[at], self.w[at])

    def edge_columns(self, block):
        return jnp.concatenate(
            [
                jnp.where(self.even_lane, self.n[2 * block + h], self.s[2 * block + h])
                for h in range(2)
            ],
            axis=0,
        )

    def columns(self, block):
        inner, outer = [], []
        for h in range(2):
            at = 2 * block + h
            inner.append(
                jnp.where(self.even_lane, roll(self.own_n[at], -1, 1), roll(self.own_s[at], 1, 1))
            )
            outer.append(jnp.where(self.even_lane, roll(self.n[at], -1, 1), roll(self.s[at], 1, 1)))
        east = self.n.shape[0] - 2 * self.corners + block
        west = east + self.corners
        corner = jnp.where(
            self.sub < 4,
            jnp.where(self.even_lane, self.n[east], self.s[east]),
            jnp.where(self.even_lane, self.n[west], self.s[west]),
        )
        return (
            jnp.concatenate(inner, axis=0),
            jnp.concatenate([self.edge_columns(block), corner], axis=0),
            jnp.concatenate(outer, axis=0),
        )


def ends(v):
    return pltpu.roll(v, v.shape[0] - 1, 0), pltpu.roll(v, 1, 0)


def step_kernel(
    final,
    temp, salt, temp_response, salt_response, east, north, wets, fixed, basis, gathered,
    *refs,
):
    if not final:
        kept, refs = refs[0], refs[1:]

        def weight(n, level):
            value = kept[n, level]
            return jnp.concatenate([value, value], axis=0)

    a_halo = Halo(refs[:8], 0, A_CORNERS)
    if final:
        t_halo = Halo(refs[8:16], T_ROWS, T_CORNERS)
        new_temp, new_salt, new_surface = refs[16:]
    else:
        t_halo = a_halo
        inverses, ratios, new_temp, new_salt, *messages = refs[8:]
    tracers = ((temp, temp_response, 0, 3, 1.0), (salt, salt_response, 1, 4, -1.0))

    weights = coefficients(gathered[...])
    weights = [jnp.concatenate([jnp.concatenate([w] * 4, axis=0)] * 2, axis=1) for w in weights]
    full = sum(weights[k] * basis[k] for k in range(4))
    multiplier = full[:ROWS, :COLS]
    surface = fixed[1, :ROWS, :COLS] * multiplier
    if final:
        new_surface[...] = surface

    sub = iota((8, COLS), 0)
    even_row = sub % 2 == 0
    ring = jnp.concatenate([full[:ROWS], jnp.where(
        iota((8, 2 * COLS), 0) < 4, full[16:24], full[24:])], axis=0)
    even_lane = iota((24, COLS), 1) % 2 == 0

    def lanes(a, b):
        return jnp.where(
            even_lane,
            jnp.broadcast_to(ring[:, a : a + 1], (24, COLS)),
            jnp.broadcast_to(ring[:, b : b + 1], (24, COLS)),
        )

    def both_rows(a, b):
        return jnp.where(
            even_row,
            jnp.broadcast_to(full[a : a + 1, :COLS], (8, COLS)),
            jnp.broadcast_to(full[b : b + 1, :COLS], (8, COLS)),
        )

    column_m = [lanes(127, 0)[:ROWS], lanes(128, 255), lanes(129, 254)[:ROWS]]
    row_m = [both_rows(15, 0), both_rows(16, 31), both_rows(17, 30)]

    own = slice(0, ROWS)
    lane_sign = jnp.where(even_lane[own], 0.05, -0.05)
    wet0, wet1, wet2 = a_halo.columns(3)
    north1 = lane_sign * a_halo.edge_columns(6)
    e, w = ends(wet1)
    around1 = wet1[own] * ((e + w)[own] + (wet0 + wet2))
    column_wet = wet1
    column_q, column_out = [], []
    for _, _, field, response, sign in tracers:
        g = [
            b + (sign * m) * a
            for b, m, a in zip(t_halo.columns(field + 1), column_m, a_halo.columns(response + 1))
        ]
        q = wet1 * g[1]
        e, w = ends(q)
        near = (e + w)[own] + (wet0 * g[0] + wet2 * g[2])
        lap = wet1[own] * near - around1 * g[1][own]
        column_q.append(q)
        column_out.append(north1 * q[own] - 0.01 * lap)

    def corner_rows(v):
        return jnp.where(
            even_row,
            jnp.broadcast_to(v[16:17], (8, COLS)),
            jnp.broadcast_to(v[23:24], (8, COLS)),
        )

    corner_wet = corner_rows(column_wet)
    corner_q = [corner_rows(q) for q in column_q]
    column_wet = column_wet[own]
    column_q = [q[own] for q in column_q]

    lane8 = iota((8, COLS), 1)
    lane = iota((ROWS, COLS), 1)
    row = iota((ROWS, COLS), 0)
    row_sign = jnp.where(even_row, 0.05, -0.05)

    def beside(v, corner):
        return jnp.where(lane8 == COLS - 1, corner, pltpu.roll(v, COLS - 1, 1)) + jnp.where(
            lane8 == 0, corner, pltpu.roll(v, 1, 1)
        )

    def strips(group):
        shifts = [(127 - 2 * (group * 4 + j)) & 127 for j in range(4)]

        def corners(v):
            out = pltpu.roll(v, shifts[0], 1)
            for j in range(1, 4):
                out = jnp.where(sub // 2 == j, pltpu.roll(v, shifts[j], 1), out)
            return out

        wet0, wet1, wet2 = a_halo.rows(2, group)
        east1 = row_sign * a_halo.edge_rows(5, group)
        around1 = wet1 * ((wet0 + wet2) + beside(wet1, corners(corner_wet)))
        qs, outs = [], []
        for n, (_, _, field, response, sign) in enumerate(tracers):
            g = [
                b + (sign * m) * a
                for b, m, a in zip(
                    t_halo.rows(field, group), row_m, a_halo.rows(response, group)
                )
            ]
            q = wet1 * g[1]
            near = (wet0 * g[0] + wet2 * g[2]) + beside(q, corners(corner_q[n]))
            lap = wet1 * near - around1 * g[1]
            qs.append(q)
            outs.append(east1 * q - 0.01 * lap)
        return wet1, qs, outs

    def body(group, carry):
        row_wet, row_q, row_out = strips(group)
        for j in range(4):
            level = group * 4 + j
            shift = (127 - 2 * level) & 127

            def four(ve, vw, vn, vs, row_strip, column_strip):
                r = roll(row_strip, 7 - 2 * j, 0)
                r = jnp.concatenate([r, r], axis=0)
                c = pltpu.roll(column_strip, shift, 1)
                return (
                    jnp.where(row == ROWS - 1, r, pltpu.roll(ve, ROWS - 1, 0)),
                    jnp.where(row == 0, r, pltpu.roll(vw, 1, 0)),
                    jnp.where(lane == COLS - 1, c, pltpu.roll(vn, COLS - 1, 1)),
                    jnp.where(lane == 0, c, pltpu.roll(vs, 1, 1)),
                )

            wet = wets[level]
            fe, fn = east[level], north[level]
            we, ww, wn, ws = four(wet, wet, wet, wet, row_wet, column_wet)
            around = wet * ((we + ww) + (wn + ws))
            diagonal = around + wet * (fe * (ww - we) + fn * (ws - wn))
            done = []
            for n, (field, response, _, _, sign) in enumerate(tracers):
                g = field[level] + (sign * multiplier) * response[level]
                q = wet * g
                e, w, no, so = four(q, q, q, q, row_q[n], column_q[n])
                near = wet * ((e + w) + (no + so))
                small = 0.01 * (near - around * g)
                u, v = (0.05 * fe) * q, (0.05 * fn) * q
                e, w, no, so = four(
                    u - small, -u - small, v - small, -v - small, row_out[n], column_out[n]
                )
                done.append(
                    (g + 0.05 * (near - diagonal * g))
                    + (wet * ((e + w) + (no + so)) + around * small)
                )
            t, s = done
            if final:
                new_temp[level] = t
                new_salt[level] = s
            else:
                above, total, pt, ps = carry
                total = total + wet * (weight(1, level) * t - weight(2, level) * s)
                up = weight(0, jnp.maximum(level - 1, 0)) * (above * wet)
                inverse = inverses[level]
                pt = (t + up * pt) * inverse
                ps = (s + up * ps) * inverse
                new_temp[level] = pt
                new_salt[level] = ps
                carry = (wet, total, pt, ps)
        return carry

    zero = jnp.zeros((ROWS, COLS), F32)
    if final:
        lax.fori_loop(0, GROUPS, body, 0)
    else:
        _, total, _, _ = lax.fori_loop(0, GROUPS, body, (zero,) * 4)
        put_surface(messages, T_SURFACE, (surface + total,))
        back_substitute(
            messages, messages[:2], T_ROWS, (new_temp, new_salt), ratios, ((0, 1), (1, 2))
        )


def shape(*dims):
    return jax.ShapeDtypeStruct(dims, F32)


VMEM = pl.BlockSpec(memory_space=pltpu.VMEM)
HBM = pl.BlockSpec(memory_space=pltpu.HBM)
SMEM = pl.BlockSpec(memory_space=pltpu.SMEM)


def head(*block):
    return pl.BlockSpec(block, lambda i: (0,) * len(block), memory_space=pltpu.VMEM)


def call(kernel, outs, in_specs, out_specs=None, scratch=(), name=None, grid=None, room=40):
    extra = {} if grid is None else {"grid": grid}
    return pl.pallas_call(
        kernel,
        out_shape=outs,
        in_specs=in_specs,
        out_specs=[VMEM] * len(outs) if out_specs is None else out_specs,
        scratch_shapes=scratch,
        compiler_params=pltpu.CompilerParams(vmem_limit_bytes=room * 1024 * 1000),
        name=name,
        **extra,
    )


def message_shapes(surfaces, row_fields, col_fields, corner_fields):
    rows = shape(2 * (1 + corner_fields) + surfaces + GROUPS * row_fields, 8, COLS)
    cols = shape(2 * (1 + col_fields), 8, COLS)
    return [rows, rows, cols, cols]


def solution(mesh):
    nx, ny = mesh.shape["gx"], mesh.shape["gy"]
    devices = nx * ny
    both = ("gx", "gy")
    eastward = [(i, (i + 1) % nx) for i in range(nx)]
    northward = [(j, (j + 1) % ny) for j in range(ny)]

    def back(pairs):
        return [(b, a) for a, b in pairs]

    def exchange(messages, corners):
        row_low, row_high, col_low, col_high = messages
        rows_e = lax.ppermute(row_low, "gx", back(eastward))
        rows_w = lax.ppermute(row_high, "gx", eastward)
        own = col_low.shape[0]
        out = shape(own + 2 * corners, 8, COLS)
        to_south, to_north = call(
            forward_kernel, [out, out],
            [head(own, 8, COLS)] * 2 + [head(2 * corners, 8, COLS)] * 2,
            [head(*out.shape)] * 2, name="corners", grid=(1,),
        )(col_low, col_high, rows_e, rows_w)
        cols_n = lax.ppermute(to_south, "gy", back(northward))
        cols_s = lax.ppermute(to_north, "gy", northward)
        return [rows_e, rows_w, cols_n, cols_s]

    def exchange_strips(low, high, after):
        low, high, _ = lax.optimization_barrier((low, high, after))
        return [lax.ppermute(low, "gx", back(eastward)), lax.ppermute(high, "gx", eastward)]

    def all_sum(block):
        return lax.all_to_all(block, both, 0, 0, tiled=True)

    def surface_specs(rows, cols):
        return [head(rows, 8, COLS)] * 4 + [head(cols, 8, COLS)] * 2

    basis_shape = shape(4, 32, 2 * COLS)
    gram_shape = shape(devices, COLS)
    field = shape(LEVELS, ROWS, COLS)
    tile = shape(ROWS, COLS)

    def whole(*dims):
        return head(*dims)

    def per_device(
        sens_temp, sens_salt, sens_surface, flow_east, flow_north, mix_profile,
        thermal_weight, haline_weight, surface_diag, land_mask, bottom_level,
    ):
        *sent, strip_low, strip_high, temp, salt, temp_response, salt_response, inverses, ratios, east, north, wets, kept = call(
            prepare_kernel,
            message_shapes(3, 0, 6, 5)
            + [shape(6 * GROUPS, 8, COLS)] * 2
            + [field] * 9
            + [shape(3, LEVELS, 8, COLS)],
            [SMEM] * 3 + [HBM] * 5 + [VMEM] * 3,
            scratch=[pltpu.VMEM((LEVELS, ROWS, COLS), F32)] * 2
            + [pltpu.VMEM((LEVELS, ROWS, COLS), jnp.int32)]
            + [pltpu.SemaphoreType.DMA((5, LEVELS // CHUNK))],
            name="prepare",
        )(
            *(
                pltpu.with_memory_space_constraint(x, pltpu.HBM)
                for x in (
                    mix_profile, thermal_weight, haline_weight, sens_temp, sens_salt, flow_east,
                    flow_north, land_mask, bottom_level, sens_surface, surface_diag,
                )
            )
        )
        got = exchange(sent, A_CORNERS)
        strips = exchange_strips(strip_low, strip_high, got[2])
        halo = [strip_low, strip_high, *sent[2:], *strips, *got[2:]]
        basis, gram, fixed = call(
            first_surface_kernel,
            [basis_shape, gram_shape, shape(2, 32, 2 * COLS)],
            surface_specs(A_ROWS, 2 * 7 + 2 * A_CORNERS),
            [head(4, 32, 2 * COLS), head(devices, COLS), head(2, 32, 2 * COLS)],
            name="first_surface",
            grid=(1,),
        )(sent[0], sent[1], *got)
        gathered = all_sum(gram)

        def step(final, temp, salt, basis, gathered, more, outs):
            weights = [] if final else [kept]
            return call(
                functools.partial(step_kernel, final),
                outs,
                [VMEM] * (18 + len(weights) + len(more)),
                name="last_step" if final else "first_step",
            )(
                temp, salt, temp_response, salt_response, east, north, wets, fixed,
                basis, gathered, *weights, *halo, *more,
            )

        temp, salt, *second = step(
            False, temp, salt, basis, gathered, [inverses, ratios],
            [field, field] + message_shapes(1, 2, 2, 2),
        )
        more = exchange(second, T_CORNERS)
        basis, gram = call(
            next_surface_kernel,
            [basis_shape, gram_shape],
            surface_specs(T_ROWS, 2 * 3 + 2 * T_CORNERS) + [head(2, 32, 2 * COLS)],
            [head(4, 32, 2 * COLS), head(devices, COLS)],
            name="next_surface",
            grid=(1,),
        )(second[0], second[1], *more, fixed)
        gathered = all_sum(gram)
        return tuple(
            step(True, temp, salt, basis, gathered, [*second, *more], [field, field, tile])
        )

    in_specs = (
        P(None, "gx", "gy"),
        P(None, "gx", "gy"),
        P("gx", "gy"),
        P(None, "gx", "gy"),
        P(None, "gx", "gy"),
        P(),
        P(),
        P(),
        P("gx", "gy"),
        P(None, "gx", "gy"),
        P("gx", "gy"),
    )
    out_specs = (P(None, "gx", "gy"), P(None, "gx", "gy"), P("gx", "gy"))
    return jax.shard_map(
        per_device, mesh=mesh, in_specs=in_specs, out_specs=out_specs, check_vma=False
    )
```

```python
import functools

import jax
import jax.numpy as jnp
from jax import lax
from jax.experimental import pallas as pl
from jax.experimental.pallas import tpu as pltpu
from jax.sharding import PartitionSpec as P

LEVELS = 48
ROWS = 16
COLS = 128
GROUPS = LEVELS // 4
CHUNK = 12
F32 = jnp.float32
PAIRS = [(i, j) for i in range(4) for j in range(i, 5)]


def two_sum(a, b):
    s = a + b
    t = s - a
    return s, (a - (s - t)) + (b - t)


def fast_two_sum(a, b):
    s = a + b
    return s, b - (s - a)


def split(a):
    c = a * 4097.0
    high = c - (c - a)
    return high, a - high


def two_prod(a, b, a_parts=None, b_parts=None):
    ah, al = split(a) if a_parts is None else a_parts
    bh, bl = split(b) if b_parts is None else b_parts
    p = a * b
    return p, ((ah * bh - p) + ah * bl + al * bh) + al * bl


def pair_add(x, y):
    s, t = two_sum(x[0], y[0])
    return fast_two_sum(s, t + (x[1] + y[1]))


def pair_scale(x, c):
    p, e = two_prod(x[0], c)
    return fast_two_sum(p, e + x[1] * c)


def pair_dot(xs, ys):
    terms, rest = [], []
    for x, y in zip(xs, ys):
        p, e = two_prod(x[0], y[0])
        terms.append(p)
        rest.append(e + (x[0] * y[1] + x[1] * y[0]))
    while len(terms) > 1:
        sums = [two_sum(a, b) for a, b in zip(terms[::2], terms[1::2])]
        rest += [e for _, e in sums]
        terms = [s for s, _ in sums] + terms[len(sums) * 2 :]
    while len(rest) > 1:
        rest = [a + b for a, b in zip(rest[::2], rest[1::2])] + rest[len(rest) // 2 * 2 :]
    return terms[0] + rest[0]


def roll(x, shift, axis):
    shift = shift % x.shape[axis]
    return x if shift == 0 else pltpu.roll(x, shift, axis)


def iota(shape, axis):
    return lax.broadcasted_iota(jnp.int32, shape, axis)


A_CORNERS, T_CORNERS = 1, 3
A_SURFACE, T_SURFACE = 2 * A_CORNERS, 2 * T_CORNERS
A_ROWS, T_ROWS = A_SURFACE + 3, T_SURFACE + 1
STRIPS = 12


def put_rows(low_ref, high_ref, first, field, group, j, cells):
    at = first + field * GROUPS + group
    low_ref[at, 2 * j : 2 * j + 2, :] = cells[:2]
    high_ref[at, 2 * j : 2 * j + 2, :] = cells[ROWS - 2 :]


def packed(acc, cells, level):
    low, high = acc
    mine = lax.shift_right_logical(iota((ROWS, COLS), 1), 1) == level
    low = jnp.where(mine, pltpu.roll(cells, 2 * level, 1), low)
    high = jnp.where(mine, pltpu.roll(cells, 2 * level + 2, 1), high)
    return low, high


def put_surface(refs, first, fields):
    row_low, row_high, col_low, col_high = refs
    low = jnp.zeros((ROWS, COLS), F32)
    high = low
    lane_group = iota((ROWS, COLS), 1) // 8
    for n, cells in enumerate(fields):
        row_low[first + n] = cells[:8]
        row_high[first + n] = cells[8:]
        low = jnp.where(lane_group == n, roll(cells, 8 * n, 1), low)
        high = jnp.where(lane_group == n, roll(cells, 8 * n + 8, 1), high)
    put_cols(refs, 0, low, high)


def put_cols(refs, n, low, high):
    row_low, row_high, col_low, col_high = refs
    count = 0 if row_low is None else corners_of(row_low)
    for col, side, cells in ((col_low, 0, low), (col_high, count, high)):
        col[2 * n] = cells[:8]
        col[2 * n + 1] = cells[8:]
        if n < count:
            row_low[side + n] = cells[:8]
            row_high[side + n] = cells[8:]


def corners_of(rows):
    return A_CORNERS if rows.shape[0] == A_ROWS else T_CORNERS


def forward_kernel(own_low, own_high, rows_e, rows_w, *refs):
    count = rows_e.shape[0] // 2
    own = own_low.shape[0]
    more, outs = refs[:-2], refs[-2:]
    place = lax.axis_index("gy")
    ends_at = 0, lax.axis_size("gy") - 1
    for n, (out, mine, end) in enumerate(zip(outs, (own_low, own_high), ends_at)):
        inner = place != end
        side = n * count
        out[:own] = jnp.where(inner, mine[...], 0.0)
        out[own : own + count] = jnp.where(inner, rows_e[side : side + count], 0.0)
        out[own + count : own + 2 * count] = jnp.where(inner, rows_w[side : side + count], 0.0)
        if more:
            out[own + 2 * count :] = jnp.where(inner, more[n][...], 0.0)


def strip_corner_kernel(_low, _high, cols_n, cols_s, out_low, out_high):
    for side, cols in enumerate((cols_n, cols_s)):
        for n in range(5):
            out_low[5 * side + n] = cols[4 + 2 * n]
            out_high[5 * side + n] = cols[5 + 2 * n]
    for out in (out_low, out_high):
        out[10:] = jnp.zeros((STRIPS - 10, 8, COLS), F32)


def wet_at(mask, last, level):
    return jnp.where(last > level, mask[jnp.minimum(level, LEVELS - 1)], 0).astype(F32)


def combine_kernel(
    mix, thermal, haline, temp_in, salt_in, mask_in, bottom, surface, diag,
    row_low, row_high, col_low, col_high, temp, salt, wets, kept, mask, sems,
):
    last = bottom[...]
    zero = jnp.zeros((ROWS, COLS), F32)
    fields = (mask_in, mask), (temp_in, temp), (salt_in, salt)
    parts = LEVELS // CHUNK

    def copy(n, part):
        source, target = fields[n]
        levels = pl.ds(part * CHUNK, CHUNK)
        return pltpu.make_async_copy(source.at[levels], target.at[levels], sems.at[n, part])

    for part in range(parts):
        for n in range(3):
            copy(n, part).start()

    def body(group, carry):
        total, depth = carry
        for j in range(4):
            level = group * 4 + j
            wet = jnp.where(last > level, mask[level], 0).astype(F32)
            wets[level] = wet
            for n, weight in enumerate((mix, thermal, haline)):
                kept[n, level] = jnp.full((8, COLS), weight[level], F32)
            total = total + wet * (thermal[level] * temp[level] - haline[level] * salt[level])
            depth = depth + wet
        return total, depth

    carry = zero, zero
    step = CHUNK // 4
    for part in range(parts):
        for n in range(3):
            copy(n, part).wait()
        carry = lax.fori_loop(part * step, (part + 1) * step, body, carry)
    total, depth = carry
    refs = row_low, row_high, col_low, col_high
    put_surface(refs, A_SURFACE, (surface[...] + total, depth / LEVELS, diag[...]))


def weight_at(kept, n, level):
    value = kept[n, level]
    return jnp.concatenate([value, value], axis=0)


def solve_kernel(
    temp, salt, wets, kept, east_in, north_in,
    col_low, col_high, strip_low, strip_high, *rest,
):
    solved, (inverses, ratios, east, north, sems) = rest[:4], rest[4:]
    zero = jnp.zeros((ROWS, COLS), F32)
    pair = (zero, zero)
    copies = [
        pltpu.make_async_copy(source, target, sems.at[n])
        for n, (source, target) in enumerate(((east_in, east), (north_in, north)))
    ]
    for copy in copies:
        copy.start()

    def down_body(group, carry):
        up, ratio, values, wet, pack = carry
        for j in range(4):
            level = group * 4 + j
            below = jnp.where(
                level < LEVELS - 1, wets[jnp.minimum(level + 1, LEVELS - 1)], 0.0
            )
            down = weight_at(kept, 0, level) * (wet * below)
            inverse = 1.0 / ((1.0 + up + down) - up * ratio)
            sources = (
                temp[level],
                salt[level],
                weight_at(kept, 1, level) * wet,
                weight_at(kept, 2, level) * wet,
            )
            values = tuple((r + up * v) * inverse for r, v in zip(sources, values))
            for ref, v in zip(solved, values):
                ref[level] = v
            ratio = down * inverse
            inverses[level] = inverse
            ratios[level] = ratio
            put_rows(strip_low, strip_high, STRIPS, 2, group, j, wet)
            pack = packed(pack, wet, level)
            up = down
            wet = below
        return up, ratio, values, wet, pack

    carry = lax.fori_loop(0, GROUPS, down_body, (zero, zero, (zero,) * 4, wets[0], pair))
    refs = None, None, col_low, col_high
    put_cols(refs, 2, *carry[-1])
    for copy in copies:
        copy.wait()

    def flow_body(group, pack):
        for j in range(4):
            level = group * 4 + j
            put_rows(strip_low, strip_high, STRIPS, 5, group, j, east[level])
            pack = packed(pack, north[level], level)
        return pack

    put_cols(refs, 5, *lax.fori_loop(0, GROUPS, flow_body, pair))
    strips = strip_low, strip_high
    back_substitute(refs, strips, STRIPS, solved, ratios, ((0, 0), (1, 1), (3, 3), (4, 4)))


def back_substitute(refs, strips, first, solved, ratios, places):
    zero = jnp.zeros((ROWS, COLS), F32)

    def up_body(count, carry):
        values, packs = carry
        group = GROUPS - 1 - count
        for j in (3, 2, 1, 0):
            level = group * 4 + j
            ratio = ratios[level]
            values = tuple(ref[level] + ratio * v for ref, v in zip(solved, values))
            for ref, v, (field, _) in zip(solved, values, places):
                ref[level] = v
                put_rows(*strips, first, field, group, j, v)
            packs = tuple(packed(acc, v, level) for acc, v in zip(packs, values))
        return values, packs

    n = len(places)
    _, packs = lax.fori_loop(0, GROUPS, up_body, ((zero,) * n, ((zero, zero),) * n))
    for (_, block), acc in zip(places, packs):
        put_cols(refs, block, *acc)


def wide_surface(n, own, rows_e, rows_w, from_north, from_south):
    main = jnp.concatenate([own, rows_e, rows_w], axis=0)
    to_north = jnp.concatenate(from_north, axis=0)
    to_south = jnp.concatenate(from_south, axis=0)
    lane = iota((32, COLS), 1)
    side = jnp.where(
        lane < 8,
        roll(to_north, -8 * n, 1),
        jnp.where(lane >= COLS - 8, roll(to_south, 120 - 8 * n, 1), 0.0),
    )
    return jnp.concatenate([main, side], axis=1)


def krylov(c, diag, depth, basis_ref, gram_ref):
    def nb(v):
        return pltpu.roll(v, 31, 0), pltpu.roll(v, 1, 0), pltpu.roll(v, 255, 1), pltpu.roll(v, 1, 1)

    faces = [jnp.minimum(depth, d) for d in nb(depth)]
    centre = (diag - 1.0) + ((faces[0] + faces[1]) + (faces[2] + faces[3]))
    v = c
    own = []
    for k in range(5):
        if k < 4:
            basis_ref[k] = v
        mine = v[:ROWS, :COLS]
        own.append((mine, split(mine)))
        if k < 4:
            e, w, n, s = nb(v)
            v = centre * v - ((faces[0] * e + faces[1] * w) + (faces[2] * n + faces[3] * s))
    highs, lows = [], []
    for i, j in PAIRS:
        p, e = two_prod(own[i][0], own[j][0], own[i][1], own[j][1])
        s, t = two_sum(p[:8], p[8:])
        highs.append(s)
        lows.append(t + (e[:8] + e[8:]))
    pad = [jnp.zeros((8, COLS), F32)] * (16 - len(PAIRS))
    high = jnp.concatenate(highs + pad, axis=0).T
    low = jnp.concatenate(lows + pad, axis=0).T
    parts = [(high[8 * n : 8 * n + 8], low[8 * n : 8 * n + 8]) for n in range(16)]
    while len(parts) > 1:
        parts = [pair_add(a, b) for a, b in zip(parts[::2], parts[1::2])]
    total = parts[0]
    for shift in (4, 2, 1):
        total = pair_add(total, tuple(roll(x, shift, 0) for x in total))
    total = pair_add(total, tuple(roll(x, 124, 1) for x in total))
    first_half = (iota((8, COLS), 1) % 8) < 4
    sums = jnp.where(first_half, total[0], roll(total[1], 4, 1))
    gram_ref[...] = jnp.concatenate([sums] * (gram_ref.shape[0] // 8), axis=0)


def surface_fields(low, high, rows_e, rows_w, cols_n, cols_s, count):
    corners = A_CORNERS if count == 3 else T_CORNERS
    first = 2 * corners

    def column(cols):
        own = cols.shape[0] - 2 * corners
        return [cols[0], cols[1], cols[own], cols[own + corners]]

    return [
        wide_surface(
            n, jnp.concatenate([low[first + n], high[first + n]], axis=0),
            rows_e[first + n], rows_w[first + n], column(cols_n), column(cols_s),
        )
        for n in range(count)
    ]


def first_surface_kernel(low, high, rows_e, rows_w, cols_n, cols_s, basis, gram, fixed):
    c, depth, diag = surface_fields(low, high, rows_e, rows_w, cols_n, cols_s, 3)
    fixed[0] = depth
    fixed[1] = diag
    krylov(c, diag, depth, basis, gram)


def next_surface_kernel(low, high, rows_e, rows_w, cols_n, cols_s, fixed, basis, gram):
    (c,) = surface_fields(low, high, rows_e, rows_w, cols_n, cols_s, 1)
    krylov(c, fixed[1], fixed[0], basis, gram)


def coefficients(gathered):
    parts = [(gathered[8 * n : 8 * n + 8], None) for n in range(gathered.shape[0] // 8)]
    parts = [(p, jnp.zeros_like(p)) for p, _ in parts]
    while len(parts) > 1:
        parts = [pair_add(a, b) for a, b in zip(parts[::2], parts[1::2])]
    total = parts[0]
    for shift in (4, 2, 1):
        total = pair_add(total, tuple(roll(x, shift, 0) for x in total))
    for shift in (4, 2, 1):
        total = pair_add(total, tuple(roll(x, COLS - shift, 1) for x in total))
    table = {}
    for n, (i, j) in enumerate(PAIRS):
        entry = tuple(jnp.broadcast_to(x[:, 8 * n : 8 * n + 1], (8, COLS)) for x in total)
        table[i, j] = table[j, i] = entry
    imaged = {(i, k): pair_add(table[i, k], table[i, k + 1]) for i in range(4) for k in range(i + 1)}
    one = (jnp.ones((8, COLS), F32), jnp.zeros((8, COLS), F32))
    r, p, x = [one], [one], []
    rr = table[0, 0][0]
    for it in range(4):
        den = pair_dot([imaged[it, k] for k in range(it + 1)], p)
        step = rr / (p[it][0] * den)
        x = [x[k] + step * p[k][0] if k < len(x) else step * p[k][0] for k in range(it + 1)]
        if it < 3:
            image = [p[0]] + [pair_add(p[k], p[k - 1]) for k in range(1, it + 1)] + [p[it]]
            moved = [pair_scale(a, -step) for a in image]
            r = [pair_add(r[k], moved[k]) if k < len(r) else moved[k] for k in range(it + 2)]
            new = r[it + 1][0] * pair_dot([table[it + 1, k] for k in range(it + 2)], r)
            ratio = new / rr
            p = [
                pair_add(r[k], pair_scale(p[k], ratio)) if k < len(p) else r[k]
                for k in range(it + 2)
            ]
            rr = new
    return x


class Halo:
    def __init__(self, refs, late):
        self.low, self.high, self.own_s, self.own_n, self.e, self.w, self.n, self.s = refs
        self.late = late
        self.first = STRIPS if late else T_ROWS
        self.own_at, self.far_at = (-2, 2) if late else (0, 0)
        self.even_row = iota((8, COLS), 0) % 2 == 0
        self.even_lane = iota((8, COLS), 1) % 2 == 0
        self.sub = iota((8, COLS), 0)

    def rows(self, field, group):
        at = self.first + field * GROUPS + group
        e, w = self.e[at], self.w[at]
        return (
            jnp.where(self.even_row, roll(self.high[at], -1, 0), roll(self.low[at], 1, 0)),
            jnp.where(self.even_row, e, w),
            jnp.where(self.even_row, roll(e, -1, 0), roll(w, 1, 0)),
        )

    def edge_rows(self, field, group):
        at = self.first + field * GROUPS + group
        return jnp.where(self.even_row, self.e[at], self.w[at])

    def edge_columns(self, block):
        at = self.far_at + 2 * block
        return jnp.concatenate(
            [jnp.where(self.even_lane, self.n[at + h], self.s[at + h]) for h in range(2)], axis=0
        )

    def corners(self, block):
        if self.late:
            at = block - 1
            return self.e[at], self.e[at + 5], self.w[at], self.w[at + 5]
        east = self.n.shape[0] - 2 * T_CORNERS + block
        west = east + T_CORNERS
        return self.n[east], self.s[east], self.n[west], self.s[west]

    def columns(self, block):
        inner, outer = [], []
        for h in range(2):
            at = self.own_at + 2 * block + h
            inner.append(
                jnp.where(self.even_lane, roll(self.own_n[at], -1, 1), roll(self.own_s[at], 1, 1))
            )
            at = self.far_at + 2 * block + h
            outer.append(jnp.where(self.even_lane, roll(self.n[at], -1, 1), roll(self.s[at], 1, 1)))
        ne, se, nw, sw = self.corners(block)
        corner = jnp.where(
            self.sub < 4,
            jnp.where(self.even_lane, ne, se),
            jnp.where(self.even_lane, nw, sw),
        )
        return (
            jnp.concatenate(inner, axis=0),
            jnp.concatenate([self.edge_columns(block), corner], axis=0),
            jnp.concatenate(outer, axis=0),
        )


def ends(v):
    return pltpu.roll(v, v.shape[0] - 1, 0), pltpu.roll(v, 1, 0)


def step_kernel(
    final,
    temp, salt, temp_response, salt_response, east, north, wets, fixed, basis, gathered,
    *refs,
):
    if not final:
        kept, refs = refs[0], refs[1:]
        weight = functools.partial(weight_at, kept)
    a_halo = Halo(refs[:8], True)
    if final:
        t_halo = Halo(refs[8:16], False)
        new_temp, new_salt, new_surface = refs[16:]
    else:
        t_halo = a_halo
        inverses, ratios, new_temp, new_salt, *messages = refs[8:]
    tracers = ((temp, temp_response, 0, 3, 1.0), (salt, salt_response, 1, 4, -1.0))

    weights = coefficients(gathered[...])
    weights = [jnp.concatenate([jnp.concatenate([w] * 4, axis=0)] * 2, axis=1) for w in weights]
    full = sum(weights[k] * basis[k] for k in range(4))
    multiplier = full[:ROWS, :COLS]
    surface = fixed[1, :ROWS, :COLS] * multiplier
    if final:
        new_surface[...] = surface

    sub = iota((8, COLS), 0)
    even_row = sub % 2 == 0
    ring = jnp.concatenate([full[:ROWS], jnp.where(
        iota((8, 2 * COLS), 0) < 4, full[16:24], full[24:])], axis=0)
    even_lane = iota((24, COLS), 1) % 2 == 0

    def lanes(a, b):
        return jnp.where(
            even_lane,
            jnp.broadcast_to(ring[:, a : a + 1], (24, COLS)),
            jnp.broadcast_to(ring[:, b : b + 1], (24, COLS)),
        )

    def both_rows(a, b):
        return jnp.where(
            even_row,
            jnp.broadcast_to(full[a : a + 1, :COLS], (8, COLS)),
            jnp.broadcast_to(full[b : b + 1, :COLS], (8, COLS)),
        )

    column_m = [lanes(127, 0)[:ROWS], lanes(128, 255), lanes(129, 254)[:ROWS]]
    row_m = [both_rows(15, 0), both_rows(16, 31), both_rows(17, 30)]

    own = slice(0, ROWS)
    lane_sign = jnp.where(even_lane[own], 0.05, -0.05)
    wet0, wet1, wet2 = a_halo.columns(3)
    north1 = lane_sign * a_halo.edge_columns(6)
    e, w = ends(wet1)
    around1 = wet1[own] * ((e + w)[own] + (wet0 + wet2))
    column_wet = wet1
    column_q, column_out = [], []
    for _, _, field, response, sign in tracers:
        g = [
            b + (sign * m) * a
            for b, m, a in zip(t_halo.columns(field + 1), column_m, a_halo.columns(response + 1))
        ]
        q = wet1 * g[1]
        e, w = ends(q)
        near = (e + w)[own] + (wet0 * g[0] + wet2 * g[2])
        lap = wet1[own] * near - around1 * g[1][own]
        column_q.append(q)
        column_out.append(north1 * q[own] - 0.01 * lap)

    def corner_rows(v):
        return jnp.where(
            even_row,
            jnp.broadcast_to(v[16:17], (8, COLS)),
            jnp.broadcast_to(v[23:24], (8, COLS)),
        )

    corner_wet = corner_rows(column_wet)
    corner_q = [corner_rows(q) for q in column_q]
    column_wet = column_wet[own]
    column_q = [q[own] for q in column_q]

    lane8 = iota((8, COLS), 1)
    lane = iota((ROWS, COLS), 1)
    row = iota((ROWS, COLS), 0)
    row_sign = jnp.where(even_row, 0.05, -0.05)

    def beside(v, corner):
        return jnp.where(lane8 == COLS - 1, corner, pltpu.roll(v, COLS - 1, 1)) + jnp.where(
            lane8 == 0, corner, pltpu.roll(v, 1, 1)
        )

    def strips(group):
        shifts = [(127 - 2 * (group * 4 + j)) & 127 for j in range(4)]

        def corners(v):
            out = pltpu.roll(v, shifts[0], 1)
            for j in range(1, 4):
                out = jnp.where(sub // 2 == j, pltpu.roll(v, shifts[j], 1), out)
            return out

        wet0, wet1, wet2 = a_halo.rows(2, group)
        east1 = row_sign * a_halo.edge_rows(5, group)
        around1 = wet1 * ((wet0 + wet2) + beside(wet1, corners(corner_wet)))
        qs, outs = [], []
        for n, (_, _, field, response, sign) in enumerate(tracers):
            g = [
                b + (sign * m) * a
                for b, m, a in zip(
                    t_halo.rows(field, group), row_m, a_halo.rows(response, group)
                )
            ]
            q = wet1 * g[1]
            near = (wet0 * g[0] + wet2 * g[2]) + beside(q, corners(corner_q[n]))
            lap = wet1 * near - around1 * g[1]
            qs.append(q)
            outs.append(east1 * q - 0.01 * lap)
        return wet1, qs, outs

    def body(group, carry):
        row_wet, row_q, row_out = strips(group)
        for j in range(4):
            level = group * 4 + j
            shift = (127 - 2 * level) & 127

            def four(ve, vw, vn, vs, row_strip, column_strip):
                r = roll(row_strip, 7 - 2 * j, 0)
                r = jnp.concatenate([r, r], axis=0)
                c = pltpu.roll(column_strip, shift, 1)
                return (
                    jnp.where(row == ROWS - 1, r, pltpu.roll(ve, ROWS - 1, 0)),
                    jnp.where(row == 0, r, pltpu.roll(vw, 1, 0)),
                    jnp.where(lane == COLS - 1, c, pltpu.roll(vn, COLS - 1, 1)),
                    jnp.where(lane == 0, c, pltpu.roll(vs, 1, 1)),
                )

            wet = wets[level]
            fe, fn = east[level], north[level]
            we, ww, wn, ws = four(wet, wet, wet, wet, row_wet, column_wet)
            around = wet * ((we + ww) + (wn + ws))
            diagonal = around + wet * (fe * (ww - we) + fn * (ws - wn))
            done = []
            for n, (field, response, _, _, sign) in enumerate(tracers):
                g = field[level] + (sign * multiplier) * response[level]
                q = wet * g
                e, w, no, so = four(q, q, q, q, row_q[n], column_q[n])
                near = wet * ((e + w) + (no + so))
                small = 0.01 * (near - around * g)
                u, v = (0.05 * fe) * q, (0.05 * fn) * q
                e, w, no, so = four(
                    u - small, -u - small, v - small, -v - small, row_out[n], column_out[n]
                )
                done.append(
                    (g + 0.05 * (near - diagonal * g))
                    + (wet * ((e + w) + (no + so)) + around * small)
                )
            t, s = done
            if final:
                new_temp[level] = t
                new_salt[level] = s
            else:
                above, total, pt, ps = carry
                total = total + wet * (weight(1, level) * t - weight(2, level) * s)
                up = weight(0, jnp.maximum(level - 1, 0)) * (above * wet)
                inverse = inverses[level]
                pt = (t + up * pt) * inverse
                ps = (s + up * ps) * inverse
                new_temp[level] = pt
                new_salt[level] = ps
                carry = (wet, total, pt, ps)
        return carry

    zero = jnp.zeros((ROWS, COLS), F32)
    if final:
        lax.fori_loop(0, GROUPS, body, 0)
    else:
        _, total, _, _ = lax.fori_loop(0, GROUPS, body, (zero,) * 4)
        put_surface(messages, T_SURFACE, (surface + total,))
        back_substitute(
            messages, messages[:2], T_ROWS, (new_temp, new_salt), ratios, ((0, 1), (1, 2))
        )


def shape(*dims):
    return jax.ShapeDtypeStruct(dims, F32)


VMEM = pl.BlockSpec(memory_space=pltpu.VMEM)
HBM = pl.BlockSpec(memory_space=pltpu.HBM)
SMEM = pl.BlockSpec(memory_space=pltpu.SMEM)


def head(*block):
    return pl.BlockSpec(block, lambda i: (0,) * len(block), memory_space=pltpu.VMEM)


def call(kernel, outs, in_specs, out_specs=None, scratch=(), name=None, grid=None, room=40, aliases=None):
    extra = {} if grid is None else {"grid": grid}
    if aliases:
        extra["input_output_aliases"] = aliases
    return pl.pallas_call(
        kernel,
        out_shape=outs,
        in_specs=in_specs,
        out_specs=[VMEM] * len(outs) if out_specs is None else out_specs,
        scratch_shapes=scratch,
        compiler_params=pltpu.CompilerParams(vmem_limit_bytes=room * 1024 * 1000),
        name=name,
        **extra,
    )


def message_shapes(surfaces, row_fields, col_fields, corner_fields):
    rows = shape(2 * (1 + corner_fields) + surfaces + GROUPS * row_fields, 8, COLS)
    cols = shape(2 * (1 + col_fields), 8, COLS)
    return [rows, rows, cols, cols]


def solution(mesh):
    nx, ny = mesh.shape["gx"], mesh.shape["gy"]
    devices = nx * ny
    both = ("gx", "gy")
    eastward = [(i, (i + 1) % nx) for i in range(nx)]
    northward = [(j, (j + 1) % ny) for j in range(ny)]

    def back(pairs):
        return [(b, a) for a, b in pairs]

    def exchange(messages, corners, behind=()):
        row_low, row_high, col_low, col_high = messages
        rows_e = lax.ppermute(row_low, "gx", back(eastward))
        rows_w = lax.ppermute(row_high, "gx", eastward)
        own = col_low.shape[0]
        out = shape(own + 2 * corners + sum(b.shape[0] for b in behind[:1]), 8, COLS)
        to_south, to_north = call(
            forward_kernel, [out, out],
            [head(own, 8, COLS)] * 2
            + [head(2 * corners, 8, COLS)] * 2
            + [head(*b.shape) for b in behind],
            [head(*out.shape)] * 2, name="corners", grid=(1,),
        )(col_low, col_high, rows_e, rows_w, *behind)
        cols_n = lax.ppermute(to_south, "gy", back(northward))
        cols_s = lax.ppermute(to_north, "gy", northward)
        return [rows_e, rows_w, cols_n, cols_s]

    def exchange_strips(low, high, cols_n, cols_s):
        block = head(STRIPS, 8, COLS)
        low, high = call(
            strip_corner_kernel, [shape(*low.shape)] * 2,
            [block] * 2 + [head(*cols_n.shape)] * 2, [block] * 2,
            name="strip_corners", grid=(1,), aliases={0: 0, 1: 1},
        )(low, high, cols_n, cols_s)
        return [low, high], [
            lax.ppermute(low, "gx", back(eastward)), lax.ppermute(high, "gx", eastward)
        ]

    def all_sum(block):
        return lax.all_to_all(block, both, 0, 0, tiled=True)

    def surface_specs(rows, cols):
        return [head(rows, 8, COLS)] * 4 + [head(cols, 8, COLS)] * 2

    basis_shape = shape(4, 32, 2 * COLS)
    gram_shape = shape(devices, COLS)
    field = shape(LEVELS, ROWS, COLS)
    tile = shape(ROWS, COLS)

    def whole(*dims):
        return head(*dims)

    def per_device(
        sens_temp, sens_salt, sens_surface, flow_east, flow_north, mix_profile,
        thermal_weight, haline_weight, surface_diag, land_mask, bottom_level,
    ):
        def in_hbm(*xs):
            return [pltpu.with_memory_space_constraint(x, pltpu.HBM) for x in xs]

        *sent, temp, salt, wets, kept = call(
            combine_kernel,
            message_shapes(3, 0, 0, 0) + [field] * 3 + [shape(3, LEVELS, 8, COLS)],
            [SMEM] * 3 + [HBM] * 3 + [VMEM] * 3,
            scratch=[
                pltpu.VMEM((LEVELS, ROWS, COLS), jnp.int32),
                pltpu.SemaphoreType.DMA((3, LEVELS // CHUNK)),
            ],
            name="combine",
        )(
            *in_hbm(
                mix_profile, thermal_weight, haline_weight, sens_temp, sens_salt, land_mask,
                bottom_level, sens_surface, surface_diag,
            )
        )
        cols = shape(12, 8, COLS)
        strip = shape(STRIPS + 6 * GROUPS, 8, COLS)
        (col_low, col_high, strip_low, strip_high,
         temp, salt, temp_response, salt_response, inverses, ratios, east, north) = call(
            solve_kernel,
            [cols, cols, strip, strip] + [field] * 8,
            [VMEM] * 4 + [HBM] * 2,
            scratch=[pltpu.SemaphoreType.DMA((2,))],
            name="solve",
        )(temp, salt, wets, kept, *in_hbm(flow_east, flow_north))
        got = exchange(sent, A_CORNERS, (col_low, col_high))
        strips, far_strips = exchange_strips(strip_low, strip_high, got[2], got[3])
        halo = [*strips, col_low, col_high, *far_strips, *got[2:]]
        basis, gram, fixed = call(
            first_surface_kernel,
            [basis_shape, gram_shape, shape(2, 32, 2 * COLS)],
            surface_specs(A_ROWS, 2 + 2 * A_CORNERS),
            [head(4, 32, 2 * COLS), head(devices, COLS), head(2, 32, 2 * COLS)],
            name="first_surface",
            grid=(1,),
        )(sent[0], sent[1], *got)
        gathered = all_sum(gram)

        def step(final, temp, salt, basis, gathered, more, outs):
            weights = [] if final else [kept]
            return call(
                functools.partial(step_kernel, final),
                outs,
                [VMEM] * (18 + len(weights) + len(more)),
                name="last_step" if final else "first_step",
            )(
                temp, salt, temp_response, salt_response, east, north, wets, fixed,
                basis, gathered, *weights, *halo, *more,
            )

        temp, salt, *second = step(
            False, temp, salt, basis, gathered, [inverses, ratios],
            [field, field] + message_shapes(1, 2, 2, 2),
        )
        more = exchange(second, T_CORNERS)
        basis, gram = call(
            next_surface_kernel,
            [basis_shape, gram_shape],
            surface_specs(T_ROWS, 2 * 3 + 2 * T_CORNERS) + [head(2, 32, 2 * COLS)],
            [head(4, 32, 2 * COLS), head(devices, COLS)],
            name="next_surface",
            grid=(1,),
        )(second[0], second[1], *more, fixed)
        gathered = all_sum(gram)
        return tuple(
            step(True, temp, salt, basis, gathered, [*second, *more], [field, field, tile])
        )

    in_specs = (
        P(None, "gx", "gy"),
        P(None, "gx", "gy"),
        P("gx", "gy"),
        P(None, "gx", "gy"),
        P(None, "gx", "gy"),
        P(),
        P(),
        P(),
        P("gx", "gy"),
        P(None, "gx", "gy"),
        P("gx", "gy"),
    )
    out_specs = (P(None, "gx", "gy"), P(None, "gx", "gy"), P("gx", "gy"))
    return jax.shard_map(
        per_device, mesh=mesh, in_specs=in_specs, out_specs=out_specs, check_vma=False
    )
```

```python
import functools

import jax
import jax.numpy as jnp
from jax import lax
from jax.experimental import pallas as pl
from jax.experimental.pallas import tpu as pltpu
from jax.sharding import PartitionSpec as P

LEVELS = 48
ROWS = 16
COLS = 128
GROUPS = LEVELS // 4
CHUNK = 12
F32 = jnp.float32
PAIRS = [(i, j) for i in range(4) for j in range(i, 5)]


def two_sum(a, b):
    s = a + b
    t = s - a
    return s, (a - (s - t)) + (b - t)


def fast_two_sum(a, b):
    s = a + b
    return s, b - (s - a)


def split(a):
    c = a * 4097.0
    high = c - (c - a)
    return high, a - high


def two_prod(a, b, a_parts=None, b_parts=None):
    ah, al = split(a) if a_parts is None else a_parts
    bh, bl = split(b) if b_parts is None else b_parts
    p = a * b
    return p, ((ah * bh - p) + ah * bl + al * bh) + al * bl


def pair_add(x, y):
    s, t = two_sum(x[0], y[0])
    return fast_two_sum(s, t + (x[1] + y[1]))


def pair_scale(x, c):
    p, e = two_prod(x[0], c)
    return fast_two_sum(p, e + x[1] * c)


def pair_dot(xs, ys):
    terms, rest = [], []
    for x, y in zip(xs, ys):
        p, e = two_prod(x[0], y[0])
        terms.append(p)
        rest.append(e + (x[0] * y[1] + x[1] * y[0]))
    while len(terms) > 1:
        sums = [two_sum(a, b) for a, b in zip(terms[::2], terms[1::2])]
        rest += [e for _, e in sums]
        terms = [s for s, _ in sums] + terms[len(sums) * 2 :]
    while len(rest) > 1:
        rest = [a + b for a, b in zip(rest[::2], rest[1::2])] + rest[len(rest) // 2 * 2 :]
    return terms[0] + rest[0]


def roll(x, shift, axis):
    shift = shift % x.shape[axis]
    return x if shift == 0 else pltpu.roll(x, shift, axis)


def iota(shape, axis):
    return lax.broadcasted_iota(jnp.int32, shape, axis)


A_CORNERS, T_CORNERS = 1, 3
A_SURFACE, T_SURFACE = 2 * A_CORNERS, 2 * T_CORNERS
A_ROWS, T_ROWS = A_SURFACE + 3, T_SURFACE + 1
STRIPS = 12


def put_rows(low_ref, high_ref, first, field, group, j, cells):
    at = first + field * GROUPS + group
    low_ref[at, 2 * j : 2 * j + 2, :] = cells[:2]
    high_ref[at, 2 * j : 2 * j + 2, :] = cells[ROWS - 2 :]


def packed(acc, cells, level):
    low, high = acc
    mine = lax.shift_right_logical(iota((ROWS, COLS), 1), 1) == level
    low = jnp.where(mine, pltpu.roll(cells, 2 * level, 1), low)
    high = jnp.where(mine, pltpu.roll(cells, 2 * level + 2, 1), high)
    return low, high


def put_surface(refs, first, fields):
    row_low, row_high, col_low, col_high = refs
    low = jnp.zeros((ROWS, COLS), F32)
    high = low
    lane_group = iota((ROWS, COLS), 1) // 8
    for n, cells in enumerate(fields):
        row_low[first + n] = cells[:8]
        row_high[first + n] = cells[8:]
        low = jnp.where(lane_group == n, roll(cells, 8 * n, 1), low)
        high = jnp.where(lane_group == n, roll(cells, 8 * n + 8, 1), high)
    put_cols(refs, 0, low, high)


def put_cols(refs, n, low, high):
    row_low, row_high, col_low, col_high = refs
    count = 0 if row_low is None else corners_of(row_low)
    for col, side, cells in ((col_low, 0, low), (col_high, count, high)):
        col[2 * n] = cells[:8]
        col[2 * n + 1] = cells[8:]
        if n < count:
            row_low[side + n] = cells[:8]
            row_high[side + n] = cells[8:]


def corners_of(rows):
    return A_CORNERS if rows.shape[0] == A_ROWS else T_CORNERS


def forward_kernel(own_low, own_high, rows_e, rows_w, *refs):
    count = rows_e.shape[0] // 2
    own = own_low.shape[0]
    more, outs = refs[:-2], refs[-2:]
    place = lax.axis_index("gy")
    ends_at = 0, lax.axis_size("gy") - 1
    for n, (out, mine, end) in enumerate(zip(outs, (own_low, own_high), ends_at)):
        inner = place != end
        side = n * count
        out[:own] = jnp.where(inner, mine[...], 0.0)
        out[own : own + count] = jnp.where(inner, rows_e[side : side + count], 0.0)
        out[own + count : own + 2 * count] = jnp.where(inner, rows_w[side : side + count], 0.0)
        if more:
            out[own + 2 * count :] = jnp.where(inner, more[n][...], 0.0)


def strip_corner_kernel(_low, _high, cols_n, cols_s, out_low, out_high):
    for side, cols in enumerate((cols_n, cols_s)):
        for n in range(5):
            out_low[5 * side + n] = cols[4 + 2 * n]
            out_high[5 * side + n] = cols[5 + 2 * n]
    for out in (out_low, out_high):
        out[10:] = jnp.zeros((STRIPS - 10, 8, COLS), F32)


def wet_at(mask, last, level):
    return jnp.where(last > level, mask[jnp.minimum(level, LEVELS - 1)], 0).astype(F32)


def combine_kernel(
    mix, thermal, haline, temp_in, salt_in, mask_in, bottom, surface, diag,
    row_low, row_high, col_low, col_high, temp, salt, wets, kept, mask, sems,
):
    last = bottom[...]
    zero = jnp.zeros((ROWS, COLS), F32)
    fields = (mask_in, mask), (temp_in, temp), (salt_in, salt)
    parts = LEVELS // CHUNK

    def copy(n, part):
        source, target = fields[n]
        levels = pl.ds(part * CHUNK, CHUNK)
        return pltpu.make_async_copy(source.at[levels], target.at[levels], sems.at[n, part])

    for part in range(parts):
        for n in range(3):
            copy(n, part).start()

    def body(group, carry):
        total, depth = carry
        for j in range(4):
            level = group * 4 + j
            wet = jnp.where(last > level, mask[level], 0).astype(F32)
            wets[level] = wet
            for n, weight in enumerate((mix, thermal, haline)):
                kept[n, level] = jnp.full((8, COLS), weight[level], F32)
            total = total + wet * (thermal[level] * temp[level] - haline[level] * salt[level])
            depth = depth + wet
        return total, depth

    carry = zero, zero
    step = CHUNK // 4
    for part in range(parts):
        for n in range(3):
            copy(n, part).wait()
        carry = lax.fori_loop(part * step, (part + 1) * step, body, carry)
    total, depth = carry
    refs = row_low, row_high, col_low, col_high
    put_surface(refs, A_SURFACE, (surface[...] + total, depth / LEVELS, diag[...]))


def weight_at(kept, n, level):
    value = kept[n, level]
    return jnp.concatenate([value, value], axis=0)


def solve_kernel(
    temp, salt, wets, kept, east_in, north_in,
    col_low, col_high, strip_low, strip_high, *rest,
):
    solved, (inverses, ratios, east, north, sems) = rest[:4], rest[4:]
    zero = jnp.zeros((ROWS, COLS), F32)
    pair = (zero, zero)
    copies = [
        pltpu.make_async_copy(source, target, sems.at[n])
        for n, (source, target) in enumerate(((east_in, east), (north_in, north)))
    ]
    for copy in copies:
        copy.start()

    def down_body(group, carry):
        up, ratio, values, wet, pack = carry
        for j in range(4):
            level = group * 4 + j
            below = jnp.where(
                level < LEVELS - 1, wets[jnp.minimum(level + 1, LEVELS - 1)], 0.0
            )
            down = weight_at(kept, 0, level) * (wet * below)
            inverse = 1.0 / ((1.0 + up + down) - up * ratio)
            sources = (
                temp[level],
                salt[level],
                weight_at(kept, 1, level) * wet,
                weight_at(kept, 2, level) * wet,
            )
            values = tuple((r + up * v) * inverse for r, v in zip(sources, values))
            for ref, v in zip(solved, values):
                ref[level] = v
            ratio = down * inverse
            inverses[level] = inverse
            ratios[level] = ratio
            put_rows(strip_low, strip_high, STRIPS, 2, group, j, wet)
            pack = packed(pack, wet, level)
            up = down
            wet = below
        return up, ratio, values, wet, pack

    carry = lax.fori_loop(0, GROUPS, down_body, (zero, zero, (zero,) * 4, wets[0], pair))
    refs = None, None, col_low, col_high
    put_cols(refs, 2, *carry[-1])
    for copy in copies:
        copy.wait()

    def flow_body(group, pack):
        for j in range(4):
            level = group * 4 + j
            put_rows(strip_low, strip_high, STRIPS, 5, group, j, east[level])
            pack = packed(pack, north[level], level)
        return pack

    put_cols(refs, 5, *lax.fori_loop(0, GROUPS, flow_body, pair))
    strips = strip_low, strip_high
    back_substitute(refs, strips, STRIPS, solved, ratios, ((0, 0), (1, 1), (3, 3), (4, 4)))


def back_substitute(refs, strips, first, solved, ratios, places):
    zero = jnp.zeros((ROWS, COLS), F32)

    def up_body(count, carry):
        values, packs = carry
        group = GROUPS - 1 - count
        for j in (3, 2, 1, 0):
            level = group * 4 + j
            ratio = ratios[level]
            values = tuple(ref[level] + ratio * v for ref, v in zip(solved, values))
            for ref, v, (field, _) in zip(solved, values, places):
                ref[level] = v
                put_rows(*strips, first, field, group, j, v)
            packs = tuple(packed(acc, v, level) for acc, v in zip(packs, values))
        return values, packs

    n = len(places)
    _, packs = lax.fori_loop(0, GROUPS, up_body, ((zero,) * n, ((zero, zero),) * n))
    for (_, block), acc in zip(places, packs):
        put_cols(refs, block, *acc)


def wide_surface(n, own, rows_e, rows_w, from_north, from_south):
    main = jnp.concatenate([own, rows_e, rows_w], axis=0)
    to_north = jnp.concatenate(from_north, axis=0)
    to_south = jnp.concatenate(from_south, axis=0)
    lane = iota((32, COLS), 1)
    side = jnp.where(
        lane < 8,
        roll(to_north, -8 * n, 1),
        jnp.where(lane >= COLS - 8, roll(to_south, 120 - 8 * n, 1), 0.0),
    )
    return jnp.concatenate([main, side], axis=1)


def krylov(c, diag, depth, basis_ref, gram_ref):
    def nb(v):
        return pltpu.roll(v, 31, 0), pltpu.roll(v, 1, 0), pltpu.roll(v, 255, 1), pltpu.roll(v, 1, 1)

    faces = [jnp.minimum(depth, d) for d in nb(depth)]
    centre = (diag - 1.0) + ((faces[0] + faces[1]) + (faces[2] + faces[3]))
    v = c
    own = []
    for k in range(5):
        if k < 4:
            basis_ref[k] = v
        mine = v[:ROWS, :COLS]
        own.append((mine, split(mine)))
        if k < 4:
            e, w, n, s = nb(v)
            v = centre * v - ((faces[0] * e + faces[1] * w) + (faces[2] * n + faces[3] * s))
    highs, lows = [], []
    for i, j in PAIRS:
        p, e = two_prod(own[i][0], own[j][0], own[i][1], own[j][1])
        s, t = two_sum(p[:8], p[8:])
        highs.append(s)
        lows.append(t + (e[:8] + e[8:]))
    pad = [jnp.zeros((8, COLS), F32)] * (16 - len(PAIRS))
    high = jnp.concatenate(highs + pad, axis=0).T
    low = jnp.concatenate(lows + pad, axis=0).T
    parts = [(high[8 * n : 8 * n + 8], low[8 * n : 8 * n + 8]) for n in range(16)]
    while len(parts) > 1:
        parts = [pair_add(a, b) for a, b in zip(parts[::2], parts[1::2])]
    total = parts[0]
    for shift in (4, 2, 1):
        total = pair_add(total, tuple(roll(x, shift, 0) for x in total))
    total = pair_add(total, tuple(roll(x, 124, 1) for x in total))
    first_half = (iota((8, COLS), 1) % 8) < 4
    sums = jnp.where(first_half, total[0], roll(total[1], 4, 1))
    gram_ref[...] = jnp.concatenate([sums] * (gram_ref.shape[0] // 8), axis=0)


def surface_fields(low, high, rows_e, rows_w, cols_n, cols_s, count):
    corners = A_CORNERS if count == 3 else T_CORNERS
    first = 2 * corners

    def column(cols):
        own = cols.shape[0] - 2 * corners
        return [cols[0], cols[1], cols[own], cols[own + corners]]

    return [
        wide_surface(
            n, jnp.concatenate([low[first + n], high[first + n]], axis=0),
            rows_e[first + n], rows_w[first + n], column(cols_n), column(cols_s),
        )
        for n in range(count)
    ]


def first_surface_kernel(low, high, rows_e, rows_w, cols_n, cols_s, basis, gram, fixed):
    c, depth, diag = surface_fields(low, high, rows_e, rows_w, cols_n, cols_s, 3)
    fixed[0] = depth
    fixed[1] = diag
    krylov(c, diag, depth, basis, gram)


def next_surface_kernel(low, high, rows_e, rows_w, cols_n, cols_s, fixed, basis, gram):
    (c,) = surface_fields(low, high, rows_e, rows_w, cols_n, cols_s, 1)
    krylov(c, fixed[1], fixed[0], basis, gram)


def coefficients(gathered):
    parts = [(gathered[8 * n : 8 * n + 8], None) for n in range(gathered.shape[0] // 8)]
    parts = [(p, jnp.zeros_like(p)) for p, _ in parts]
    while len(parts) > 1:
        parts = [pair_add(a, b) for a, b in zip(parts[::2], parts[1::2])]
    total = parts[0]
    for shift in (4, 2, 1):
        total = pair_add(total, tuple(roll(x, shift, 0) for x in total))
    for shift in (4, 2, 1):
        total = pair_add(total, tuple(roll(x, COLS - shift, 1) for x in total))
    table = {}
    for n, (i, j) in enumerate(PAIRS):
        entry = tuple(jnp.broadcast_to(x[:, 8 * n : 8 * n + 1], (8, COLS)) for x in total)
        table[i, j] = table[j, i] = entry
    imaged = {(i, k): pair_add(table[i, k], table[i, k + 1]) for i in range(4) for k in range(i + 1)}
    one = (jnp.ones((8, COLS), F32), jnp.zeros((8, COLS), F32))
    r, p, x = [one], [one], []
    rr = table[0, 0][0]
    for it in range(4):
        den = pair_dot([imaged[it, k] for k in range(it + 1)], p)
        step = rr / (p[it][0] * den)
        x = [x[k] + step * p[k][0] if k < len(x) else step * p[k][0] for k in range(it + 1)]
        if it < 3:
            image = [p[0]] + [pair_add(p[k], p[k - 1]) for k in range(1, it + 1)] + [p[it]]
            moved = [pair_scale(a, -step) for a in image]
            r = [pair_add(r[k], moved[k]) if k < len(r) else moved[k] for k in range(it + 2)]
            new = r[it + 1][0] * pair_dot([table[it + 1, k] for k in range(it + 2)], r)
            ratio = new / rr
            p = [
                pair_add(r[k], pair_scale(p[k], ratio)) if k < len(p) else r[k]
                for k in range(it + 2)
            ]
            rr = new
    return x


class Halo:
    def __init__(self, refs, late):
        self.low, self.high, self.own_s, self.own_n, self.e, self.w, self.n, self.s = refs
        self.late = late
        self.first = STRIPS if late else T_ROWS
        self.own_at, self.far_at = (-2, 2) if late else (0, 0)
        self.even_row = iota((8, COLS), 0) % 2 == 0
        self.even_lane = iota((8, COLS), 1) % 2 == 0
        self.sub = iota((8, COLS), 0)

    def rows(self, field, group):
        at = self.first + field * GROUPS + group
        e, w = self.e[at], self.w[at]
        return (
            jnp.where(self.even_row, roll(self.high[at], -1, 0), roll(self.low[at], 1, 0)),
            jnp.where(self.even_row, e, w),
            jnp.where(self.even_row, roll(e, -1, 0), roll(w, 1, 0)),
        )

    def edge_rows(self, field, group):
        at = self.first + field * GROUPS + group
        return jnp.where(self.even_row, self.e[at], self.w[at])

    def edge_columns(self, block):
        at = self.far_at + 2 * block
        return jnp.concatenate(
            [jnp.where(self.even_lane, self.n[at + h], self.s[at + h]) for h in range(2)], axis=0
        )

    def corners(self, block):
        if self.late:
            at = block - 1
            return self.e[at], self.e[at + 5], self.w[at], self.w[at + 5]
        east = self.n.shape[0] - 2 * T_CORNERS + block
        west = east + T_CORNERS
        return self.n[east], self.s[east], self.n[west], self.s[west]

    def columns(self, block):
        inner, outer = [], []
        for h in range(2):
            at = self.own_at + 2 * block + h
            inner.append(
                jnp.where(self.even_lane, roll(self.own_n[at], -1, 1), roll(self.own_s[at], 1, 1))
            )
            at = self.far_at + 2 * block + h
            outer.append(jnp.where(self.even_lane, roll(self.n[at], -1, 1), roll(self.s[at], 1, 1)))
        ne, se, nw, sw = self.corners(block)
        corner = jnp.where(
            self.sub < 4,
            jnp.where(self.even_lane, ne, se),
            jnp.where(self.even_lane, nw, sw),
        )
        return (
            jnp.concatenate(inner, axis=0),
            jnp.concatenate([self.edge_columns(block), corner], axis=0),
            jnp.concatenate(outer, axis=0),
        )


def ends(v):
    return pltpu.roll(v, v.shape[0] - 1, 0), pltpu.roll(v, 1, 0)


def step_kernel(
    final,
    temp, salt, temp_response, salt_response, east, north, wets, fixed, basis, gathered,
    *refs,
):
    if not final:
        kept, refs = refs[0], refs[1:]
        weight = functools.partial(weight_at, kept)
    a_halo = Halo(refs[:8], True)
    if final:
        t_halo = Halo(refs[8:16], False)
        arounds, diagonals = refs[16:18]
        temp_out, salt_out, new_surface, new_temp, new_salt, sems = refs[18:]
    else:
        t_halo = a_halo
        inverses, ratios, new_temp, new_salt, arounds, diagonals, *messages = refs[8:]
    tracers = ((temp, temp_response, 0, 3, 1.0), (salt, salt_response, 1, 4, -1.0))

    weights = coefficients(gathered[...])
    weights = [jnp.concatenate([jnp.concatenate([w] * 4, axis=0)] * 2, axis=1) for w in weights]
    full = sum(weights[k] * basis[k] for k in range(4))
    multiplier = full[:ROWS, :COLS]
    surface = fixed[1, :ROWS, :COLS] * multiplier
    if final:
        new_surface[...] = surface

    sub = iota((8, COLS), 0)
    even_row = sub % 2 == 0
    ring = jnp.concatenate([full[:ROWS], jnp.where(
        iota((8, 2 * COLS), 0) < 4, full[16:24], full[24:])], axis=0)
    even_lane = iota((24, COLS), 1) % 2 == 0

    def lanes(a, b):
        return jnp.where(
            even_lane,
            jnp.broadcast_to(ring[:, a : a + 1], (24, COLS)),
            jnp.broadcast_to(ring[:, b : b + 1], (24, COLS)),
        )

    def both_rows(a, b):
        return jnp.where(
            even_row,
            jnp.broadcast_to(full[a : a + 1, :COLS], (8, COLS)),
            jnp.broadcast_to(full[b : b + 1, :COLS], (8, COLS)),
        )

    column_m = [lanes(127, 0)[:ROWS], lanes(128, 255), lanes(129, 254)[:ROWS]]
    row_m = [both_rows(15, 0), both_rows(16, 31), both_rows(17, 30)]

    own = slice(0, ROWS)
    lane_sign = jnp.where(even_lane[own], 0.05, -0.05)
    wet0, wet1, wet2 = a_halo.columns(3)
    north1 = lane_sign * a_halo.edge_columns(6)
    e, w = ends(wet1)
    around1 = wet1[own] * ((e + w)[own] + (wet0 + wet2))
    column_wet = wet1
    column_q, column_out = [], []
    for _, _, field, response, sign in tracers:
        g = [
            b + (sign * m) * a
            for b, m, a in zip(t_halo.columns(field + 1), column_m, a_halo.columns(response + 1))
        ]
        q = wet1 * g[1]
        e, w = ends(q)
        near = (e + w)[own] + (wet0 * g[0] + wet2 * g[2])
        lap = wet1[own] * near - around1 * g[1][own]
        column_q.append(q)
        column_out.append(north1 * q[own] - 0.01 * lap)

    def corner_rows(v):
        return jnp.where(
            even_row,
            jnp.broadcast_to(v[16:17], (8, COLS)),
            jnp.broadcast_to(v[23:24], (8, COLS)),
        )

    corner_wet = corner_rows(column_wet)
    corner_q = [corner_rows(q) for q in column_q]
    column_wet = column_wet[own]
    column_q = [q[own] for q in column_q]

    lane8 = iota((8, COLS), 1)
    lane = iota((ROWS, COLS), 1)
    row = iota((ROWS, COLS), 0)
    row_sign = jnp.where(even_row, 0.05, -0.05)

    def beside(v, corner):
        return jnp.where(lane8 == COLS - 1, corner, pltpu.roll(v, COLS - 1, 1)) + jnp.where(
            lane8 == 0, corner, pltpu.roll(v, 1, 1)
        )

    def strips(group):
        shifts = [(127 - 2 * (group * 4 + j)) & 127 for j in range(4)]

        def corners(v):
            out = pltpu.roll(v, shifts[0], 1)
            for j in range(1, 4):
                out = jnp.where(sub // 2 == j, pltpu.roll(v, shifts[j], 1), out)
            return out

        wet0, wet1, wet2 = a_halo.rows(2, group)
        east1 = row_sign * a_halo.edge_rows(5, group)
        around1 = wet1 * ((wet0 + wet2) + beside(wet1, corners(corner_wet)))
        qs, outs = [], []
        for n, (_, _, field, response, sign) in enumerate(tracers):
            g = [
                b + (sign * m) * a
                for b, m, a in zip(
                    t_halo.rows(field, group), row_m, a_halo.rows(response, group)
                )
            ]
            q = wet1 * g[1]
            near = (wet0 * g[0] + wet2 * g[2]) + beside(q, corners(corner_q[n]))
            lap = wet1 * near - around1 * g[1]
            qs.append(q)
            outs.append(east1 * q - 0.01 * lap)
        return wet1, qs, outs

    def body(group, carry):
        row_wet, row_q, row_out = strips(group)
        for j in range(4):
            level = group * 4 + j
            shift = (127 - 2 * level) & 127

            def four(ve, vw, vn, vs, row_strip, column_strip):
                r = roll(row_strip, 7 - 2 * j, 0)
                r = jnp.concatenate([r, r], axis=0)
                c = pltpu.roll(column_strip, shift, 1)
                return (
                    jnp.where(row == ROWS - 1, r, pltpu.roll(ve, ROWS - 1, 0)),
                    jnp.where(row == 0, r, pltpu.roll(vw, 1, 0)),
                    jnp.where(lane == COLS - 1, c, pltpu.roll(vn, COLS - 1, 1)),
                    jnp.where(lane == 0, c, pltpu.roll(vs, 1, 1)),
                )

            wet = wets[level]
            fe, fn = east[level], north[level]
            if final:
                around, diagonal = arounds[level], diagonals[level]
            else:
                we, ww, wn, ws = four(wet, wet, wet, wet, row_wet, column_wet)
                around = wet * ((we + ww) + (wn + ws))
                diagonal = around + wet * (fe * (ww - we) + fn * (ws - wn))
                arounds[level] = around
                diagonals[level] = diagonal
            done = []
            for n, (field, response, _, _, sign) in enumerate(tracers):
                g = field[level] + (sign * multiplier) * response[level]
                q = wet * g
                e, w, no, so = four(q, q, q, q, row_q[n], column_q[n])
                near = wet * ((e + w) + (no + so))
                small = 0.01 * (near - around * g)
                u, v = (0.05 * fe) * q, (0.05 * fn) * q
                e, w, no, so = four(
                    u - small, -u - small, v - small, -v - small, row_out[n], column_out[n]
                )
                done.append(
                    (g + 0.05 * (near - diagonal * g))
                    + (wet * ((e + w) + (no + so)) + around * small)
                )
            t, s = done
            if final:
                new_temp[level] = t
                new_salt[level] = s
            else:
                above, total, pt, ps = carry
                total = total + wet * (weight(1, level) * t - weight(2, level) * s)
                up = weight(0, jnp.maximum(level - 1, 0)) * (above * wet)
                inverse = inverses[level]
                pt = (t + up * pt) * inverse
                ps = (s + up * ps) * inverse
                new_temp[level] = pt
                new_salt[level] = ps
                carry = (wet, total, pt, ps)
        return carry

    zero = jnp.zeros((ROWS, COLS), F32)
    if final:
        copies = []
        for part in range(LEVELS // CHUNK):
            lax.fori_loop(part * CHUNK // 4, (part + 1) * CHUNK // 4, body, 0)
            levels = pl.ds(part * CHUNK, CHUNK)
            for n, (source, target) in enumerate(((new_temp, temp_out), (new_salt, salt_out))):
                copies.append(
                    pltpu.make_async_copy(source.at[levels], target.at[levels], sems.at[n, part])
                )
                copies[-1].start()
        for copy in copies:
            copy.wait()
    else:
        _, total, _, _ = lax.fori_loop(0, GROUPS, body, (zero,) * 4)
        put_surface(messages, T_SURFACE, (surface + total,))
        back_substitute(
            messages, messages[:2], T_ROWS, (new_temp, new_salt), ratios, ((0, 1), (1, 2))
        )


def shape(*dims):
    return jax.ShapeDtypeStruct(dims, F32)


VMEM = pl.BlockSpec(memory_space=pltpu.VMEM)
HBM = pl.BlockSpec(memory_space=pltpu.HBM)
SMEM = pl.BlockSpec(memory_space=pltpu.SMEM)


def head(*block):
    return pl.BlockSpec(block, lambda i: (0,) * len(block), memory_space=pltpu.VMEM)


def call(kernel, outs, in_specs, out_specs=None, scratch=(), name=None, grid=None, room=40, aliases=None):
    extra = {} if grid is None else {"grid": grid}
    if aliases:
        extra["input_output_aliases"] = aliases
    return pl.pallas_call(
        kernel,
        out_shape=outs,
        in_specs=in_specs,
        out_specs=[VMEM] * len(outs) if out_specs is None else out_specs,
        scratch_shapes=scratch,
        compiler_params=pltpu.CompilerParams(vmem_limit_bytes=room * 1024 * 1000),
        name=name,
        **extra,
    )


def message_shapes(surfaces, row_fields, col_fields, corner_fields):
    rows = shape(2 * (1 + corner_fields) + surfaces + GROUPS * row_fields, 8, COLS)
    cols = shape(2 * (1 + col_fields), 8, COLS)
    return [rows, rows, cols, cols]


def solution(mesh):
    nx, ny = mesh.shape["gx"], mesh.shape["gy"]
    devices = nx * ny
    both = ("gx", "gy")
    eastward = [(i, (i + 1) % nx) for i in range(nx)]
    northward = [(j, (j + 1) % ny) for j in range(ny)]

    def back(pairs):
        return [(b, a) for a, b in pairs]

    def exchange(messages, corners, behind=()):
        row_low, row_high, col_low, col_high = messages
        rows_e = lax.ppermute(row_low, "gx", back(eastward))
        rows_w = lax.ppermute(row_high, "gx", eastward)
        own = col_low.shape[0]
        out = shape(own + 2 * corners + sum(b.shape[0] for b in behind[:1]), 8, COLS)
        to_south, to_north = call(
            forward_kernel, [out, out],
            [head(own, 8, COLS)] * 2
            + [head(2 * corners, 8, COLS)] * 2
            + [head(*b.shape) for b in behind],
            [head(*out.shape)] * 2, name="corners", grid=(1,),
        )(col_low, col_high, rows_e, rows_w, *behind)
        cols_n = lax.ppermute(to_south, "gy", back(northward))
        cols_s = lax.ppermute(to_north, "gy", northward)
        return [rows_e, rows_w, cols_n, cols_s]

    def exchange_strips(low, high, cols_n, cols_s):
        block = head(STRIPS, 8, COLS)
        low, high = call(
            strip_corner_kernel, [shape(*low.shape)] * 2,
            [block] * 2 + [head(*cols_n.shape)] * 2, [block] * 2,
            name="strip_corners", grid=(1,), aliases={0: 0, 1: 1},
        )(low, high, cols_n, cols_s)
        return [low, high], [
            lax.ppermute(low, "gx", back(eastward)), lax.ppermute(high, "gx", eastward)
        ]

    def all_sum(block):
        return lax.all_to_all(block, both, 0, 0, tiled=True)

    def surface_specs(rows, cols):
        return [head(rows, 8, COLS)] * 4 + [head(cols, 8, COLS)] * 2

    basis_shape = shape(4, 32, 2 * COLS)
    gram_shape = shape(devices, COLS)
    field = shape(LEVELS, ROWS, COLS)
    tile = shape(ROWS, COLS)

    def whole(*dims):
        return head(*dims)

    def per_device(
        sens_temp, sens_salt, sens_surface, flow_east, flow_north, mix_profile,
        thermal_weight, haline_weight, surface_diag, land_mask, bottom_level,
    ):
        def in_hbm(*xs):
            return [pltpu.with_memory_space_constraint(x, pltpu.HBM) for x in xs]

        *sent, temp, salt, wets, kept = call(
            combine_kernel,
            message_shapes(3, 0, 0, 0) + [field] * 3 + [shape(3, LEVELS, 8, COLS)],
            [SMEM] * 3 + [HBM] * 3 + [VMEM] * 3,
            scratch=[
                pltpu.VMEM((LEVELS, ROWS, COLS), jnp.int32),
                pltpu.SemaphoreType.DMA((3, LEVELS // CHUNK)),
            ],
            name="combine",
        )(
            *in_hbm(
                mix_profile, thermal_weight, haline_weight, sens_temp, sens_salt, land_mask,
                bottom_level, sens_surface, surface_diag,
            )
        )
        cols = shape(12, 8, COLS)
        strip = shape(STRIPS + 6 * GROUPS, 8, COLS)
        (col_low, col_high, strip_low, strip_high,
         temp, salt, temp_response, salt_response, inverses, ratios, east, north) = call(
            solve_kernel,
            [cols, cols, strip, strip] + [field] * 8,
            [VMEM] * 4 + [HBM] * 2,
            scratch=[pltpu.SemaphoreType.DMA((2,))],
            name="solve",
        )(temp, salt, wets, kept, *in_hbm(flow_east, flow_north))
        got = exchange(sent, A_CORNERS, (col_low, col_high))
        strips, far_strips = exchange_strips(strip_low, strip_high, got[2], got[3])
        halo = [*strips, col_low, col_high, *far_strips, *got[2:]]
        basis, gram, fixed = call(
            first_surface_kernel,
            [basis_shape, gram_shape, shape(2, 32, 2 * COLS)],
            surface_specs(A_ROWS, 2 + 2 * A_CORNERS),
            [head(4, 32, 2 * COLS), head(devices, COLS), head(2, 32, 2 * COLS)],
            name="first_surface",
            grid=(1,),
        )(sent[0], sent[1], *got)
        gathered = all_sum(gram)

        def step(final, temp, salt, basis, gathered, more, outs):
            if final:
                places = {
                    "out_specs": [HBM, HBM, VMEM],
                    "scratch": [pltpu.VMEM((LEVELS, ROWS, COLS), F32)] * 2
                    + [pltpu.SemaphoreType.DMA((2, LEVELS // CHUNK))],
                }
            else:
                places = {}
            weights = [] if final else [kept]
            return call(
                functools.partial(step_kernel, final),
                outs,
                [VMEM] * (18 + len(weights) + len(more)),
                name="last_step" if final else "first_step",
                **places,
            )(
                temp, salt, temp_response, salt_response, east, north, wets, fixed,
                basis, gathered, *weights, *halo, *more,
            )

        temp, salt, arounds, diagonals, *second = step(
            False, temp, salt, basis, gathered, [inverses, ratios],
            [field] * 4 + message_shapes(1, 2, 2, 2),
        )
        more = exchange(second, T_CORNERS)
        basis, gram = call(
            next_surface_kernel,
            [basis_shape, gram_shape],
            surface_specs(T_ROWS, 2 * 3 + 2 * T_CORNERS) + [head(2, 32, 2 * COLS)],
            [head(4, 32, 2 * COLS), head(devices, COLS)],
            name="next_surface",
            grid=(1,),
        )(second[0], second[1], *more, fixed)
        gathered = all_sum(gram)
        return tuple(
            step(True, temp, salt, basis, gathered, [*second, *more, arounds, diagonals], [field, field, tile])
        )

    in_specs = (
        P(None, "gx", "gy"),
        P(None, "gx", "gy"),
        P("gx", "gy"),
        P(None, "gx", "gy"),
        P(None, "gx", "gy"),
        P(),
        P(),
        P(),
        P("gx", "gy"),
        P(None, "gx", "gy"),
        P("gx", "gy"),
    )
    out_specs = (P(None, "gx", "gy"), P(None, "gx", "gy"), P("gx", "gy"))
    return jax.shard_map(
        per_device, mesh=mesh, in_specs=in_specs, out_specs=out_specs, check_vma=False
    )
```

```python
import functools

import jax
import jax.numpy as jnp
from jax import lax
from jax.experimental import pallas as pl
from jax.experimental.pallas import tpu as pltpu
from jax.sharding import PartitionSpec as P

LEVELS = 48
ROWS = 16
COLS = 128
GROUPS = LEVELS // 4
CHUNK = 12
F32 = jnp.float32
PAIRS = [(i, j) for i in range(4) for j in range(i, 5)]


def two_sum(a, b):
    s = a + b
    t = s - a
    return s, (a - (s - t)) + (b - t)


def fast_two_sum(a, b):
    s = a + b
    return s, b - (s - a)


def split(a):
    c = a * 4097.0
    high = c - (c - a)
    return high, a - high


def two_prod(a, b, a_parts=None, b_parts=None):
    ah, al = split(a) if a_parts is None else a_parts
    bh, bl = split(b) if b_parts is None else b_parts
    p = a * b
    return p, ((ah * bh - p) + ah * bl + al * bh) + al * bl


def pair_add(x, y):
    s, t = two_sum(x[0], y[0])
    return fast_two_sum(s, t + (x[1] + y[1]))


def pair_scale(x, c):
    p, e = two_prod(x[0], c)
    return fast_two_sum(p, e + x[1] * c)


def pair_dot(xs, ys):
    terms, rest = [], []
    for x, y in zip(xs, ys):
        p, e = two_prod(x[0], y[0])
        terms.append(p)
        rest.append(e + (x[0] * y[1] + x[1] * y[0]))
    while len(terms) > 1:
        sums = [two_sum(a, b) for a, b in zip(terms[::2], terms[1::2])]
        rest += [e for _, e in sums]
        terms = [s for s, _ in sums] + terms[len(sums) * 2 :]
    while len(rest) > 1:
        rest = [a + b for a, b in zip(rest[::2], rest[1::2])] + rest[len(rest) // 2 * 2 :]
    return terms[0] + rest[0]


def roll(x, shift, axis):
    shift = shift % x.shape[axis]
    return x if shift == 0 else pltpu.roll(x, shift, axis)


def iota(shape, axis):
    return lax.broadcasted_iota(jnp.int32, shape, axis)


A_CORNERS, T_CORNERS = 1, 3
A_SURFACE, T_SURFACE = 2 * A_CORNERS, 2 * T_CORNERS
A_ROWS, T_ROWS = A_SURFACE + 3, T_SURFACE + 1
STRIPS = 12


def put_rows(low_ref, high_ref, first, field, group, j, cells):
    at = first + field * GROUPS + group
    low_ref[at, 2 * j : 2 * j + 2, :] = cells[:2]
    high_ref[at, 2 * j : 2 * j + 2, :] = cells[ROWS - 2 :]


def packed(acc, cells, level):
    low, high = acc
    mine = lax.shift_right_logical(iota((ROWS, COLS), 1), 1) == level
    low = jnp.where(mine, pltpu.roll(cells, 2 * level, 1), low)
    high = jnp.where(mine, pltpu.roll(cells, 2 * level + 2, 1), high)
    return low, high


def put_surface(refs, first, fields):
    row_low, row_high, col_low, col_high = refs
    low = jnp.zeros((ROWS, COLS), F32)
    high = low
    lane_group = iota((ROWS, COLS), 1) // 8
    for n, cells in enumerate(fields):
        row_low[first + n] = cells[:8]
        row_high[first + n] = cells[8:]
        low = jnp.where(lane_group == n, roll(cells, 8 * n, 1), low)
        high = jnp.where(lane_group == n, roll(cells, 8 * n + 8, 1), high)
    put_cols(refs, 0, low, high)


def put_cols(refs, n, low, high):
    row_low, row_high, col_low, col_high = refs
    count = 0 if row_low is None else corners_of(row_low)
    for col, side, cells in ((col_low, 0, low), (col_high, count, high)):
        col[2 * n] = cells[:8]
        col[2 * n + 1] = cells[8:]
        if n < count:
            row_low[side + n] = cells[:8]
            row_high[side + n] = cells[8:]


def corners_of(rows):
    return A_CORNERS if rows.shape[0] == A_ROWS else T_CORNERS


def forward_kernel(own_low, own_high, rows_e, rows_w, *refs):
    count = rows_e.shape[0] // 2
    own = own_low.shape[0]
    more, outs = refs[:-2], refs[-2:]
    place = lax.axis_index("gy")
    ends_at = 0, lax.axis_size("gy") - 1
    for n, (out, mine, end) in enumerate(zip(outs, (own_low, own_high), ends_at)):
        inner = place != end
        side = n * count
        out[:own] = jnp.where(inner, mine[...], 0.0)
        out[own : own + count] = jnp.where(inner, rows_e[side : side + count], 0.0)
        out[own + count : own + 2 * count] = jnp.where(inner, rows_w[side : side + count], 0.0)
        if more:
            out[own + 2 * count :] = jnp.where(inner, more[n][...], 0.0)


def strip_corner_kernel(_low, _high, cols_n, cols_s, out_low, out_high):
    for side, cols in enumerate((cols_n, cols_s)):
        for n in range(5):
            out_low[5 * side + n] = cols[4 + 2 * n]
            out_high[5 * side + n] = cols[5 + 2 * n]
    for out in (out_low, out_high):
        out[10:] = jnp.zeros((STRIPS - 10, 8, COLS), F32)


def wet_at(mask, last, level):
    return jnp.where(last > level, mask[jnp.minimum(level, LEVELS - 1)], 0).astype(F32)


def combine_kernel(
    mix, thermal, haline, temp_in, salt_in, mask_in, bottom, surface, diag,
    row_low, row_high, col_low, col_high, temp, salt, wets, kept, mask, sems,
):
    last = bottom[...]
    zero = jnp.zeros((ROWS, COLS), F32)
    fields = (mask_in, mask), (temp_in, temp), (salt_in, salt)
    parts = LEVELS // CHUNK

    def copy(n, part):
        source, target = fields[n]
        levels = pl.ds(part * CHUNK, CHUNK)
        return pltpu.make_async_copy(source.at[levels], target.at[levels], sems.at[n, part])

    for part in range(parts):
        for n in range(3):
            copy(n, part).start()

    def body(group, carry):
        total, depth = carry
        for j in range(4):
            level = group * 4 + j
            wet = jnp.where(last > level, mask[level], 0).astype(F32)
            wets[level] = wet
            for n, weight in enumerate((mix, thermal, haline)):
                kept[n, level] = jnp.full((8, COLS), weight[level], F32)
            total = total + wet * (thermal[level] * temp[level] - haline[level] * salt[level])
            depth = depth + wet
        return total, depth

    carry = zero, zero
    step = CHUNK // 4
    for part in range(parts):
        for n in range(3):
            copy(n, part).wait()
        carry = lax.fori_loop(part * step, (part + 1) * step, body, carry, unroll=True)
    total, depth = carry
    refs = row_low, row_high, col_low, col_high
    put_surface(refs, A_SURFACE, (surface[...] + total, depth / LEVELS, diag[...]))


def weight_at(kept, n, level):
    value = kept[n, level]
    return jnp.concatenate([value, value], axis=0)


def solve_kernel(
    temp, salt, wets, kept, east_in, north_in,
    col_low, col_high, strip_low, strip_high, *rest,
):
    solved, (inverses, ratios, east, north, sems) = rest[:4], rest[4:]
    zero = jnp.zeros((ROWS, COLS), F32)
    pair = (zero, zero)
    copies = [
        pltpu.make_async_copy(source, target, sems.at[n])
        for n, (source, target) in enumerate(((east_in, east), (north_in, north)))
    ]
    for copy in copies:
        copy.start()

    def down_body(group, carry):
        up, ratio, values, wet, pack = carry
        for j in range(4):
            level = group * 4 + j
            below = jnp.where(
                level < LEVELS - 1, wets[jnp.minimum(level + 1, LEVELS - 1)], 0.0
            )
            down = weight_at(kept, 0, level) * (wet * below)
            inverse = 1.0 / ((1.0 + up + down) - up * ratio)
            sources = (
                temp[level],
                salt[level],
                weight_at(kept, 1, level) * wet,
                weight_at(kept, 2, level) * wet,
            )
            values = tuple((r + up * v) * inverse for r, v in zip(sources, values))
            for ref, v in zip(solved, values):
                ref[level] = v
            ratio = down * inverse
            inverses[level] = inverse
            ratios[level] = ratio
            put_rows(strip_low, strip_high, STRIPS, 2, group, j, wet)
            pack = packed(pack, wet, level)
            up = down
            wet = below
        return up, ratio, values, wet, pack

    carry = lax.fori_loop(0, GROUPS, down_body, (zero, zero, (zero,) * 4, wets[0], pair))
    refs = None, None, col_low, col_high
    put_cols(refs, 2, *carry[-1])
    for copy in copies:
        copy.wait()

    def flow_body(group, pack):
        for j in range(4):
            level = group * 4 + j
            put_rows(strip_low, strip_high, STRIPS, 5, group, j, east[level])
            pack = packed(pack, north[level], level)
        return pack

    put_cols(refs, 5, *lax.fori_loop(0, GROUPS, flow_body, pair))
    strips = strip_low, strip_high
    back_substitute(refs, strips, STRIPS, solved, ratios, ((0, 0), (1, 1), (3, 3), (4, 4)))


def back_substitute(refs, strips, first, solved, ratios, places):
    zero = jnp.zeros((ROWS, COLS), F32)

    def up_body(count, carry):
        values, packs = carry
        group = GROUPS - 1 - count
        for j in (3, 2, 1, 0):
            level = group * 4 + j
            ratio = ratios[level]
            values = tuple(ref[level] + ratio * v for ref, v in zip(solved, values))
            for ref, v, (field, _) in zip(solved, values, places):
                ref[level] = v
                put_rows(*strips, first, field, group, j, v)
            packs = tuple(packed(acc, v, level) for acc, v in zip(packs, values))
        return values, packs

    n = len(places)
    _, packs = lax.fori_loop(0, GROUPS, up_body, ((zero,) * n, ((zero, zero),) * n), unroll=2)
    for (_, block), acc in zip(places, packs):
        put_cols(refs, block, *acc)


def wide_surface(n, own, rows_e, rows_w, from_north, from_south):
    main = jnp.concatenate([own, rows_e, rows_w], axis=0)
    to_north = jnp.concatenate(from_north, axis=0)
    to_south = jnp.concatenate(from_south, axis=0)
    lane = iota((32, COLS), 1)
    side = jnp.where(
        lane < 8,
        roll(to_north, -8 * n, 1),
        jnp.where(lane >= COLS - 8, roll(to_south, 120 - 8 * n, 1), 0.0),
    )
    return jnp.concatenate([main, side], axis=1)


def krylov(c, diag, depth, basis_ref, gram_ref):
    def nb(v):
        return pltpu.roll(v, 31, 0), pltpu.roll(v, 1, 0), pltpu.roll(v, 255, 1), pltpu.roll(v, 1, 1)

    faces = [jnp.minimum(depth, d) for d in nb(depth)]
    centre = (diag - 1.0) + ((faces[0] + faces[1]) + (faces[2] + faces[3]))
    v = c
    own = []
    for k in range(5):
        if k < 4:
            basis_ref[k] = v
        mine = v[:ROWS, :COLS]
        own.append((mine, split(mine)))
        if k < 4:
            e, w, n, s = nb(v)
            v = centre * v - ((faces[0] * e + faces[1] * w) + (faces[2] * n + faces[3] * s))
    highs, lows = [], []
    for i, j in PAIRS:
        p, e = two_prod(own[i][0], own[j][0], own[i][1], own[j][1])
        s, t = two_sum(p[:8], p[8:])
        highs.append(s)
        lows.append(t + (e[:8] + e[8:]))
    pad = [jnp.zeros((8, COLS), F32)] * (16 - len(PAIRS))
    high = jnp.concatenate(highs + pad, axis=0).T
    low = jnp.concatenate(lows + pad, axis=0).T
    parts = [(high[8 * n : 8 * n + 8], low[8 * n : 8 * n + 8]) for n in range(16)]
    while len(parts) > 1:
        parts = [pair_add(a, b) for a, b in zip(parts[::2], parts[1::2])]
    total = parts[0]
    for shift in (4, 2, 1):
        total = pair_add(total, tuple(roll(x, shift, 0) for x in total))
    total = pair_add(total, tuple(roll(x, 124, 1) for x in total))
    first_half = (iota((8, COLS), 1) % 8) < 4
    sums = jnp.where(first_half, total[0], roll(total[1], 4, 1))
    gram_ref[...] = jnp.concatenate([sums] * (gram_ref.shape[0] // 8), axis=0)


def surface_fields(low, high, rows_e, rows_w, cols_n, cols_s, count):
    corners = A_CORNERS if count == 3 else T_CORNERS
    first = 2 * corners

    def column(cols):
        own = cols.shape[0] - 2 * corners
        return [cols[0], cols[1], cols[own], cols[own + corners]]

    return [
        wide_surface(
            n, jnp.concatenate([low[first + n], high[first + n]], axis=0),
            rows_e[first + n], rows_w[first + n], column(cols_n), column(cols_s),
        )
        for n in range(count)
    ]


def first_surface_kernel(low, high, rows_e, rows_w, cols_n, cols_s, basis, gram, fixed):
    c, depth, diag = surface_fields(low, high, rows_e, rows_w, cols_n, cols_s, 3)
    fixed[0] = depth
    fixed[1] = diag
    krylov(c, diag, depth, basis, gram)


def next_surface_kernel(low, high, rows_e, rows_w, cols_n, cols_s, fixed, basis, gram):
    (c,) = surface_fields(low, high, rows_e, rows_w, cols_n, cols_s, 1)
    krylov(c, fixed[1], fixed[0], basis, gram)


def coefficients(gathered):
    parts = [(gathered[8 * n : 8 * n + 8], None) for n in range(gathered.shape[0] // 8)]
    parts = [(p, jnp.zeros_like(p)) for p, _ in parts]
    while len(parts) > 1:
        parts = [pair_add(a, b) for a, b in zip(parts[::2], parts[1::2])]
    total = parts[0]
    for shift in (4, 2, 1):
        total = pair_add(total, tuple(roll(x, shift, 0) for x in total))
    for shift in (4, 2, 1):
        total = pair_add(total, tuple(roll(x, COLS - shift, 1) for x in total))
    table = {}
    for n, (i, j) in enumerate(PAIRS):
        entry = tuple(jnp.broadcast_to(x[:, 8 * n : 8 * n + 1], (8, COLS)) for x in total)
        table[i, j] = table[j, i] = entry
    imaged = {(i, k): pair_add(table[i, k], table[i, k + 1]) for i in range(4) for k in range(i + 1)}
    one = (jnp.ones((8, COLS), F32), jnp.zeros((8, COLS), F32))
    r, p, x = [one], [one], []
    rr = table[0, 0][0]
    for it in range(4):
        den = pair_dot([imaged[it, k] for k in range(it + 1)], p)
        step = rr / (p[it][0] * den)
        x = [x[k] + step * p[k][0] if k < len(x) else step * p[k][0] for k in range(it + 1)]
        if it < 3:
            image = [p[0]] + [pair_add(p[k], p[k - 1]) for k in range(1, it + 1)] + [p[it]]
            moved = [pair_scale(a, -step) for a in image]
            r = [pair_add(r[k], moved[k]) if k < len(r) else moved[k] for k in range(it + 2)]
            new = r[it + 1][0] * pair_dot([table[it + 1, k] for k in range(it + 2)], r)
            ratio = new / rr
            p = [
                pair_add(r[k], pair_scale(p[k], ratio)) if k < len(p) else r[k]
                for k in range(it + 2)
            ]
            rr = new
    return x


class Halo:
    def __init__(self, refs, late):
        self.low, self.high, self.own_s, self.own_n, self.e, self.w, self.n, self.s = refs
        self.late = late
        self.first = STRIPS if late else T_ROWS
        self.own_at, self.far_at = (-2, 2) if late else (0, 0)
        self.even_row = iota((8, COLS), 0) % 2 == 0
        self.even_lane = iota((8, COLS), 1) % 2 == 0
        self.sub = iota((8, COLS), 0)

    def rows(self, field, group):
        at = self.first + field * GROUPS + group
        e, w = self.e[at], self.w[at]
        return (
            jnp.where(self.even_row, roll(self.high[at], -1, 0), roll(self.low[at], 1, 0)),
            jnp.where(self.even_row, e, w),
            jnp.where(self.even_row, roll(e, -1, 0), roll(w, 1, 0)),
        )

    def edge_rows(self, field, group):
        at = self.first + field * GROUPS + group
        return jnp.where(self.even_row, self.e[at], self.w[at])

    def edge_columns(self, block):
        at = self.far_at + 2 * block
        return jnp.concatenate(
            [jnp.where(self.even_lane, self.n[at + h], self.s[at + h]) for h in range(2)], axis=0
        )

    def corners(self, block):
        if self.late:
            at = block - 1
            return self.e[at], self.e[at + 5], self.w[at], self.w[at + 5]
        east = self.n.shape[0] - 2 * T_CORNERS + block
        west = east + T_CORNERS
        return self.n[east], self.s[east], self.n[west], self.s[west]

    def columns(self, block):
        inner, outer = [], []
        for h in range(2):
            at = self.own_at + 2 * block + h
            inner.append(
                jnp.where(self.even_lane, roll(self.own_n[at], -1, 1), roll(self.own_s[at], 1, 1))
            )
            at = self.far_at + 2 * block + h
            outer.append(jnp.where(self.even_lane, roll(self.n[at], -1, 1), roll(self.s[at], 1, 1)))
        ne, se, nw, sw = self.corners(block)
        corner = jnp.where(
            self.sub < 4,
            jnp.where(self.even_lane, ne, se),
            jnp.where(self.even_lane, nw, sw),
        )
        return (
            jnp.concatenate(inner, axis=0),
            jnp.concatenate([self.edge_columns(block), corner], axis=0),
            jnp.concatenate(outer, axis=0),
        )


def ends(v):
    return pltpu.roll(v, v.shape[0] - 1, 0), pltpu.roll(v, 1, 0)


def step_kernel(
    final,
    temp, salt, temp_response, salt_response, east, north, wets, fixed, basis, gathered,
    *refs,
):
    if not final:
        kept, refs = refs[0], refs[1:]
        weight = functools.partial(weight_at, kept)
    a_halo = Halo(refs[:8], True)
    if final:
        t_halo = Halo(refs[8:16], False)
        arounds, diagonals = refs[16:18]
        temp_out, salt_out, new_surface, new_temp, new_salt, sems = refs[18:]
    else:
        t_halo = a_halo
        inverses, ratios, new_temp, new_salt, arounds, diagonals, *messages = refs[8:]
    tracers = ((temp, temp_response, 0, 3, 1.0), (salt, salt_response, 1, 4, -1.0))

    weights = coefficients(gathered[...])
    weights = [jnp.concatenate([jnp.concatenate([w] * 4, axis=0)] * 2, axis=1) for w in weights]
    full = sum(weights[k] * basis[k] for k in range(4))
    multiplier = full[:ROWS, :COLS]
    surface = fixed[1, :ROWS, :COLS] * multiplier
    if final:
        new_surface[...] = surface

    sub = iota((8, COLS), 0)
    even_row = sub % 2 == 0
    ring = jnp.concatenate([full[:ROWS], jnp.where(
        iota((8, 2 * COLS), 0) < 4, full[16:24], full[24:])], axis=0)
    even_lane = iota((24, COLS), 1) % 2 == 0

    def lanes(a, b):
        return jnp.where(
            even_lane,
            jnp.broadcast_to(ring[:, a : a + 1], (24, COLS)),
            jnp.broadcast_to(ring[:, b : b + 1], (24, COLS)),
        )

    def both_rows(a, b):
        return jnp.where(
            even_row,
            jnp.broadcast_to(full[a : a + 1, :COLS], (8, COLS)),
            jnp.broadcast_to(full[b : b + 1, :COLS], (8, COLS)),
        )

    column_m = [lanes(127, 0)[:ROWS], lanes(128, 255), lanes(129, 254)[:ROWS]]
    row_m = [both_rows(15, 0), both_rows(16, 31), both_rows(17, 30)]

    own = slice(0, ROWS)
    lane_sign = jnp.where(even_lane[own], 0.05, -0.05)
    wet0, wet1, wet2 = a_halo.columns(3)
    north1 = lane_sign * a_halo.edge_columns(6)
    e, w = ends(wet1)
    around1 = wet1[own] * ((e + w)[own] + (wet0 + wet2))
    column_wet = wet1
    column_q, column_out = [], []
    for _, _, field, response, sign in tracers:
        g = [
            b + (sign * m) * a
            for b, m, a in zip(t_halo.columns(field + 1), column_m, a_halo.columns(response + 1))
        ]
        q = wet1 * g[1]
        e, w = ends(q)
        near = (e + w)[own] + (wet0 * g[0] + wet2 * g[2])
        lap = wet1[own] * near - around1 * g[1][own]
        column_q.append(q)
        column_out.append(north1 * q[own] - 0.01 * lap)

    def corner_rows(v):
        return jnp.where(
            even_row,
            jnp.broadcast_to(v[16:17], (8, COLS)),
            jnp.broadcast_to(v[23:24], (8, COLS)),
        )

    corner_wet = corner_rows(column_wet)
    corner_q = [corner_rows(q) for q in column_q]
    column_wet = column_wet[own]
    column_q = [q[own] for q in column_q]

    lane8 = iota((8, COLS), 1)
    lane = iota((ROWS, COLS), 1)
    row = iota((ROWS, COLS), 0)
    row_sign = jnp.where(even_row, 0.05, -0.05)

    def beside(v, corner):
        return jnp.where(lane8 == COLS - 1, corner, pltpu.roll(v, COLS - 1, 1)) + jnp.where(
            lane8 == 0, corner, pltpu.roll(v, 1, 1)
        )

    def strips(group):
        shifts = [(127 - 2 * (group * 4 + j)) & 127 for j in range(4)]

        def corners(v):
            out = pltpu.roll(v, shifts[0], 1)
            for j in range(1, 4):
                out = jnp.where(sub // 2 == j, pltpu.roll(v, shifts[j], 1), out)
            return out

        wet0, wet1, wet2 = a_halo.rows(2, group)
        east1 = row_sign * a_halo.edge_rows(5, group)
        around1 = wet1 * ((wet0 + wet2) + beside(wet1, corners(corner_wet)))
        qs, outs = [], []
        for n, (_, _, field, response, sign) in enumerate(tracers):
            g = [
                b + (sign * m) * a
                for b, m, a in zip(
                    t_halo.rows(field, group), row_m, a_halo.rows(response, group)
                )
            ]
            q = wet1 * g[1]
            near = (wet0 * g[0] + wet2 * g[2]) + beside(q, corners(corner_q[n]))
            lap = wet1 * near - around1 * g[1]
            qs.append(q)
            outs.append(east1 * q - 0.01 * lap)
        return wet1, qs, outs

    def body(group, carry):
        row_wet, row_q, row_out = strips(group)
        for j in range(4):
            level = group * 4 + j
            shift = (127 - 2 * level) & 127

            def four(ve, vw, vn, vs, row_strip, column_strip):
                r = roll(row_strip, 7 - 2 * j, 0)
                r = jnp.concatenate([r, r], axis=0)
                c = pltpu.roll(column_strip, shift, 1)
                return (
                    jnp.where(row == ROWS - 1, r, pltpu.roll(ve, ROWS - 1, 0)),
                    jnp.where(row == 0, r, pltpu.roll(vw, 1, 0)),
                    jnp.where(lane == COLS - 1, c, pltpu.roll(vn, COLS - 1, 1)),
                    jnp.where(lane == 0, c, pltpu.roll(vs, 1, 1)),
                )

            wet = wets[level]
            fe, fn = east[level], north[level]
            if final:
                around, diagonal = arounds[level], diagonals[level]
            else:
                we, ww, wn, ws = four(wet, wet, wet, wet, row_wet, column_wet)
                around = wet * ((we + ww) + (wn + ws))
                diagonal = around + wet * (fe * (ww - we) + fn * (ws - wn))
                arounds[level] = around
                diagonals[level] = diagonal
            done = []
            for n, (field, response, _, _, sign) in enumerate(tracers):
                g = field[level] + (sign * multiplier) * response[level]
                q = wet * g
                e, w, no, so = four(q, q, q, q, row_q[n], column_q[n])
                near = wet * ((e + w) + (no + so))
                small = 0.01 * (near - around * g)
                u, v = (0.05 * fe) * q, (0.05 * fn) * q
                e, w, no, so = four(
                    u - small, -u - small, v - small, -v - small, row_out[n], column_out[n]
                )
                done.append(
                    (g + 0.05 * (near - diagonal * g))
                    + (wet * ((e + w) + (no + so)) + around * small)
                )
            t, s = done
            if final:
                new_temp[level] = t
                new_salt[level] = s
            else:
                above, total, pt, ps = carry
                total = total + wet * (weight(1, level) * t - weight(2, level) * s)
                up = weight(0, jnp.maximum(level - 1, 0)) * (above * wet)
                inverse = inverses[level]
                pt = (t + up * pt) * inverse
                ps = (s + up * ps) * inverse
                new_temp[level] = pt
                new_salt[level] = ps
                carry = (wet, total, pt, ps)
        return carry

    zero = jnp.zeros((ROWS, COLS), F32)
    if final:
        copies = []
        for part in range(LEVELS // CHUNK):
            lax.fori_loop(part * CHUNK // 4, (part + 1) * CHUNK // 4, body, 0)
            levels = pl.ds(part * CHUNK, CHUNK)
            for n, (source, target) in enumerate(((new_temp, temp_out), (new_salt, salt_out))):
                copies.append(
                    pltpu.make_async_copy(source.at[levels], target.at[levels], sems.at[n, part])
                )
                copies[-1].start()
        for copy in copies:
            copy.wait()
    else:
        _, total, _, _ = lax.fori_loop(0, GROUPS, body, (zero,) * 4)
        put_surface(messages, T_SURFACE, (surface + total,))
        back_substitute(
            messages, messages[:2], T_ROWS, (new_temp, new_salt), ratios, ((0, 1), (1, 2))
        )


def shape(*dims):
    return jax.ShapeDtypeStruct(dims, F32)


VMEM = pl.BlockSpec(memory_space=pltpu.VMEM)
HBM = pl.BlockSpec(memory_space=pltpu.HBM)
SMEM = pl.BlockSpec(memory_space=pltpu.SMEM)


def head(*block):
    return pl.BlockSpec(block, lambda i: (0,) * len(block), memory_space=pltpu.VMEM)


def call(kernel, outs, in_specs, out_specs=None, scratch=(), name=None, grid=None, room=40, aliases=None):
    extra = {} if grid is None else {"grid": grid}
    if aliases:
        extra["input_output_aliases"] = aliases
    return pl.pallas_call(
        kernel,
        out_shape=outs,
        in_specs=in_specs,
        out_specs=[VMEM] * len(outs) if out_specs is None else out_specs,
        scratch_shapes=scratch,
        compiler_params=pltpu.CompilerParams(vmem_limit_bytes=room * 1024 * 1000),
        name=name,
        **extra,
    )


def message_shapes(surfaces, row_fields, col_fields, corner_fields):
    rows = shape(2 * (1 + corner_fields) + surfaces + GROUPS * row_fields, 8, COLS)
    cols = shape(2 * (1 + col_fields), 8, COLS)
    return [rows, rows, cols, cols]


def solution(mesh):
    nx, ny = mesh.shape["gx"], mesh.shape["gy"]
    devices = nx * ny
    both = ("gx", "gy")
    eastward = [(i, (i + 1) % nx) for i in range(nx)]
    northward = [(j, (j + 1) % ny) for j in range(ny)]

    def back(pairs):
        return [(b, a) for a, b in pairs]

    def exchange(messages, corners, behind=()):
        row_low, row_high, col_low, col_high = messages
        rows_e = lax.ppermute(row_low, "gx", back(eastward))
        rows_w = lax.ppermute(row_high, "gx", eastward)
        own = col_low.shape[0]
        out = shape(own + 2 * corners + sum(b.shape[0] for b in behind[:1]), 8, COLS)
        to_south, to_north = call(
            forward_kernel, [out, out],
            [head(own, 8, COLS)] * 2
            + [head(2 * corners, 8, COLS)] * 2
            + [head(*b.shape) for b in behind],
            [head(*out.shape)] * 2, name="corners", grid=(1,),
        )(col_low, col_high, rows_e, rows_w, *behind)
        cols_n = lax.ppermute(to_south, "gy", back(northward))
        cols_s = lax.ppermute(to_north, "gy", northward)
        return [rows_e, rows_w, cols_n, cols_s]

    def exchange_strips(low, high, cols_n, cols_s):
        block = head(STRIPS, 8, COLS)
        low, high = call(
            strip_corner_kernel, [shape(*low.shape)] * 2,
            [block] * 2 + [head(*cols_n.shape)] * 2, [block] * 2,
            name="strip_corners", grid=(1,), aliases={0: 0, 1: 1},
        )(low, high, cols_n, cols_s)
        return [low, high], [
            lax.ppermute(low, "gx", back(eastward)), lax.ppermute(high, "gx", eastward)
        ]

    def all_sum(block):
        return lax.all_to_all(block, both, 0, 0, tiled=True)

    def surface_specs(rows, cols):
        return [head(rows, 8, COLS)] * 4 + [head(cols, 8, COLS)] * 2

    basis_shape = shape(4, 32, 2 * COLS)
    gram_shape = shape(devices, COLS)
    field = shape(LEVELS, ROWS, COLS)
    tile = shape(ROWS, COLS)

    def whole(*dims):
        return head(*dims)

    def per_device(
        sens_temp, sens_salt, sens_surface, flow_east, flow_north, mix_profile,
        thermal_weight, haline_weight, surface_diag, land_mask, bottom_level,
    ):
        def in_hbm(*xs):
            return [pltpu.with_memory_space_constraint(x, pltpu.HBM) for x in xs]

        *sent, temp, salt, wets, kept = call(
            combine_kernel,
            message_shapes(3, 0, 0, 0) + [field] * 3 + [shape(3, LEVELS, 8, COLS)],
            [SMEM] * 3 + [HBM] * 3 + [VMEM] * 3,
            scratch=[
                pltpu.VMEM((LEVELS, ROWS, COLS), jnp.int32),
                pltpu.SemaphoreType.DMA((3, LEVELS // CHUNK)),
            ],
            name="combine",
        )(
            *in_hbm(
                mix_profile, thermal_weight, haline_weight, sens_temp, sens_salt, land_mask,
                bottom_level, sens_surface, surface_diag,
            )
        )
        cols = shape(12, 8, COLS)
        strip = shape(STRIPS + 6 * GROUPS, 8, COLS)
        (col_low, col_high, strip_low, strip_high,
         temp, salt, temp_response, salt_response, inverses, ratios, east, north) = call(
            solve_kernel,
            [cols, cols, strip, strip] + [field] * 8,
            [VMEM] * 4 + [HBM] * 2,
            scratch=[pltpu.SemaphoreType.DMA((2,))],
            name="solve",
        )(temp, salt, wets, kept, *in_hbm(flow_east, flow_north))
        got = exchange(sent, A_CORNERS, (col_low, col_high))
        strips, far_strips = exchange_strips(strip_low, strip_high, got[2], got[3])
        halo = [*strips, col_low, col_high, *far_strips, *got[2:]]
        basis, gram, fixed = call(
            first_surface_kernel,
            [basis_shape, gram_shape, shape(2, 32, 2 * COLS)],
            surface_specs(A_ROWS, 2 + 2 * A_CORNERS),
            [head(4, 32, 2 * COLS), head(devices, COLS), head(2, 32, 2 * COLS)],
            name="first_surface",
            grid=(1,),
        )(sent[0], sent[1], *got)
        gathered = all_sum(gram)

        def step(final, temp, salt, basis, gathered, more, outs):
            if final:
                places = {
                    "out_specs": [HBM, HBM, VMEM],
                    "scratch": [pltpu.VMEM((LEVELS, ROWS, COLS), F32)] * 2
                    + [pltpu.SemaphoreType.DMA((2, LEVELS // CHUNK))],
                }
            else:
                places = {}
            weights = [] if final else [kept]
            return call(
                functools.partial(step_kernel, final),
                outs,
                [VMEM] * (18 + len(weights) + len(more)),
                name="last_step" if final else "first_step",
                **places,
            )(
                temp, salt, temp_response, salt_response, east, north, wets, fixed,
                basis, gathered, *weights, *halo, *more,
            )

        temp, salt, arounds, diagonals, *second = step(
            False, temp, salt, basis, gathered, [inverses, ratios],
            [field] * 4 + message_shapes(1, 2, 2, 2),
        )
        more = exchange(second, T_CORNERS)
        basis, gram = call(
            next_surface_kernel,
            [basis_shape, gram_shape],
            surface_specs(T_ROWS, 2 * 3 + 2 * T_CORNERS) + [head(2, 32, 2 * COLS)],
            [head(4, 32, 2 * COLS), head(devices, COLS)],
            name="next_surface",
            grid=(1,),
        )(second[0], second[1], *more, fixed)
        gathered = all_sum(gram)
        return tuple(
            step(True, temp, salt, basis, gathered, [*second, *more, arounds, diagonals], [field, field, tile])
        )

    in_specs = (
        P(None, "gx", "gy"),
        P(None, "gx", "gy"),
        P("gx", "gy"),
        P(None, "gx", "gy"),
        P(None, "gx", "gy"),
        P(),
        P(),
        P(),
        P("gx", "gy"),
        P(None, "gx", "gy"),
        P("gx", "gy"),
    )
    out_specs = (P(None, "gx", "gy"), P(None, "gx", "gy"), P("gx", "gy"))
    return jax.shard_map(
        per_device, mesh=mesh, in_specs=in_specs, out_specs=out_specs, check_vma=False
    )
```
